256 devices in a mesh: lat: 64 (over y_hi, x, z), depth: 4 (over y_lo, core).
Axes of the slice: x: 4, y: 4 (y_hi: 2, y_lo: 2; y = y_hi * 2 + y_lo), z: 8, core: 2. Of those that a mesh axis runs over, the one named last changes fastest.
Arguments:
- head: float32 [64, 512, 4096], P('depth', 'lat'), may hold values from -1 to 0.5
- head_old: float32 [64, 512, 4096], P('depth', 'lat'), may hold values from -1 to 0.5
- soil: int32 [64, 512, 4096], P('depth', 'lat'), may hold values from 0 to 11
- cond_table: float32 [12], replicated, may hold values from 0.3 to 2
- shape_table: float32 [12], replicated, may hold values from 0.3 to 1.5
- pore_table: float32 [12], replicated, may hold values from 0.2 to 0.5
- pond: float32 [512, 4096], P('lat'), may hold values from 0.02 to 0.6
- ground: float32 [512, 4096], P('lat'), may hold values from -1.5 to 1.5
- ponded: int32 [512, 4096], P('lat'), may hold values 0 or 1
- river: int32 [512, 4096], P('lat'), may hold values 0 or 1
Outputs:
- head_new: float32 [64, 512, 4096], P('depth', 'lat')
- surface_new: float32 [512, 4096], P('lat', 'depth')
The draws below stay inside these ranges and needn't reach their ends.
All inputs are finite; a program needn't handle non-finite values. No bound on the sum of `ponded` or of `river` on one device may be relied on, other than what follows from the above.
Results may differ from the reference program's by a relative error of at most 0.0003.
Values sent between devices are 32-bit elements; how exact they have to be, the bound alone decides.
No kernel may reach another device: no remote copies, remote signals or barrier semaphores. Data moves between devices by JAX's collectives and lax.ppermute only.
A program may use at most 128 MiB of HBM per device.

```python
import math
import jax
import jax.numpy as jnp

NY = 4096
NSOIL = 12
SWEEPS = 4
NX = 512
NZ = 64


def touch_ends(drawn, rng, low, high):
    spot = [jax.random.randint(jax.random.fold_in(rng, axis), (), 0, length) for axis, length in enumerate(drawn.shape)]
    main_axis = drawn.shape.index(max(drawn.shape))
    neighbour = spot[:main_axis] + [(spot[main_axis] + 1) % drawn.shape[main_axis]] + spot[main_axis + 1:]
    return drawn.at[tuple(spot)].set(low).at[tuple(neighbour)].set(high)


def steps_of(stream_key, dims, cuts, smallest, top_value):
    def one(position, parts):
        draws = jax.random.uniform(jax.random.fold_in(jax.random.fold_in(stream_key, 6), position), (parts,), jnp.float32, smallest / len(cuts), top_value / len(cuts))
        return jnp.repeat(jnp.exp(draws), dims[position] // parts).reshape((-1,) + (1,) * (len(dims) - position - 1))

    gain = one(*cuts[0])
    for cut in cuts[1:]:
        gain = gain * one(*cut)
    return gain


def scatter_about(own_key, shape, deviation, bound, shards=(), held_as=jnp.bfloat16):
    drawn = jax.random.normal(own_key, shape, jnp.float32) * deviation
    if len(shards) > 0:
        drawn = steps_of(own_key, shape, shards, -0.22, 0.18) * drawn
    return jnp.clip(drawn, min=-bound, max=bound).astype(held_as)


def setup_inputs(seed: int = 0) -> dict:
    key_of = jax.random.split(jax.random.key(seed), 11)
    return {
        "head": jnp.clip(-1.0 + 1.5 * jax.random.uniform(key_of[0], (NZ, NX, NY), jnp.float32) ** steps_of(key_of[0], (NZ, NX, NY), ((0, 4), (1, 64)), -0.2, 0.2), -1.0, 0.5),
        "head_old": jnp.clip(-1.0 + 1.5 * jax.random.uniform(key_of[1], (NZ, NX, NY), jnp.float32) ** steps_of(key_of[1], (NZ, NX, NY), ((0, 4), (1, 64)), -0.2, 0.2), -1.0, 0.5),
        "soil": touch_ends(jax.random.randint(key_of[2], (NZ, NX, NY), 0, NSOIL), jax.random.fold_in(key_of[2], 1), 0, NSOIL - 1).astype(jnp.int32),
        "cond_table": jnp.clip(jnp.exp(jax.random.uniform(key_of[3], (NSOIL,), jnp.float32, math.log(0.3), math.log(2.0))), 0.3, 2.0),
        "shape_table": jnp.clip(jnp.exp(jax.random.uniform(key_of[4], (NSOIL,), jnp.float32, math.log(0.3), math.log(1.5))), 0.3, 1.5),
        "pore_table": jnp.clip(jax.random.uniform(key_of[5], (NSOIL,), jnp.float32, 0.2, 0.5), 0.2, 0.5),
        "pond": jnp.clip(0.02 + 0.58000002 * jax.random.uniform(key_of[6], (NX, NY), jnp.float32) ** steps_of(key_of[6], (NX, NY), ((0, 64),), -0.2, 0.2), 0.02, 0.6),
        "ground": scatter_about(key_of[7], (NX, NY), 0.3, 1.5, ((0, 64),), jnp.float32),
        "ponded": touch_ends((jax.random.randint(key_of[8], (NX, NY), 0, 2) < 1).astype(jnp.int32), jax.random.fold_in(key_of[8], 1), 0, 1),
        "river": touch_ends((jax.random.randint(key_of[9], (NX, NY), 0, 8) < 1).astype(jnp.int32), jax.random.fold_in(key_of[9], 1), 0, 1),
    }


TIME_STEP = 20.0
SURFACE_STEP = 2.0
SPECIFIC_STORAGE = 0.01
LAND_CONVEYANCE = 3.0
RIVER_CONVEYANCE = 10.0
SLOPE_FLOOR = 0.01

def lookup(soil, table):
    value = jnp.zeros(soil.shape, jnp.float32)
    for soil_kind in range(table.shape[0]):
        value = jnp.where(soil == soil_kind, table[soil_kind], value)
    return value

def harmonic(first, second):
    total = first + second
    return 2.0 * first * second / jnp.where(total > 0.0, total, 1.0)

def soil_state(head, head_old, soil, cond_table, shape_table, pore_table):
    saturated = lookup(soil, cond_table)
    steepness = lookup(soil, shape_table)
    porosity = lookup(soil, pore_table)
    wetness = jnp.exp(steepness * jnp.minimum(head, 0.0))
    wetness_old = jnp.exp(steepness * jnp.minimum(head_old, 0.0))
    conductivity = saturated * wetness
    storage_change = porosity * (wetness - wetness_old) + SPECIFIC_STORAGE * (head - head_old)
    capacity = SPECIFIC_STORAGE + porosity * steepness * wetness
    return (conductivity, storage_change, capacity)

def vertical_terms(cond_ext, head_ext):
    vface = harmonic(cond_ext[:-1], cond_ext[1:])
    vflux = vface * (head_ext[:-1] - head_ext[1:] + 1.0)
    return (vface, vflux)

def lateral_inflow(conductivity, head, cond_rows, head_rows):
    face_x = harmonic(cond_rows[:, :-1], cond_rows[:, 1:])
    inflow = face_x[:, 1:] * (head_rows[:, 2:] - head) + face_x[:, :-1] * (head_rows[:, :-2] - head)
    cond_cols = jnp.pad(conductivity, ((0, 0), (0, 0), (1, 1)))
    head_cols = jnp.pad(head, ((0, 0), (0, 0), (1, 1)))
    face_y = harmonic(cond_cols[:, :, :-1], cond_cols[:, :, 1:])
    inflow = inflow + face_y[:, :, 1:] * (head_cols[:, :, 2:] - head)
    return inflow + face_y[:, :, :-1] * (head_cols[:, :, :-2] - head)

def newton_system(storage_change, capacity, vface, vflux, lateral, top_term, top_cond, bottom_term):
    inflow = jnp.concatenate([(vflux[0] + top_term)[None], vflux[1:-1]], 0)
    outflow = jnp.concatenate([vflux[1:-1], (vflux[-1] + bottom_term)[None]], 0)
    residual = storage_change / TIME_STEP - (inflow - outflow) - lateral
    diagonal = capacity / TIME_STEP + vface[:-1] + vface[1:]
    diagonal = jnp.concatenate([(diagonal[0] + 2.0 * top_cond)[None], diagonal[1:]], 0)
    return (residual, diagonal, -vface[:-1], -vface[1:])

def thomas(lower, middle, upper, rhs):
    count = middle.shape[0]
    ratios = []
    partial_values = []
    for row_index in range(count):
        if row_index == 0:
            pivot = middle[0]
            partial_values.append(rhs[0] / pivot)
        else:
            pivot = middle[row_index] - lower[row_index] * ratios[-1]
            partial_values.append((rhs[row_index] - lower[row_index] * partial_values[-1]) / pivot)
        ratios.append(upper[row_index] / pivot)
    result = [partial_values[-1]]
    for row_index in reversed(range(count - 1)):
        result.insert(0, partial_values[row_index] - ratios[row_index] * result[0])
    return jnp.stack(result, 0)

def face_k(pond_one, ground_one, conv_one, pond_two, ground_two, conv_two):
    depth_face = 0.5 * (pond_one + pond_two)
    slope = pond_two + ground_two - (pond_one + ground_one)
    return jnp.power(depth_face, 5.0 / 3.0) * harmonic(conv_one, conv_two) / jnp.sqrt(jnp.abs(slope) + SLOPE_FLOOR)

def row_terms(pond, ground, conv, exfil, pond_up, ground_up, conv_up, pond_down, ground_down, conv_down):
    k_up = face_k(pond, ground, conv, pond_up, ground_up, conv_up)
    k_down = face_k(pond, ground, conv, pond_down, ground_down, conv_down)
    k_cols = face_k(pond[:, :-1], ground[:, :-1], conv[:, :-1], pond[:, 1:], ground[:, 1:], conv[:, 1:])
    k_left = jnp.pad(k_cols, ((0, 0), (1, 0)))
    k_right = jnp.pad(k_cols, ((0, 0), (0, 1)))
    ground_left = jnp.pad(ground[:, :-1], ((0, 0), (1, 0)))
    ground_right = jnp.pad(ground[:, 1:], ((0, 0), (0, 1)))
    sdiag = 1.0 / SURFACE_STEP + k_up + k_down + k_left + k_right
    srhs = pond / SURFACE_STEP + exfil + k_up * (ground_up - ground) + k_down * (ground_down - ground)
    srhs = srhs + k_left * (ground_left - ground) + k_right * (ground_right - ground)
    return (k_up, k_down, k_left, k_right, sdiag, srhs)

def sweep(level, level_up, level_down, terms):
    k_up, k_down, k_left, k_right, sdiag, srhs = terms
    left = jnp.pad(level[:, :-1], ((0, 0), (1, 0)))
    right = jnp.pad(level[:, 1:], ((0, 0), (0, 1)))
    return (srhs + k_up * level_up + k_down * level_down + k_left * left + k_right * right) / sdiag

def pad_above(field):
    return jnp.pad(field[:-1], ((1, 0), (0, 0)))

def pad_below(field):
    return jnp.pad(field[1:], ((0, 1), (0, 0)))

def reference(head, head_old, soil, cond_table, shape_table, pore_table, pond, ground, ponded, river):
    conductivity, storage_change, capacity = soil_state(head, head_old, soil, cond_table, shape_table, pore_table)
    zero_layer = jnp.zeros((1,) + head.shape[1:], jnp.float32)
    vface, vflux = vertical_terms(jnp.concatenate([zero_layer, conductivity, zero_layer], 0), jnp.concatenate([zero_layer, head, zero_layer], 0))
    lateral = lateral_inflow(conductivity, head, jnp.pad(conductivity, ((0, 0), (1, 1), (0, 0))), jnp.pad(head, ((0, 0), (1, 1), (0, 0))))
    wet_pond = ponded.astype(jnp.float32) * pond
    top_flux = conductivity[0] * (2.0 * (wet_pond - head[0]) + 1.0)
    residual, diagonal, lower, upper = newton_system(storage_change, capacity, vface, vflux, lateral, top_flux, conductivity[0], conductivity[-1])
    step = thomas(lower, diagonal, upper, -residual)
    head_new = head + step
    exfil = -top_flux
    conveyance = LAND_CONVEYANCE + (RIVER_CONVEYANCE - LAND_CONVEYANCE) * river.astype(jnp.float32)
    terms = row_terms(pond, ground, conveyance, exfil, pad_above(pond), pad_above(ground), pad_above(conveyance), pad_below(pond), pad_below(ground), pad_below(conveyance))
    level = pond
    for sweep_index in range(SWEEPS):
        level = sweep(level, pad_above(level), pad_below(level), terms)
    return (head_new, level)
```

```python
import jax
import jax.numpy as jnp
from jax import lax
from jax.experimental import pallas as pl
from jax.experimental.pallas import tpu as pltpu
from jax.sharding import PartitionSpec as P

SWEEPS = 4

TIME_STEP = 20.0
SURFACE_STEP = 2.0
SPECIFIC_STORAGE = 0.01
LAND_CONVEYANCE = 3.0
RIVER_CONVEYANCE = 10.0
SLOPE_FLOOR = 0.01

LOG2E = 1.4426950408889634
LN2 = 0.6931471805599453
CLOSED = 1e37

LANES = 128
ROWS = 8
CHUNK = 512
VMEM_LIMIT = 40 * 1024 * 1024

VMEM = pl.BlockSpec(memory_space=pltpu.VMEM)
SMEM = pl.BlockSpec(memory_space=pltpu.SMEM)
ANY = pl.BlockSpec(memory_space=pl.ANY)


def f32(*shape):
    return pltpu.VMEM(shape, jnp.float32)


def in_vmem(x):
    return pltpu.with_memory_space_constraint(x, pltpu.VMEM)


def params():
    return pltpu.CompilerParams(vmem_limit_bytes=VMEM_LIMIT)


def cost(flops, bytes_accessed=0):
    return pl.CostEstimate(flops=flops, bytes_accessed=bytes_accessed, transcendentals=0)


def rcp(x):
    r = pl.reciprocal(x, approx=True)
    return r * (2.0 - x * r)


def table_registers(*tables):
    lane = lax.broadcasted_iota(jnp.int32, (ROWS, LANES), 1)
    result = []
    for table in tables:
        value = jnp.ones((ROWS, LANES), jnp.float32)
        for soil_kind in range(table.shape[0]):
            value = jnp.where(lane == soil_kind, table[soil_kind], value)
        result.append(value)
    return result


def lookup(table, soil):
    parts = []
    for start in range(0, soil.shape[1], LANES):
        index = soil[:, start : start + LANES]
        parts.append(
            jnp.take_along_axis(table, index, axis=1, mode="promise_in_bounds")
        )
    return jnp.concatenate(parts, axis=1) if len(parts) > 1 else parts[0]


def lookup_rows(table, soil):
    return jnp.concatenate(
        [lookup(table, soil[start : start + ROWS]) for start in range(0, soil.shape[0], ROWS)], axis=0
    )


def window_start(quarter, width, window):
    return jnp.clip(quarter * width - LANES, 0, 4 * width - window)


def pack_kernel(
    cond_ref, shape_ref, head_ref, soil_ref, pond_ref, ground_ref, ponded_ref, river_ref,
    up_ref, down_ref, exfil_ref, soil_rows, soil_top, head_top, sem,
):
    nz = head_ref.shape[0]
    width = pond_ref.shape[1]
    quarter = width // 4
    window = quarter + 2 * LANES
    copies = [
        pltpu.make_async_copy(soil_ref.at[0], soil_top, sem.at[0]),
        pltpu.make_async_copy(head_ref.at[0], head_top, sem.at[1]),
        pltpu.make_async_copy(soil_ref.at[:, ROWS - 1, :], soil_rows.at[0], sem.at[2]),
        pltpu.make_async_copy(soil_ref.at[:, 0, :], soil_rows.at[1], sem.at[3]),
        pltpu.make_async_copy(head_ref.at[:, ROWS - 1, :], up_ref.at[pl.ds(0, nz)], sem.at[4]),
        pltpu.make_async_copy(head_ref.at[:, 0, :], down_ref.at[pl.ds(0, nz)], sem.at[5]),
    ]
    for copy in copies:
        copy.start()
    start = window_start(lax.axis_index("depth"), quarter, window)
    start = pl.multiple_of(start, LANES)
    lower_half = lax.broadcasted_iota(jnp.int32, (ROWS, window), 0) >= 4
    cut = pl.ds(start, window)
    conv = LAND_CONVEYANCE + (RIVER_CONVEYANCE - LAND_CONVEYANCE) * river_ref[:, cut].astype(jnp.float32)
    fields = [pond_ref[:, cut], ground_ref[:, cut], conv]
    cond_table, shape_table = table_registers(cond_ref, shape_ref)
    copies[0].wait()
    copies[1].wait()
    conductivity = lookup(cond_table, soil_top[...]) * jnp.exp(
        lookup(shape_table, soil_top[...]) * jnp.minimum(head_top[...], 0.0)
    )
    wet_pond = ponded_ref[...].astype(jnp.float32) * pond_ref[...]
    exfil = -conductivity * (2.0 * (wet_pond - head_top[...]) + 1.0)
    exfil_ref[...] = exfil
    tail = pl.ds(2 * nz, ROWS)
    up_ref[tail, :] = pltpu.roll(exfil, 4, 0)
    down_ref[tail, :] = exfil
    for place, field in enumerate(fields):
        lanes = pl.ds(place * window, window)
        up_ref[tail, lanes] = jnp.where(lower_half, field, up_ref[tail, lanes])
        down_ref[tail, lanes] = jnp.where(lower_half, pltpu.roll(field, 4, 0), down_ref[tail, lanes])
    copies[2].wait()
    up_ref[pl.ds(nz, nz), :] = soil_rows[0].astype(jnp.float32)
    copies[3].wait()
    down_ref[pl.ds(nz, nz), :] = soil_rows[1].astype(jnp.float32)
    copies[4].wait()
    copies[5].wait()


def state_chunk(chunk, tables, head_ref, old_ref, soil_ref, sigma, headx, base, diag):
    nz = head_ref.shape[0]
    half_res, steep, porosity, porosity_steep = tables
    lanes = pl.ds(pl.multiple_of(chunk * CHUNK, CHUNK), CHUNK)
    for z in range(nz):
        head = head_ref[z, :, lanes]
        old = old_ref[z, :, lanes]
        soil = soil_ref[z, :, lanes]
        alpha = lookup(steep, soil)
        pore = lookup(porosity, soil)
        power = alpha * jnp.minimum(head, 0.0)
        wet = jnp.exp2(power)
        wet_old = jnp.exp2(alpha * jnp.minimum(old, 0.0))
        sigma[z, :, lanes] = lookup(half_res, soil) * jnp.exp2(-power)
        headx[z, :, lanes] = head
        base[z, :, lanes] = pore * (wet_old - wet) + (SPECIFIC_STORAGE / TIME_STEP) * (old - head)
        diag[z, :, lanes] = SPECIFIC_STORAGE / TIME_STEP + lookup(porosity_steep, soil) * wet


def solve_chunk(
    chunk, flags, pond_ref, ponded_ref, sigma, headx, diag, last_flux,
    base, ratio, inv, top_col, bottom_col, resist_ref, sums_ref,
):
    nz = base.shape[0]
    is_top, is_bottom = flags
    start = pl.multiple_of(chunk * CHUNK, CHUNK)
    lanes = pl.ds(start, CHUNK)
    wide = pl.ds(start, CHUNK + LANES)
    sublane = lax.broadcasted_iota(jnp.int32, (ROWS, CHUNK), 0)
    inner = sublane < ROWS - 1
    face_above = flux_above = ratio_above = column = None
    for z in range(nz):
        sw, hw = sigma[z, :, wide], headx[z, :, wide]
        s, h = sw[:, :CHUNK], hw[:, :CHUNK]
        s_right = pltpu.roll(sw, CHUNK + LANES - 1, 1)[:, :CHUNK]
        h_right = pltpu.roll(hw, CHUNK + LANES - 1, 1)[:, :CHUNK]
        flux_y = rcp(s + s_right) * (h_right - h)
        shifted = jnp.concatenate([last_flux[z], flux_y], axis=1)
        flux_left = pltpu.roll(shifted, 1, 1)[:, LANES:]
        last_flux[z] = flux_y[:, CHUNK - LANES :]
        flux_x = rcp(s + pltpu.roll(s, ROWS - 1, 0)) * (pltpu.roll(h, ROWS - 1, 0) - h)
        flux_x = jnp.where(inner, flux_x, 0.0)
        b = base[z, :, lanes] + (flux_y - flux_left) + (flux_x - pltpu.roll(flux_x, 1, 0))
        d = diag[z, :, lanes]
        if z == 0:
            cond_top = 0.5 * rcp(s) * is_top
            wet_pond = ponded_ref[:, lanes].astype(jnp.float32) * pond_ref[:, lanes]
            b = b + cond_top * (2.0 * (wet_pond - h) + 1.0)
            d = d + 2.0 * cond_top
        else:
            b = b + flux_above
            d = d + face_above * (1.0 - ratio_above)
        if z == nz - 1:
            b = b - 0.5 * rcp(s) * is_bottom
        else:
            face = rcp(s + sigma[z + 1, :, lanes])
            flux = face * (h - headx[z + 1, :, lanes] + 1.0)
            b = b - flux
            d = d + face
        pivot_inv = rcp(d)
        base[z, :, lanes] = b
        inv[z, :, lanes] = pivot_inv
        column = pivot_inv if z == 0 else column * pivot_inv
        if z < nz - 1:
            ratio_above = face * pivot_inv
            ratio[z, :, lanes] = ratio_above
            top_col[z, :, lanes] = column
            column = column * face
            face_above, flux_above = face, flux
    first, last = column, pivot_inv
    top_col[nz - 1, :, lanes] = first
    bottom_col[nz - 1, :, lanes] = last
    corner = first
    resist_ref[pl.ds(2 * ROWS, ROWS), lanes] = corner
    resist_ref[pl.ds(ROWS, ROWS), lanes] = sigma[nz - 1, :, lanes] + last
    top_sum = first * b
    bottom_sum = last * b
    for z in reversed(range(nz - 1)):
        m = ratio[z, :, lanes]
        b = base[z, :, lanes]
        first = top_col[z, :, lanes] + m * first
        last = m * last
        top_col[z, :, lanes] = first
        bottom_col[z, :, lanes] = last
        top_sum = top_sum + first * b
        bottom_sum = bottom_sum + last * b
    resist_ref[pl.ds(0, ROWS), lanes] = sigma[0, :, lanes] + first
    sums_ref[pl.ds(0, ROWS), lanes] = top_sum + headx[0, :, lanes]
    sums_ref[pl.ds(ROWS, ROWS), lanes] = bottom_sum + headx[nz - 1, :, lanes]


def cells_kernel(
    cond_ref, shape_ref, pore_ref, head_ref, old_ref, soil_ref, pond_ref, ponded_ref,
    base, ratio, inv, top_col, bottom_col, resist_ref, sums_ref, rows_ref,
    sigma, headx, last_flux, sem,
):
    nz, _, width = head_ref.shape
    depth = lax.axis_index("depth")
    is_top = jnp.where(depth == 0, 1.0, 0.0)
    is_bottom = jnp.where(depth == 3, 1.0, 0.0)
    cond, shape, pore = table_registers(cond_ref, shape_ref, pore_ref)
    pore = pore * (1.0 / TIME_STEP)
    tables = (0.5 / cond, shape * LOG2E, pore, pore * shape)
    last_flux[...] = jnp.zeros_like(last_flux)
    sigma[:, :, pl.ds(width, LANES)] = jnp.full((nz, ROWS, LANES), CLOSED, jnp.float32)
    headx[:, :, pl.ds(width, LANES)] = jnp.zeros((nz, ROWS, LANES), jnp.float32)
    diag = inv

    @pl.loop(0, width // CHUNK)
    def _(chunk):
        state_chunk(chunk, tables, head_ref, old_ref, soil_ref, sigma, headx, base, diag)

    @pl.loop(0, width // CHUNK)
    def _(chunk):
        solve_chunk(
            chunk, (is_top, is_bottom), pond_ref, ponded_ref, sigma, headx, diag, last_flux,
            base, ratio, inv, top_col, bottom_col, resist_ref, sums_ref,
        )

    full = pl.ds(0, width)
    copies = []
    for place, array in enumerate((sigma, top_col, bottom_col)):
        for side, row in enumerate((ROWS - 1, 0)):
            source = array.at[:, row, full] if array is sigma else array.at[:, row, :]
            index = 2 * place + side
            copies.append(pltpu.make_async_copy(source, rows_ref.at[index], sem.at[index]))
    for copy in copies:
        copy.start()
    for copy in copies:
        copy.wait()


def halo_kernel(
    cond_ref, shape_ref, own_up, own_down, from_above, from_below, rows_ref, sums_ref, exfil_ref,
    ends_ref, flux_ref, sent_ref, kept_ref,
):
    nz = flux_ref.shape[1]
    width = own_up.shape[1]
    quarter = width // 4
    window = quarter + 2 * LANES
    lat = lax.axis_index("lat")
    has_above = jnp.where(lat == 0, 0.0, 1.0)
    has_below = jnp.where(lat == lax.axis_size("lat") - 1, 0.0, 1.0)
    is_even = lax.rem(lax.axis_index("depth"), 2) == 0
    cond, shape = table_registers(cond_ref, shape_ref)
    half_res, steep = 0.5 / cond, shape * LOG2E
    sublane = lax.broadcasted_iota(jnp.int32, (ROWS, CHUNK), 0)

    @pl.loop(0, width // CHUNK)
    def _(chunk):
        lanes = pl.ds(pl.multiple_of(chunk * CHUNK, CHUNK), CHUNK)
        totals = []
        for side, other, own, scale in ((0, from_below, own_up, has_below), (1, from_above, own_down, has_above)):
            total = None
            for start in range(0, nz, ROWS):
                here = pl.ds(start, ROWS)
                head = other[here, lanes]
                soil = other[pl.ds(nz + start, ROWS), lanes].astype(jnp.int32)
                res = lookup(half_res, soil) * jnp.exp2(-lookup(steep, soil) * jnp.minimum(head, 0.0))
                flux = rcp(res + rows_ref[side, here, lanes]) * (head - own[here, lanes]) * scale
                flux_ref[side, here, lanes] = flux
                part = (flux * rows_ref[2 + side, here, lanes], flux * rows_ref[4 + side, here, lanes])
                total = part if total is None else tuple(a + b for a, b in zip(total, part))
            totals.append([jnp.sum(part, axis=0, keepdims=True) for part in total])
        ends = []
        for place in range(2):
            added = jnp.where(sublane == 0, totals[1][place], 0.0)
            added = jnp.where(sublane == ROWS - 1, totals[0][place], added)
            ends.append(sums_ref[pl.ds(place * ROWS, ROWS), lanes] + added)
        ends_ref[pl.ds(0, ROWS), lanes] = jnp.where(is_even, ends[1], ends[0])
        ends_ref[pl.ds(ROWS, ROWS), lanes] = jnp.where(is_even, ends[0], ends[1])

    upper_half = lax.broadcasted_iota(jnp.int32, (ROWS, window), 0) < 4
    for place in range(4):
        lanes = pl.ds(min(max(place * quarter - LANES, 0), width - window), window)
        own = pltpu.roll(exfil_ref[:, lanes], 4, 0)
        above = from_above[pl.ds(2 * nz, ROWS), lanes]
        below = pltpu.roll(from_below[pl.ds(2 * nz, ROWS), lanes], 4, 0)
        target = (kept_ref, sent_ref)[place % 2]
        into = pl.ds((place // 2) * window, window)
        target[pl.ds(0, ROWS), into] = jnp.where(upper_half, above, own)
        target[pl.ds(ROWS, ROWS), into] = jnp.where(upper_half, own, below)


def local_kernel(flux_ref, base, ratio, inv, head_ref, out_ref):
    nz, _, width = base.shape
    sublane = lax.broadcasted_iota(jnp.int32, (ROWS, CHUNK), 0)

    @pl.loop(0, width // CHUNK)
    def _(chunk):
        lanes = pl.ds(pl.multiple_of(chunk * CHUNK, CHUNK), CHUNK)
        y = None
        for z in range(nz):
            below = flux_ref[0, pl.ds(z, 1), lanes]
            above = flux_ref[1, pl.ds(z, 1), lanes]
            added = jnp.where(sublane == 0, above, 0.0)
            added = jnp.where(sublane == ROWS - 1, below, added)
            rhs = base[z, :, lanes] + added
            y = rhs if z == 0 else rhs + ratio[z - 1, :, lanes] * y
            if z < nz - 1:
                out_ref[z, :, lanes] = y
        x = y * inv[nz - 1, :, lanes]
        out_ref[nz - 1, :, lanes] = x + head_ref[nz - 1, :, lanes]
        for z in reversed(range(nz - 1)):
            x = out_ref[z, :, lanes] * inv[z, :, lanes] + ratio[z, :, lanes] * x
            out_ref[z, :, lanes] = x + head_ref[z, :, lanes]


def final_kernel(local_ref, top_col, bottom_col, flow_in, flow_out, out_ref):
    nz, _, width = local_ref.shape

    @pl.loop(0, width // CHUNK)
    def _(chunk):
        lanes = pl.ds(pl.multiple_of(chunk * CHUNK, CHUNK), CHUNK)
        j_in, j_out = flow_in[:, lanes], flow_out[:, lanes]
        for z in range(nz):
            out_ref[z, :, lanes] = (
                local_ref[z, :, lanes] + top_col[z, :, lanes] * j_in - bottom_col[z, :, lanes] * j_out
            )


def shift_rows(x, by):
    return pltpu.roll(x, by % x.shape[0], 0)


def shift_lanes(x, by):
    return pltpu.roll(x, by % x.shape[1], 1)


def harmonic(first, second):
    total = first + second
    return 2.0 * first * second * rcp(jnp.where(total > 0.0, total, 1.0))


def face_k(pond, ground, conv, shift):
    pond_two, ground_two, conv_two = shift(pond), shift(ground), shift(conv)
    depth_face = 0.5 * (pond + pond_two)
    slope = pond_two + ground_two - (pond + ground)
    return (
        jnp.exp2((5.0 / 3.0 * LOG2E) * jnp.log(depth_face))
        * harmonic(conv, conv_two)
        * lax.rsqrt(jnp.abs(slope) + SLOPE_FLOOR)
    )


def surface_kernel(
    pond_ref, ground_ref, river_ref, from_above, from_below, level_ref, terms_ref,
):
    width = pond_ref.shape[1]
    quarter = width // 4
    window = quarter + 2 * LANES
    tail = pl.ds(from_above.shape[0] - ROWS, ROWS)
    lat = lax.axis_index("lat")
    start = pl.multiple_of(window_start(lax.axis_index("depth"), quarter, window), LANES)
    cut = pl.ds(start, window)
    upper_half = lax.broadcasted_iota(jnp.int32, (ROWS, window), 0) < 4
    conv_own = LAND_CONVEYANCE + (RIVER_CONVEYANCE - LAND_CONVEYANCE) * river_ref[:, cut].astype(jnp.float32)

    def extended(place, own):
        lanes = pl.ds(place * window, window)
        own = pltpu.roll(own, 4, 0)
        above = pltpu.roll(from_above[tail, lanes], 4, 0)
        below = from_below[tail, lanes]
        return jnp.concatenate(
            [jnp.where(upper_half, above, own), jnp.where(upper_half, own, below)], axis=0
        )

    pond = extended(0, pond_ref[:, cut])
    ground = extended(1, ground_ref[:, cut])
    conv = extended(2, conv_own)
    row = lax.broadcasted_iota(jnp.int32, conv.shape, 0)
    outside = ((row < 4) & (lat == 0)) | ((row >= 12) & (lat == lax.axis_size("lat") - 1))
    conv = jnp.where(outside, 0.0, conv)
    k_down = face_k(pond, ground, conv, lambda x: shift_rows(x, -1))
    k_up = shift_rows(k_down, 1)
    k_right = face_k(pond, ground, conv, lambda x: shift_lanes(x, -1))
    lane = lax.broadcasted_iota(jnp.int32, conv.shape, 1)
    k_right = jnp.where(lane < window - 1, k_right, 0.0)
    k_left = shift_lanes(k_right, 1)
    diag = 1.0 / SURFACE_STEP + k_up + k_down + k_left + k_right
    rhs = pond * (1.0 / SURFACE_STEP)
    rhs = rhs + k_up * (shift_rows(ground, 1) - ground) + k_down * (shift_rows(ground, -1) - ground)
    rhs = rhs + k_left * (shift_lanes(ground, 1) - ground) + k_right * (shift_lanes(ground, -1) - ground)
    inv = rcp(diag)
    level_ref[...] = pond
    for place, value in enumerate((k_up * inv, k_down * inv, k_left * inv, k_right * inv, rhs * inv, inv)):
        terms_ref[place] = value


def sweep_kernel(level_ref, terms_ref, exfil_ref, out_ref, last):
    quarter = out_ref.shape[1]
    k_up, k_down, k_left, k_right = (terms_ref[place] for place in range(4))
    rhs = terms_ref[4] + terms_ref[5] * exfil_ref[...]
    level = level_ref[...]
    for _ in range(SWEEPS):
        level = (
            rhs
            + k_up * shift_rows(level, 1)
            + k_down * shift_rows(level, -1)
            + k_left * shift_lanes(level, 1)
            + k_right * shift_lanes(level, -1)
        )
    last[...] = level
    depth = lax.axis_index("depth")
    start = pl.multiple_of(
        depth * quarter - window_start(depth, quarter, quarter + 2 * LANES), LANES
    )
    cut = pl.ds(start, quarter)
    lower_half = lax.broadcasted_iota(jnp.int32, (ROWS, quarter), 0) >= 4
    upper = pltpu.roll(last[pl.ds(0, ROWS), cut], 4, 0)
    lower = pltpu.roll(last[pl.ds(ROWS, ROWS), cut], 4, 0)
    out_ref[...] = jnp.where(lower_half, lower, upper)


def per_device(
    head, head_old, soil, cond_table, shape_table, pore_table, pond, ground, ponded, river
):
    nz, rows, width = head.shape
    window = width // 4 + 2 * LANES
    cells = nz * rows * width
    lat_count = lax.axis_size("lat")
    depth = lax.axis_index("depth")
    up = [(i, (i + 1) % lat_count) for i in range(lat_count)]
    down = [(j, i) for i, j in up]
    core = [(0, 1), (1, 0), (2, 3), (3, 2)]
    chip = [(0, 2), (2, 0), (1, 3), (3, 1)]

    own_up, own_down, exfil = pl.pallas_call(
        pack_kernel,
        out_shape=[f32(2 * nz + ROWS, width), f32(2 * nz + ROWS, width), f32(rows, width)],
        in_specs=[SMEM, SMEM, ANY, ANY, VMEM, VMEM, VMEM, VMEM],
        out_specs=[VMEM] * 3,
        scratch_shapes=[
            pltpu.VMEM((2, nz, width), jnp.int32),
            pltpu.VMEM((rows, width), jnp.int32),
            pltpu.VMEM((rows, width), jnp.float32),
            pltpu.SemaphoreType.DMA((6,)),
        ],
        compiler_params=params(),
        cost_estimate=cost(cells // 4),
        name="pack",
    )(cond_table, shape_table, head, soil, pond, ground, ponded, river)
    from_above = lax.ppermute(own_up, "lat", up)
    from_below = lax.ppermute(own_down, "lat", down)

    block = f32(nz, rows, width)
    head_v = in_vmem(head)
    base, ratio, inv, top_col, bottom_col, resist, sums, row_values = pl.pallas_call(
        cells_kernel,
        out_shape=[block] * 5 + [f32(3 * rows, width), f32(2 * rows, width), f32(6, nz, width)],
        in_specs=[SMEM] * 3 + [VMEM] * 5,
        out_specs=[VMEM] * 8,
        scratch_shapes=[
            pltpu.VMEM((nz, rows, width + LANES), jnp.float32),
            pltpu.VMEM((nz, rows, width + LANES), jnp.float32),
            pltpu.VMEM((nz, rows, LANES), jnp.float32),
            pltpu.SemaphoreType.DMA((6,)),
        ],
        compiler_params=params(),
        cost_estimate=cost(cells * 150, 20 * cells),
        name="cells",
    )(cond_table, shape_table, pore_table, head_v, in_vmem(head_old), in_vmem(soil), pond, ponded)

    even = depth % 2 == 0
    inner = (depth == 1) | (depth == 2)
    sign = jnp.where(depth < 2, 1.0, -1.0)
    r_top, r_bottom, corner = (resist[i * rows : (i + 1) * rows] for i in range(3))
    mine = jnp.concatenate([jnp.where(even, r_bottom, r_top), jnp.where(even, r_top, r_bottom), corner], 0)
    partner = lax.ppermute(mine, "depth", core)
    pair_inv = 1.0 / (mine[:rows] + partner[:rows])
    inner_corner = jnp.where(inner, mine[2 * rows :], partner[2 * rows :])
    gain = inner_corner * pair_inv
    chip_res = jnp.where(inner, mine[rows : 2 * rows], partner[rows : 2 * rows]) - inner_corner * gain
    chip_res_other = lax.ppermute(chip_res, "depth", chip)

    ends, flux, sent, kept = pl.pallas_call(
        halo_kernel,
        out_shape=[f32(2 * rows, width), f32(2, nz, width), f32(2 * rows, 2 * window), f32(2 * rows, 2 * window)],
        in_specs=[SMEM] * 2 + [VMEM] * 7,
        out_specs=[VMEM] * 4,
        compiler_params=params(),
        cost_estimate=cost(cells * 8),
        name="halo",
    )(
        cond_table, shape_table, in_vmem(own_up), in_vmem(own_down), in_vmem(from_above), in_vmem(from_below),
        in_vmem(row_values), in_vmem(sums), in_vmem(exfil),
    )
    ends_other = lax.ppermute(ends, "depth", core)
    exfil_core = lax.ppermute(sent, "depth", core)
    local = pl.pallas_call(
        local_kernel,
        out_shape=block,
        in_specs=[VMEM] * 5,
        out_specs=VMEM,
        compiler_params=params(),
        cost_estimate=cost(cells * 10),
        name="local",
    )(in_vmem(flux), in_vmem(base), in_vmem(ratio), in_vmem(inv), head_v)

    gap = sign * jnp.where(inner, ends_other[:rows] - ends[:rows], ends[:rows] - ends_other[:rows]) + 1.0
    chip_end = jnp.where(inner, ends[rows:], ends_other[rows:]) + sign * gain * gap
    chip_end_other = lax.ppermute(chip_end, "depth", chip)
    exfil_chip = lax.ppermute(
        jnp.where(depth == 0, kept[:, window:], exfil_core[:, window:]), "depth", chip
    )
    level, terms = pl.pallas_call(
        surface_kernel,
        out_shape=[f32(2 * rows, window), f32(6, 2 * rows, window)],
        in_specs=[VMEM] * 5,
        out_specs=[VMEM] * 2,
        compiler_params=params(),
        cost_estimate=cost(cells * 10),
        name="surface",
    )(pond, ground, river, in_vmem(from_above), in_vmem(from_below))

    flow_chip = (sign * (chip_end - chip_end_other) + 1.0) / (chip_res + chip_res_other)
    flow_core = gap * pair_inv + gain * flow_chip
    flow_in = jnp.where(depth == 0, 0.0, jnp.where(depth == 2, flow_chip, flow_core))
    flow_out = jnp.where(depth == 3, 0.0, jnp.where(depth == 1, flow_chip, flow_core))
    head_new = pl.pallas_call(
        final_kernel,
        out_shape=jax.ShapeDtypeStruct((nz, rows, width), jnp.float32),
        in_specs=[VMEM] * 5,
        out_specs=VMEM,
        compiler_params=params(),
        cost_estimate=cost(cells * 4),
        name="final",
    )(in_vmem(local), in_vmem(top_col), in_vmem(bottom_col), flow_in, flow_out)

    exfil_near = jnp.where(depth == 0, kept[:, :window], exfil_core[:, :window])
    exfil_window = jnp.where(depth < 2, exfil_near, exfil_chip)
    surface_new = pl.pallas_call(
        sweep_kernel,
        out_shape=jax.ShapeDtypeStruct((rows, width // 4), jnp.float32),
        in_specs=[VMEM] * 3,
        out_specs=VMEM,
        scratch_shapes=[pltpu.VMEM((2 * rows, window), jnp.float32)],
        compiler_params=params(),
        cost_estimate=cost(cells),
        name="sweep",
    )(in_vmem(level), in_vmem(terms), exfil_window)
    return (head_new, surface_new)


def solution(mesh):
    placed = (
        P("depth", "lat", None),
        P("depth", "lat", None),
        P("depth", "lat", None),
        P(),
        P(),
        P(),
        P("lat", None),
        P("lat", None),
        P("lat", None),
        P("lat", None),
    )
    return jax.shard_map(
        per_device,
        mesh=mesh,
        in_specs=placed,
        out_specs=(P("depth", "lat", None), P("lat", "depth")),
        check_vma=False,
    )
```

```python
import jax
import jax.numpy as jnp
from jax import lax
from jax.experimental import pallas as pl
from jax.experimental.pallas import tpu as pltpu
from jax.sharding import PartitionSpec as P

SWEEPS = 4

TIME_STEP = 20.0
SURFACE_STEP = 2.0
SPECIFIC_STORAGE = 0.01
LAND_CONVEYANCE = 3.0
RIVER_CONVEYANCE = 10.0
SLOPE_FLOOR = 0.01

LOG2E = 1.4426950408889634
LN2 = 0.6931471805599453
CLOSED = 1e37

LANES = 128
ROWS = 8
CHUNK = 512
VMEM_LIMIT = 6 * 1024 * 1024

VMEM = pl.BlockSpec(memory_space=pltpu.VMEM)
ANY = pl.BlockSpec(memory_space=pl.ANY)


def f32(*shape):
    return pltpu.VMEM(shape, jnp.float32)


def in_vmem(x):
    return pltpu.with_memory_space_constraint(x, pltpu.VMEM)


def in_hbm(x):
    return pltpu.with_memory_space_constraint(x, pltpu.HBM)


def call(kernel, name, args, out_shape, time, out_specs=None, scratch=()):
    from_program = kernel is pack_kernel
    return pl.pallas_call(
        kernel,
        out_shape=out_shape,
        in_specs=[ANY if from_program else VMEM] * len(args),
        out_specs=out_specs or [VMEM] * len(out_shape),
        scratch_shapes=list(scratch),
        compiler_params=pltpu.CompilerParams(vmem_limit_bytes=VMEM_LIMIT),
        cost_estimate=pl.CostEstimate(flops=0, bytes_accessed=int(time * 3e6), transcendentals=0),
        name=name,
    )(*(args if from_program else map(in_vmem, args)))


def rcp(x):
    r = pl.reciprocal(x, approx=True)
    return r * (2.0 - x * r)


def lookup(table, soil):
    blocks = []
    for top in range(0, soil.shape[0], ROWS):
        parts = []
        for start in range(0, soil.shape[1], LANES):
            index = soil[top : top + ROWS, start : start + LANES]
            parts.append(jnp.take_along_axis(table, index, axis=1, mode="promise_in_bounds"))
        blocks.append(jnp.concatenate(parts, axis=1) if len(parts) > 1 else parts[0])
    return jnp.concatenate(blocks, axis=0) if len(blocks) > 1 else blocks[0]


def window_start(quarter, width, window):
    return jnp.clip(quarter * width - LANES, 0, 4 * width - window)


def pack_kernel(
    cond_ref, shape_ref, pore_ref, head_ref, old_ref, soil_ref, pond_ref, ground_ref, ponded_ref, river_ref,
    up_ref, down_ref, exfil_ref, table_ref, head_out, old_out, soil_out,
    small, pond, ground, ponded, river, sem,
):
    nz = head_ref.shape[0]
    width = pond_ref.shape[1]
    quarter = width // 4
    window = quarter + 2 * LANES
    start = pl.multiple_of(window_start(lax.axis_index("depth"), quarter, window), LANES)
    cut = pl.ds(start, window)
    pieces = 4
    piece = width // pieces
    pairs = [
        (cond_ref, small.at[0]),
        (shape_ref, small.at[1]),
        (pore_ref, small.at[2]),
        (pond_ref, pond),
        (ponded_ref, ponded),
        (ground_ref.at[:, cut], ground),
        (river_ref.at[:, cut], river),
    ]
    for part in range(pieces):
        lanes = pl.ds(part * piece, piece)
        pairs.append((soil_ref.at[:, :, lanes], soil_out.at[:, :, lanes]))
        pairs.append((head_ref.at[:, :, lanes], head_out.at[:, :, lanes]))
    pairs.append((old_ref, old_out))
    copies = [pltpu.make_async_copy(source, target, sem.at[i]) for i, (source, target) in enumerate(pairs)]
    for copy in copies:
        copy.start()
    head_out[:, :, pl.ds(width, LANES)] = jnp.zeros((nz, ROWS, LANES), jnp.float32)

    for copy in copies[:3]:
        copy.wait()
    lane = lax.broadcasted_iota(jnp.int32, (ROWS, LANES), 1)
    registers = []
    for place in range(3):
        value = jnp.ones((ROWS, LANES), jnp.float32)
        for soil_kind in range(cond_ref.shape[0]):
            value = jnp.where(lane == soil_kind, small[place, soil_kind], value)
        registers.append(value)
    cond_table, shape_table, pore_table = registers
    half_res = 0.5 / cond_table
    steep = shape_table * LOG2E
    pore_table = pore_table * (1.0 / TIME_STEP)
    for place, value in enumerate((half_res, steep, pore_table, pore_table * shape_table)):
        table_ref[place] = value

    for copy in copies[3:7]:
        copy.wait()
    tail = pl.ds(2 * nz, ROWS)
    sublane = lax.broadcasted_iota(jnp.int32, (ROWS, piece), 0)
    for part in range(pieces):
        copies[7 + 2 * part].wait()
        copies[8 + 2 * part].wait()
        lanes = pl.ds(part * piece, piece)
        soil, head = soil_out[0, :, lanes], head_out[0, :, lanes]
        conductivity = lookup(cond_table, soil) * jnp.exp2(lookup(steep, soil) * jnp.minimum(head, 0.0))
        wet_pond = ponded[:, lanes].astype(jnp.float32) * pond[:, lanes]
        exfil = -conductivity * (2.0 * (wet_pond - head) + 1.0)
        exfil_ref[:, lanes] = exfil
        up_ref[tail, lanes] = pltpu.roll(exfil, 4, 0)
        down_ref[tail, lanes] = exfil
        for target, row in ((up_ref, ROWS - 1), (down_ref, 0)):
            for top in range(0, nz, ROWS):
                head = jnp.zeros((ROWS, piece), jnp.float32)
                soil = jnp.zeros((ROWS, piece), jnp.int32)
                for z in range(ROWS):
                    head = jnp.where(sublane == z, head_out[top + z, pl.ds(row, 1), lanes], head)
                    soil = jnp.where(sublane == z, soil_out[top + z, pl.ds(row, 1), lanes], soil)
                target[pl.ds(top, ROWS), lanes] = head
                target[pl.ds(nz + top, ROWS), lanes] = lookup(half_res, soil) * jnp.exp2(
                    -lookup(steep, soil) * jnp.minimum(head, 0.0)
                )
    lower_half = lax.broadcasted_iota(jnp.int32, (ROWS, window), 0) >= 4
    conv = LAND_CONVEYANCE + (RIVER_CONVEYANCE - LAND_CONVEYANCE) * river[...].astype(jnp.float32)
    for place, field in enumerate((pond[:, cut], ground[...], conv)):
        lanes = pl.ds(place * window, window)
        up_ref[tail, lanes] = jnp.where(lower_half, field, up_ref[tail, lanes])
        down_ref[tail, lanes] = jnp.where(lower_half, pltpu.roll(field, 4, 0), down_ref[tail, lanes])
    copies[-1].wait()


def factor_kernel(
    table_ref, head_ref, old_ref, soil_ref, exfil_ref,
    sigma, base, ratio, inv, top_col, bottom_col, resist_ref,
):
    nz, _, width = base.shape
    depth = lax.axis_index("depth")
    is_top = jnp.where(depth == 0, 1.0, 0.0)
    is_bottom = jnp.where(depth == 3, 1.0, 0.0)
    is_even = lax.rem(depth, 2) == 0
    half_res, steep, porosity, porosity_steep = (table_ref[place] for place in range(4))
    sigma[:, :, pl.ds(width, LANES)] = jnp.full((nz, ROWS, LANES), CLOSED, jnp.float32)

    @pl.loop(0, width // CHUNK)
    def _(chunk):
        lanes = pl.ds(pl.multiple_of(chunk * CHUNK, CHUNK), CHUNK)

        def state(z):
            head = head_ref[z, :, lanes]
            old = old_ref[z, :, lanes]
            soil = soil_ref[z, :, lanes]
            alpha = lookup(steep, soil)
            power = alpha * jnp.minimum(head, 0.0)
            wet = jnp.exp2(power)
            wet_old = jnp.exp2(alpha * jnp.minimum(old, 0.0))
            res = lookup(half_res, soil) * jnp.exp2(-power)
            sigma[z, :, lanes] = res
            storage = lookup(porosity, soil) * (wet_old - wet) + (SPECIFIC_STORAGE / TIME_STEP) * (old - head)
            capacity = SPECIFIC_STORAGE / TIME_STEP + lookup(porosity_steep, soil) * wet
            return head, res, storage, capacity

        now = state(0)
        sigma_top = now[1]
        face_above = flux_above = ratio_above = column = None
        for z in range(nz):
            head, res, b, d = now
            if z == 0:
                b = b - exfil_ref[:, lanes] * is_top
                d = d + rcp(res) * is_top
            else:
                b = b + flux_above
                d = d + face_above * (1.0 - ratio_above)
            if z == nz - 1:
                b = b - 0.5 * rcp(res) * is_bottom
            else:
                after = state(z + 1)
                face = rcp(res + after[1])
                flux = face * (head - after[0] + 1.0)
                b = b - flux
                d = d + face
            pivot_inv = rcp(d)
            base[z, :, lanes] = b
            inv[z, :, lanes] = pivot_inv
            column = pivot_inv if z == 0 else column * pivot_inv
            if z < nz - 1:
                ratio_above = face * pivot_inv
                ratio[z, :, lanes] = ratio_above
                top_col[z, :, lanes] = column
                column = column * face
                face_above, flux_above = face, flux
                now = after
        first, last = column, pivot_inv
        top_col[nz - 1, :, lanes] = first
        bottom_col[nz - 1, :, lanes] = last
        corner = first
        r_bottom = res + last
        for z in reversed(range(nz - 1)):
            m = ratio[z, :, lanes]
            first = top_col[z, :, lanes] + m * first
            last = m * last
            top_col[z, :, lanes] = first
            bottom_col[z, :, lanes] = last
        r_top = sigma_top + first
        resist_ref[pl.ds(0, ROWS), lanes] = jnp.where(is_even, r_bottom, r_top)
        resist_ref[pl.ds(ROWS, ROWS), lanes] = jnp.where(is_even, r_top, r_bottom)
        resist_ref[pl.ds(2 * ROWS, ROWS), lanes] = corner


def lateral_kernel(
    head_ref, sigma, base_in, top_col, bottom_col, base, sums_ref, last_flux,
):
    nz, _, width = base.shape
    last_flux[...] = jnp.zeros_like(last_flux)
    sublane = lax.broadcasted_iota(jnp.int32, (ROWS, CHUNK), 0)
    inner = sublane < ROWS - 1

    @pl.loop(0, width // CHUNK)
    def _(chunk):
        start = pl.multiple_of(chunk * CHUNK, CHUNK)
        lanes = pl.ds(start, CHUNK)
        wide = pl.ds(start, CHUNK + LANES)
        top_sum = bottom_sum = None
        for z in range(nz):
            sw, hw = sigma[z, :, wide], head_ref[z, :, wide]
            s, h = sw[:, :CHUNK], hw[:, :CHUNK]
            s_right = pltpu.roll(sw, CHUNK + LANES - 1, 1)[:, :CHUNK]
            h_right = pltpu.roll(hw, CHUNK + LANES - 1, 1)[:, :CHUNK]
            flux_y = rcp(s + s_right) * (h_right - h)
            shifted = jnp.concatenate([last_flux[z], flux_y], axis=1)
            flux_left = pltpu.roll(shifted, 1, 1)[:, LANES:]
            last_flux[z] = flux_y[:, CHUNK - LANES :]
            flux_x = rcp(s + pltpu.roll(s, ROWS - 1, 0)) * (pltpu.roll(h, ROWS - 1, 0) - h)
            flux_x = jnp.where(inner, flux_x, 0.0)
            b = base_in[z, :, lanes] + (flux_y - flux_left) + (flux_x - pltpu.roll(flux_x, 1, 0))
            base[z, :, lanes] = b
            first = top_col[z, :, lanes] * b
            last = bottom_col[z, :, lanes] * b
            top_sum = first if z == 0 else top_sum + first
            bottom_sum = last if z == 0 else bottom_sum + last
        sums_ref[pl.ds(0, ROWS), lanes] = top_sum + head_ref[0, :, lanes]
        sums_ref[pl.ds(ROWS, ROWS), lanes] = bottom_sum + head_ref[nz - 1, :, lanes]


def pair_kernel(mine, other, pair_inv_ref, gain_ref, chip_res_ref):
    depth = lax.axis_index("depth")
    inner = (depth == 1) | (depth == 2)
    near, far, corner = (pl.ds(place * ROWS, ROWS) for place in range(3))
    pair_inv = rcp(mine[near, :] + other[near, :])
    inner_corner = jnp.where(inner, mine[corner, :], other[corner, :])
    gain = inner_corner * pair_inv
    pair_inv_ref[...] = pair_inv
    gain_ref[...] = gain
    chip_res_ref[...] = jnp.where(inner, mine[far, :], other[far, :]) - inner_corner * gain


def halo_kernel(
    own_up, own_down, from_above, from_below, top_col, bottom_col, sums_ref, exfil_ref,
    flux_ref, sent_ref, kept_ref,
):
    nz = top_col.shape[0]
    width = own_up.shape[1]
    quarter = width // 4
    window = quarter + 2 * LANES
    lat = lax.axis_index("lat")
    has_above = jnp.where(lat == 0, 0.0, 1.0)
    has_below = jnp.where(lat == lax.axis_size("lat") - 1, 0.0, 1.0)
    is_even = lax.rem(lax.axis_index("depth"), 2) == 0
    heads, sigmas = pl.ds(0, nz), pl.ds(nz, nz)
    sublane = lax.broadcasted_iota(jnp.int32, (ROWS, CHUNK), 0)
    for side, other, own, scale in ((0, from_below, own_up, has_below), (1, from_above, own_down, has_above)):
        flux_ref[side] = rcp(other[sigmas, :] + own[sigmas, :]) * ((other[heads, :] - own[heads, :]) * scale)

    @pl.loop(0, width // CHUNK)
    def _(chunk):
        lanes = pl.ds(pl.multiple_of(chunk * CHUNK, CHUNK), CHUNK)
        top_sum = sums_ref[pl.ds(0, ROWS), lanes]
        bottom_sum = sums_ref[pl.ds(ROWS, ROWS), lanes]
        for z in range(nz):
            added = jnp.where(sublane == 0, flux_ref[1, pl.ds(z, 1), lanes], 0.0)
            added = jnp.where(sublane == ROWS - 1, flux_ref[0, pl.ds(z, 1), lanes], added)
            top_sum = top_sum + top_col[z, :, lanes] * added
            bottom_sum = bottom_sum + bottom_col[z, :, lanes] * added
        sent_ref[pl.ds(0, ROWS), lanes] = jnp.where(is_even, bottom_sum, top_sum)
        sent_ref[pl.ds(ROWS, ROWS), lanes] = jnp.where(is_even, top_sum, bottom_sum)

    upper_half = lax.broadcasted_iota(jnp.int32, (ROWS, window), 0) < 4
    tail = pl.ds(2 * nz, ROWS)
    for place in range(4):
        lanes = pl.ds(min(max(place * quarter - LANES, 0), width - window), window)
        own = pltpu.roll(exfil_ref[:, lanes], 4, 0)
        above = from_above[tail, lanes]
        below = pltpu.roll(from_below[tail, lanes], 4, 0)
        if place % 2:
            target, into = sent_ref, pl.ds(width + (place // 2) * window, window)
        else:
            target, into = kept_ref, pl.ds((place // 2) * window, window)
        target[pl.ds(0, ROWS), into] = jnp.where(upper_half, above, own)
        target[pl.ds(ROWS, ROWS), into] = jnp.where(upper_half, own, below)


def local_kernel(flux_ref, base, ratio, inv, head_ref, out_ref):
    nz, _, width = base.shape
    sublane = lax.broadcasted_iota(jnp.int32, (ROWS, CHUNK), 0)

    @pl.loop(0, width // CHUNK)
    def _(chunk):
        lanes = pl.ds(pl.multiple_of(chunk * CHUNK, CHUNK), CHUNK)
        y = None
        for z in range(nz):
            added = jnp.where(sublane == 0, flux_ref[1, pl.ds(z, 1), lanes], 0.0)
            added = jnp.where(sublane == ROWS - 1, flux_ref[0, pl.ds(z, 1), lanes], added)
            rhs = base[z, :, lanes] + added
            y = rhs if z == 0 else rhs + ratio[z - 1, :, lanes] * y
            if z < nz - 1:
                out_ref[z, :, lanes] = y
        x = y * inv[nz - 1, :, lanes]
        out_ref[nz - 1, :, lanes] = x + head_ref[nz - 1, :, lanes]
        for z in reversed(range(nz - 1)):
            x = out_ref[z, :, lanes] * inv[z, :, lanes] + ratio[z, :, lanes] * x
            out_ref[z, :, lanes] = x + head_ref[z, :, lanes]


def ends_kernel(mine, other, kept, pair_inv_ref, gain_ref, gap_ref, chip_end_ref, exfil_ref):
    width = gap_ref.shape[1]
    window = exfil_ref.shape[1]
    depth = lax.axis_index("depth")
    inner = (depth == 1) | (depth == 2)
    sign = jnp.where(depth < 2, 1.0, -1.0)
    lanes = pl.ds(0, width)
    near, far = pl.ds(0, ROWS), pl.ds(ROWS, ROWS)
    own, others = mine[near, lanes], other[near, lanes]
    gap = sign * jnp.where(inner, others - own, own - others) + 1.0
    gap_ref[...] = gap * pair_inv_ref[...]
    chip_end_ref[...] = jnp.where(inner, mine[far, lanes], other[far, lanes]) + sign * gain_ref[...] * gap
    exfil_ref[...] = jnp.where(
        depth == 0, kept[:, pl.ds(window, window)], other[:, pl.ds(width + window, window)]
    )


def final_kernel(
    local_ref, top_col, bottom_col, gap_ref, gain_ref, res_ref, res_other, end_ref, end_other, out_ref, held, sem
):
    nz, _, width = local_ref.shape
    depth = lax.axis_index("depth")
    sign = jnp.where(depth < 2, 1.0, -1.0)

    def out_copy(chunk):
        lanes = pl.ds(pl.multiple_of(chunk * CHUNK, CHUNK), CHUNK)
        return pltpu.make_async_copy(held.at[:, :, lanes], out_ref.at[:, :, lanes], sem.at[chunk])

    @pl.loop(0, width // CHUNK)
    def _(chunk):
        lanes = pl.ds(pl.multiple_of(chunk * CHUNK, CHUNK), CHUNK)
        flow_chip = (sign * (end_ref[:, lanes] - end_other[:, lanes]) + 1.0) * rcp(
            res_ref[:, lanes] + res_other[:, lanes]
        )
        flow_core = gap_ref[:, lanes] + gain_ref[:, lanes] * flow_chip
        j_in = jnp.where(depth == 0, 0.0, jnp.where(depth == 2, flow_chip, flow_core))
        j_out = jnp.where(depth == 3, 0.0, jnp.where(depth == 1, flow_chip, flow_core))
        for z in range(nz):
            held[z, :, lanes] = (
                local_ref[z, :, lanes] + top_col[z, :, lanes] * j_in - bottom_col[z, :, lanes] * j_out
            )
        out_copy(chunk).start()

    @pl.loop(0, width // CHUNK)
    def _(chunk):
        out_copy(chunk).wait()


def shift_rows(x, by):
    return pltpu.roll(x, by % x.shape[0], 0)


def shift_lanes(x, by):
    return pltpu.roll(x, by % x.shape[1], 1)


def harmonic(first, second):
    total = first + second
    return 2.0 * first * second * rcp(jnp.where(total > 0.0, total, 1.0))


def face_k(pond, ground, conv, shift):
    pond_two, ground_two, conv_two = shift(pond), shift(ground), shift(conv)
    depth_face = 0.5 * (pond + pond_two)
    slope = pond_two + ground_two - (pond + ground)
    return (
        jnp.exp2((5.0 / 3.0 * LOG2E) * jnp.log(depth_face))
        * harmonic(conv, conv_two)
        * lax.rsqrt(jnp.abs(slope) + SLOPE_FLOOR)
    )


def surface_kernel(
    own_up, own_down, from_above, from_below, level_ref, terms_ref,
):
    window = level_ref.shape[1]
    tail = pl.ds(from_above.shape[0] - ROWS, ROWS)
    lat = lax.axis_index("lat")
    upper_half = lax.broadcasted_iota(jnp.int32, (ROWS, window), 0) < 4

    def extended(place):
        lanes = pl.ds(place * window, window)
        above = pltpu.roll(from_above[tail, lanes], 4, 0)
        first = own_down[tail, lanes]
        last = pltpu.roll(own_up[tail, lanes], 4, 0)
        below = from_below[tail, lanes]
        return jnp.concatenate(
            [jnp.where(upper_half, above, first), jnp.where(upper_half, last, below)], axis=0
        )

    pond, ground, conv = extended(0), extended(1), extended(2)
    row = lax.broadcasted_iota(jnp.int32, conv.shape, 0)
    outside = ((row < 4) & (lat == 0)) | ((row >= 12) & (lat == lax.axis_size("lat") - 1))
    conv = jnp.where(outside, 0.0, conv)
    k_down = face_k(pond, ground, conv, lambda x: shift_rows(x, -1))
    k_up = shift_rows(k_down, 1)
    k_right = face_k(pond, ground, conv, lambda x: shift_lanes(x, -1))
    lane = lax.broadcasted_iota(jnp.int32, conv.shape, 1)
    k_right = jnp.where(lane < window - 1, k_right, 0.0)
    k_left = shift_lanes(k_right, 1)
    diag = 1.0 / SURFACE_STEP + k_up + k_down + k_left + k_right
    rhs = pond * (1.0 / SURFACE_STEP)
    rhs = rhs + k_up * (shift_rows(ground, 1) - ground) + k_down * (shift_rows(ground, -1) - ground)
    rhs = rhs + k_left * (shift_lanes(ground, 1) - ground) + k_right * (shift_lanes(ground, -1) - ground)
    inv = rcp(diag)
    level_ref[...] = pond
    for place, value in enumerate((k_up * inv, k_down * inv, k_left * inv, k_right * inv, rhs * inv, inv)):
        terms_ref[place] = value


def sweep_kernel(level_ref, terms_ref, kept, from_core, from_chip, out_ref, last):
    quarter = out_ref.shape[1]
    window = level_ref.shape[1]
    depth = lax.axis_index("depth")
    k_up, k_down, k_left, k_right = (terms_ref[place] for place in range(4))
    near = from_core[:, pl.ds(from_core.shape[1] - 2 * window, window)]
    exfil = jnp.where(depth == 0, kept[:, pl.ds(0, window)], jnp.where(depth == 1, near, from_chip[...]))
    rhs = terms_ref[4] + terms_ref[5] * exfil
    level = level_ref[...]
    for _ in range(SWEEPS):
        level = (
            rhs
            + k_up * shift_rows(level, 1)
            + k_down * shift_rows(level, -1)
            + k_left * shift_lanes(level, 1)
            + k_right * shift_lanes(level, -1)
        )
    last[...] = level
    start = pl.multiple_of(
        depth * quarter - window_start(depth, quarter, quarter + 2 * LANES), LANES
    )
    cut = pl.ds(start, quarter)
    lower_half = lax.broadcasted_iota(jnp.int32, (ROWS, quarter), 0) >= 4
    upper = pltpu.roll(last[pl.ds(0, ROWS), cut], 4, 0)
    lower = pltpu.roll(last[pl.ds(ROWS, ROWS), cut], 4, 0)
    out_ref[...] = jnp.where(lower_half, lower, upper)


def per_device(
    head, head_old, soil, cond_table, shape_table, pore_table, pond, ground, ponded, river
):
    nz, rows, width = head.shape
    window = width // 4 + 2 * LANES
    lat_count = lax.axis_size("lat")
    up = [(i, (i + 1) % lat_count) for i in range(lat_count)]
    down = [(j, i) for i, j in up]
    core = [(0, 1), (1, 0), (2, 3), (3, 2)]
    chip = [(0, 2), (2, 0), (1, 3), (3, 1)]
    block = f32(nz, rows, width)
    padded = f32(nz, rows, width + LANES)
    plane = f32(rows, width)

    own_up, own_down, exfil, tables, head_v, old_v, soil_v = call(
        pack_kernel,
        "pack",
        [in_hbm(x) for x in (cond_table, shape_table, pore_table, head, head_old, soil, pond, ground, ponded, river)],
        [f32(2 * nz + rows, width)] * 2
        + [plane, f32(4, ROWS, LANES), padded, block, pltpu.VMEM((nz, rows, width), jnp.int32)],
        scratch=[
            pltpu.SMEM((3, cond_table.shape[0]), jnp.float32),
            pltpu.VMEM((rows, width), jnp.float32),
            pltpu.VMEM((rows, window), jnp.float32),
            pltpu.VMEM((rows, width), jnp.int32),
            pltpu.VMEM((rows, window), jnp.int32),
            pltpu.SemaphoreType.DMA((16,)),
        ],
        time=3,
    )
    from_above = lax.ppermute(own_up, "lat", up)
    from_below = lax.ppermute(own_down, "lat", down)

    sigma, base, ratio, inv, top_col, bottom_col, resist = call(
        factor_kernel,
        "factor",
        [tables, head_v, old_v, soil_v, exfil],
        [padded] + [block] * 5 + [f32(3 * rows, width)],
        time=8,
    )
    resist_other = lax.ppermute(resist, "depth", core)
    base, sums = call(
        lateral_kernel,
        "lateral",
        [head_v, sigma, base, top_col, bottom_col],
        [block, f32(2 * rows, width)],
        scratch=[pltpu.VMEM((nz, rows, LANES), jnp.float32)],
        time=6,
    )
    pair_inv, gain, chip_res = call(pair_kernel, "pair", [resist, resist_other], [plane] * 3, time=0.3)
    chip_res_other = lax.ppermute(chip_res, "depth", chip)

    flux, sent, kept = call(
        halo_kernel,
        "halo",
        [own_up, own_down, from_above, from_below, top_col, bottom_col, sums, exfil],
        [f32(2, nz, width), f32(2 * rows, width + 2 * window), f32(2 * rows, 2 * window)],
        time=2,
    )
    sent_other = lax.ppermute(sent, "depth", core)
    local = call(local_kernel, "local", [flux, base, ratio, inv, head_v], [block], time=1)[0]
    level, terms = call(
        surface_kernel,
        "surface",
        [own_up, own_down, from_above, from_below],
        [f32(2 * rows, window), f32(6, 2 * rows, window)],
        time=0.3,
    )
    gap, chip_end, exfil_out = call(
        ends_kernel, "ends", [sent, sent_other, kept, pair_inv, gain], [plane, plane, f32(2 * rows, window)], time=0.3
    )
    chip_end_other = lax.ppermute(chip_end, "depth", chip)
    exfil_chip = lax.ppermute(exfil_out, "depth", chip)
    head_new = call(
        final_kernel,
        "final",
        [local, top_col, bottom_col, gap, gain, chip_res, chip_res_other, chip_end, chip_end_other],
        [jax.ShapeDtypeStruct((nz, rows, width), jnp.float32)],
        out_specs=[ANY],
        scratch=[pltpu.VMEM((nz, rows, width), jnp.float32), pltpu.SemaphoreType.DMA((width // CHUNK,))],
        time=1.5,
    )[0]
    surface_new = call(
        sweep_kernel,
        "sweep",
        [level, terms, kept, sent_other, exfil_chip],
        [jax.ShapeDtypeStruct((rows, width // 4), jnp.float32)],
        scratch=[pltpu.VMEM((2 * rows, window), jnp.float32)],
        time=1,
    )[0]
    return (head_new, surface_new)


def solution(mesh):
    placed = (
        P("depth", "lat", None),
        P("depth", "lat", None),
        P("depth", "lat", None),
        P(),
        P(),
        P(),
        P("lat", None),
        P("lat", None),
        P("lat", None),
        P("lat", None),
    )
    return jax.shard_map(
        per_device,
        mesh=mesh,
        in_specs=placed,
        out_specs=(P("depth", "lat", None), P("lat", "depth")),
        check_vma=False,
    )
```

```python
import jax
import jax.numpy as jnp
from jax import lax
from jax.experimental import pallas as pl
from jax.experimental.pallas import tpu as pltpu
from jax.sharding import PartitionSpec as P

SWEEPS = 4

TIME_STEP = 20.0
SURFACE_STEP = 2.0
SPECIFIC_STORAGE = 0.01
LAND_CONVEYANCE = 3.0
RIVER_CONVEYANCE = 10.0
SLOPE_FLOOR = 0.01

LOG2E = 1.4426950408889634
LN2 = 0.6931471805599453
CLOSED = 1e37

LANES = 128
ROWS = 8
CHUNK = 512
AHEAD = 3
VMEM_LIMIT = 8 * 1024 * 1024

VMEM = pl.BlockSpec(memory_space=pltpu.VMEM)
ANY = pl.BlockSpec(memory_space=pl.ANY)


def f32(*shape):
    return pltpu.VMEM(shape, jnp.float32)


def in_vmem(x):
    return (VMEM, pltpu.with_memory_space_constraint(x, pltpu.VMEM))


def in_hbm(x):
    return (ANY, pltpu.with_memory_space_constraint(x, pltpu.HBM))


FLOPS = {}


def call(kernel, name, args, out_shape, out_specs=None, scratch=()):
    return pl.pallas_call(
        kernel,
        out_shape=out_shape,
        in_specs=[spec for spec, _ in args],
        out_specs=out_specs or [VMEM] * len(out_shape),
        scratch_shapes=list(scratch),
        compiler_params=pltpu.CompilerParams(vmem_limit_bytes=VMEM_LIMIT),
        cost_estimate=pl.CostEstimate(flops=FLOPS.get(name, 1), bytes_accessed=1, transcendentals=0),
        name=name,
    )(*(x for _, x in args))


def rcp(x):
    return pl.reciprocal(x, approx=True)


def lookup(table, soil):
    numbers = lax.GatherDimensionNumbers(
        offset_dims=(),
        collapsed_slice_dims=(0,),
        start_index_map=(0,),
        operand_batching_dims=(1,),
        start_indices_batching_dims=(1,),
    )
    low, high = table
    blocks = []
    for top in range(0, soil.shape[0], ROWS):
        parts = []
        for start in range(0, soil.shape[1], LANES):
            kind = soil[top : top + ROWS, start : start + LANES]
            index = (kind & (ROWS - 1))[..., None]
            found = [
                lax.gather(half, index, numbers, (1, 1), mode=lax.GatherScatterMode.PROMISE_IN_BOUNDS)
                for half in table
            ]
            parts.append(jnp.where(kind < ROWS, *found))
        blocks.append(jnp.concatenate(parts, axis=1) if len(parts) > 1 else parts[0])
    return jnp.concatenate(blocks, axis=0) if len(blocks) > 1 else blocks[0]


def window_start(quarter, width, window):
    return jnp.clip(quarter * width - LANES, 0, 4 * width - window)


def static_window(quarter, width, window):
    return pl.ds(min(max(quarter * width - LANES, 0), 4 * width - window), window)


def pack_kernel(
    cond_ref, shape_ref, pore_ref, head_ref, soil_ref, pond_ref, ground_ref, ponded_ref, river_ref,
    up_ref, down_ref, table_ref, exfil_ref, own_ref,
    small, soils, head_top, soil_top, pond, ground, ponded, river, sem,
):
    nz, _, width = head_ref.shape
    groups = nz // ROWS
    quarter = width // 4
    window = quarter + 2 * LANES
    half = width // 2
    depth = lax.axis_index("depth")
    sides = (up_ref, down_ref)
    pairs = [(cond_ref, small.at[0]), (shape_ref, small.at[1]), (pore_ref, small.at[2])]
    for group in range(groups):
        layers = pl.ds(group * ROWS, ROWS)
        for side, (target, row) in enumerate(zip(sides, (ROWS - 1, 0))):
            pairs.append((soil_ref.at[layers, row, :], soils.at[side, group]))
            pairs.append((head_ref.at[layers, row, :], target.at[:, pl.ds(group * width, width)]))
    pairs += [
        (head_ref.at[0], head_top),
        (soil_ref.at[0], soil_top),
        (pond_ref, pond),
        (ponded_ref, ponded),
        (ground_ref, ground),
        (river_ref, river),
    ]
    copies = [pltpu.make_async_copy(source, target, sem.at[i]) for i, (source, target) in enumerate(pairs)]
    for copy in copies:
        copy.start()

    for copy in copies[:3]:
        copy.wait()
    row = lax.broadcasted_iota(jnp.int32, (ROWS, LANES), 0)
    registers = []
    for place in range(3):
        halves = []
        for top in (0, ROWS):
            value = jnp.ones((ROWS, LANES), jnp.float32)
            for soil_kind in range(top, min(top + ROWS, cond_ref.shape[0])):
                value = jnp.where(row == soil_kind - top, small[place, soil_kind], value)
            halves.append(value)
        registers.append(halves)
    cond_table, shape_table, pore_table = registers
    half_res = [0.5 / value for value in cond_table]
    steep = [value * LOG2E for value in shape_table]
    pore_table = [value * (1.0 / TIME_STEP) for value in pore_table]
    for place, halves in enumerate((half_res, steep, pore_table)):
        table_ref[2 * place] = halves[0]
        table_ref[2 * place + 1] = halves[1]

    following = iter(copies[3:])
    for group in range(groups):
        for side, target in enumerate(sides):
            next(following).wait()
            next(following).wait()
            head = target[:, pl.ds(group * width, width)]
            soil = soils[side, group]
            target[:, pl.ds((groups + group) * width, width)] = lookup(half_res, soil) * jnp.exp2(
                -lookup(steep, soil) * jnp.minimum(head, 0.0)
            )
    for copy in following:
        copy.wait()
    wet_pond = ponded[...].astype(jnp.float32) * pond[...]
    conductivity = lookup(cond_table, soil_top[...]) * jnp.exp2(
        lookup(steep, soil_top[...]) * jnp.minimum(head_top[...], 0.0)
    )
    exfil = -conductivity * (2.0 * (wet_pond - head_top[...]) + 1.0)
    exfil_ref[...] = exfil
    conv = LAND_CONVEYANCE + (RIVER_CONVEYANCE - LAND_CONVEYANCE) * river[...].astype(jnp.float32)
    field = jnp.where(
        depth < 2, jnp.where(depth == 0, exfil, pond[...]), jnp.where(depth == 2, ground[...], conv)
    )
    upper = lax.broadcasted_iota(jnp.int32, (ROWS, half), 0) < 4
    into = pl.ds(2 * groups * width, half)
    left, right = field[:, :half], field[:, half:]
    up_ref[:, into] = jnp.where(upper, pltpu.roll(left, 4, 0), right)
    down_ref[:, into] = jnp.where(upper, left, pltpu.roll(right, 4, 0))
    cut = pl.ds(pl.multiple_of(window_start(depth, quarter, window), LANES), window)
    own_ref[0] = pond[:, cut]
    own_ref[1] = ground[:, cut]
    own_ref[2] = LAND_CONVEYANCE + (RIVER_CONVEYANCE - LAND_CONVEYANCE) * river[:, cut].astype(jnp.float32)


def factor_kernel(
    table_ref, exfil_ref, head_hbm, old_hbm, soil_hbm,
    head_ref, sigma, base, ratio, inv, top_col, bottom_col, resist_ref, old_ref, soil_ref, sem,
):
    nz, _, width = base.shape
    depth = lax.axis_index("depth")
    is_top = jnp.where(depth == 0, 1.0, 0.0)
    is_bottom = jnp.where(depth == 3, 1.0, 0.0)
    is_even = lax.rem(depth, 2) == 0
    chunks = width // CHUNK
    quarter = width // 4
    window = quarter + 2 * LANES
    for place in range(2):
        resist_ref[:, pl.ds(3 * width + place * window, window)] = exfil_ref[
            :, static_window(2 * place + 1, quarter, window)
        ]

    def fetch(chunk):
        lanes = pl.ds(pl.multiple_of(chunk * CHUNK, CHUNK), CHUNK)
        return [
            pltpu.make_async_copy(source.at[:, :, lanes], target.at[:, :, lanes], sem.at[i, chunk])
            for i, (source, target) in enumerate(((head_hbm, head_ref), (soil_hbm, soil_ref), (old_hbm, old_ref)))
        ]

    for chunk in range(AHEAD):
        for copy in fetch(chunk):
            copy.start()
    half_res, steep, porosity = ((table_ref[2 * place], table_ref[2 * place + 1]) for place in range(3))
    sigma[:, :, pl.ds(width, LANES)] = jnp.full((nz, ROWS, LANES), CLOSED, jnp.float32)
    head_ref[:, :, pl.ds(width, LANES)] = jnp.zeros((nz, ROWS, LANES), jnp.float32)

    @pl.loop(0, chunks)
    def _(chunk):
        lanes = pl.ds(pl.multiple_of(chunk * CHUNK, CHUNK), CHUNK)
        for copy in fetch(chunk):
            copy.wait()

        @pl.when(chunk + AHEAD < chunks)
        def _():
            for copy in fetch(chunk + AHEAD):
                copy.start()

        def state(z):
            head = head_ref[z, :, lanes]
            old = old_ref[z, :, lanes]
            soil = soil_ref[z, :, lanes]
            alpha = lookup(steep, soil)
            power = alpha * jnp.minimum(head, 0.0)
            wet = jnp.exp2(power)
            wet_old = jnp.exp2(alpha * jnp.minimum(old, 0.0))
            res = lookup(half_res, soil) * rcp(wet)
            sigma[z, :, lanes] = res
            pore = lookup(porosity, soil)
            pore_wet = pore * wet
            storage = pore * wet_old - pore_wet + (SPECIFIC_STORAGE / TIME_STEP) * (old - head)
            capacity = SPECIFIC_STORAGE / TIME_STEP + (alpha * LN2) * pore_wet
            return head, res, storage, capacity

        now = state(0)
        sigma_top = now[1]
        face_above = flux_above = ratio_above = column = None
        for z in range(nz):
            head, res, b, d = now
            if z == 0:
                b = b - exfil_ref[:, lanes] * is_top
                d = d + rcp(res) * is_top
            else:
                b = b + flux_above
                d = d + face_above * (1.0 - ratio_above)
            if z == nz - 1:
                b = b - 0.5 * rcp(res) * is_bottom
            else:
                after = state(z + 1)
                face = rcp(res + after[1])
                flux = face * (head - after[0] + 1.0)
                b = b - flux
                d = d + face
            pivot_inv = rcp(d)
            base[z, :, lanes] = b
            inv[z, :, lanes] = pivot_inv
            column = pivot_inv if z == 0 else column * pivot_inv
            if z < nz - 1:
                ratio_above = face * pivot_inv
                ratio[z, :, lanes] = ratio_above
                top_col[z, :, lanes] = column
                column = column * face
                face_above, flux_above = face, flux
                now = after
        first, last = column, pivot_inv
        top_col[nz - 1, :, lanes] = first
        bottom_col[nz - 1, :, lanes] = last
        corner = first
        r_bottom = res + last
        for z in reversed(range(nz - 1)):
            m = ratio[z, :, lanes]
            first = top_col[z, :, lanes] + m * first
            last = m * last
            top_col[z, :, lanes] = first
            bottom_col[z, :, lanes] = last
        r_top = sigma_top + first
        resist_ref[:, lanes] = jnp.where(is_even, r_bottom, r_top)
        resist_ref[:, pl.ds(pl.multiple_of(width + chunk * CHUNK, CHUNK), CHUNK)] = jnp.where(is_even, r_top, r_bottom)
        resist_ref[:, pl.ds(pl.multiple_of(2 * width + chunk * CHUNK, CHUNK), CHUNK)] = corner


def lateral_kernel(
    head_ref, sigma, base_in, top_col, bottom_col, base, sums_ref, carried,
):
    nz, _, width = base.shape
    sublane = lax.broadcasted_iota(jnp.int32, (ROWS, CHUNK), 0)
    inner = sublane < ROWS - 1
    lane = lax.broadcasted_iota(jnp.int32, (ROWS, LANES), 1)
    is_first, is_last = lane == 0, lane == LANES - 1
    count = CHUNK // LANES

    def left(x):
        return pltpu.roll(x, LANES - 1, 1)

    def registers(x):
        return [x[:, k * LANES : (k + 1) * LANES] for k in range(x.shape[1] // LANES)]

    for z in range(nz):
        carried[0, z] = left(sigma[z, :, pl.ds(0, LANES)])
        carried[1, z] = left(head_ref[z, :, pl.ds(0, LANES)])
        carried[2, z] = jnp.zeros((ROWS, LANES), jnp.float32)

    @pl.loop(0, width // CHUNK)
    def _(chunk):
        start = pl.multiple_of(chunk * CHUNK, CHUNK)
        lanes = pl.ds(start, CHUNK)
        after = pl.ds(pl.multiple_of(start + LANES, LANES), CHUNK)
        top_sum = bottom_sum = None
        for z in range(nz):
            s, h = sigma[z, :, lanes], head_ref[z, :, lanes]
            moved = []
            for place, array in ((0, sigma), (1, head_ref)):
                found = [carried[place, z]] + [left(x) for x in registers(array[z, :, after])]
                carried[place, z] = found[count]
                moved.append(
                    jnp.concatenate(
                        [jnp.where(is_last, found[k + 1], found[k]) for k in range(count)], axis=1
                    )
                )
            s_right, h_right = moved
            flux_y = rcp(s + s_right) * (h_right - h)
            found = [carried[2, z]] + [pltpu.roll(x, 1, 1) for x in registers(flux_y)]
            carried[2, z] = found[count]
            flux_left = jnp.concatenate(
                [jnp.where(is_first, found[k], found[k + 1]) for k in range(count)], axis=1
            )
            flux_x = rcp(s + pltpu.roll(s, ROWS - 1, 0)) * (pltpu.roll(h, ROWS - 1, 0) - h)
            flux_x = jnp.where(inner, flux_x, 0.0)
            b = base_in[z, :, lanes] + (flux_y - flux_left) + (flux_x - pltpu.roll(flux_x, 1, 0))
            base[z, :, lanes] = b
            first = top_col[z, :, lanes] * b
            last = bottom_col[z, :, lanes] * b
            top_sum = first if z == 0 else top_sum + first
            bottom_sum = last if z == 0 else bottom_sum + last
        sums_ref[pl.ds(0, ROWS), lanes] = top_sum + head_ref[0, :, lanes]
        sums_ref[pl.ds(ROWS, ROWS), lanes] = bottom_sum + head_ref[nz - 1, :, lanes]


def pair_kernel(mine, other, exfil_ref, _, pair_inv_ref, gain_ref, sent_ref):
    width = gain_ref.shape[1]
    window = sent_ref.shape[1] - width
    depth = lax.axis_index("depth")
    inner = (depth == 1) | (depth == 2)
    near, far, corner = (pl.ds(place * width, width) for place in range(3))
    pair_inv = rcp(mine[:, near] + other[:, near])
    inner_corner = jnp.where(inner, mine[:, corner], other[:, corner])
    gain = inner_corner * pair_inv
    pair_inv_ref[...] = pair_inv
    gain_ref[...] = gain
    sent_ref[:, pl.ds(0, width)] = jnp.where(inner, mine[:, far], other[:, far]) - inner_corner * gain
    sent_ref[:, pl.ds(width, window)] = jnp.where(
        depth == 0, exfil_ref[:, static_window(2, width // 4, window)], other[:, pl.ds(3 * width + window, window)]
    )


def halo_kernel(
    own_up, own_down, from_above, from_below, top_col, bottom_col, sums_ref, _, flux_ref, sent_ref, rows_ref, windows_ref,
):
    nz, _, width = top_col.shape
    lat = lax.axis_index("lat")
    has_above = jnp.where(lat == 0, 0.0, 1.0)
    has_below = jnp.where(lat == lax.axis_size("lat") - 1, 0.0, 1.0)
    is_even = lax.rem(lax.axis_index("depth"), 2) == 0
    sublane = lax.broadcasted_iota(jnp.int32, (ROWS, CHUNK), 0)
    for side, other, own, scale in ((0, from_below, own_up, has_below), (1, from_above, own_down, has_above)):
        for group in range(nz // ROWS):
            heads = pl.ds(group * width, width)
            sigmas = pl.ds((nz // ROWS + group) * width, width)
            flux_ref[side, pl.ds(group * ROWS, ROWS), :] = rcp(other[:, sigmas] + own[:, sigmas]) * (
                (other[:, heads] - own[:, heads]) * scale
            )

    @pl.loop(0, width // CHUNK)
    def _(chunk):
        lanes = pl.ds(pl.multiple_of(chunk * CHUNK, CHUNK), CHUNK)
        top_sum = sums_ref[pl.ds(0, ROWS), lanes]
        bottom_sum = sums_ref[pl.ds(ROWS, ROWS), lanes]
        for z in range(nz):
            row = pl.ds(z, 1)
            added = jnp.where(sublane == 0, flux_ref[1, row, lanes], 0.0)
            added = jnp.where(sublane == ROWS - 1, flux_ref[0, row, lanes], added)
            top_sum = top_sum + top_col[z, :, lanes] * added
            bottom_sum = bottom_sum + bottom_col[z, :, lanes] * added
        sent_ref[pl.ds(0, ROWS), lanes] = jnp.where(is_even, bottom_sum, top_sum)
        sent_ref[pl.ds(ROWS, ROWS), lanes] = jnp.where(is_even, top_sum, bottom_sum)

    half = width // 2
    extra = pl.ds(own_up.shape[1] - half, half)
    upper = lax.broadcasted_iota(jnp.int32, (ROWS, half), 0) < 4
    above, below = from_above[:, extra], from_below[:, extra]
    rows_ref[:, pl.ds(0, half)] = jnp.where(upper, above, pltpu.roll(below, 4, 0))
    rows_ref[:, pl.ds(half, half)] = jnp.where(upper, pltpu.roll(above, 4, 0), below)
    quarter = width // 4
    window = windows_ref.shape[1] // 2
    depth = lax.axis_index("depth")
    for place, quarters in enumerate((depth ^ 1, depth ^ 3)):
        cut = pl.ds(pl.multiple_of(window_start(quarters, quarter, window), LANES), window)
        windows_ref[:, pl.ds(place * window, window)] = rows_ref[:, cut]


def local_kernel(flux_ref, base, ratio, inv, head_ref, out_ref):
    nz, _, width = base.shape
    sublane = lax.broadcasted_iota(jnp.int32, (ROWS, CHUNK), 0)

    @pl.loop(0, width // CHUNK)
    def _(chunk):
        lanes = pl.ds(pl.multiple_of(chunk * CHUNK, CHUNK), CHUNK)
        y = None
        for z in range(nz):
            row = pl.ds(z, 1)
            added = jnp.where(sublane == 0, flux_ref[1, row, lanes], 0.0)
            added = jnp.where(sublane == ROWS - 1, flux_ref[0, row, lanes], added)
            rhs = base[z, :, lanes] + added
            y = rhs if z == 0 else rhs + ratio[z - 1, :, lanes] * y
            if z < nz - 1:
                out_ref[z, :, lanes] = y
        x = y * inv[nz - 1, :, lanes]
        out_ref[nz - 1, :, lanes] = x + head_ref[nz - 1, :, lanes]
        for z in reversed(range(nz - 1)):
            x = out_ref[z, :, lanes] * inv[z, :, lanes] + ratio[z, :, lanes] * x
            out_ref[z, :, lanes] = x + head_ref[z, :, lanes]


def ends_kernel(mine, other, pair_inv_ref, gain_ref, gap_ref, chip_end_ref):
    depth = lax.axis_index("depth")
    inner = (depth == 1) | (depth == 2)
    sign = jnp.where(depth < 2, 1.0, -1.0)
    near, far = pl.ds(0, ROWS), pl.ds(ROWS, ROWS)
    own, others = mine[near, :], other[near, :]
    gap = sign * jnp.where(inner, others - own, own - others) + 1.0
    gap_ref[...] = gap * pair_inv_ref[...]
    chip_end_ref[...] = jnp.where(inner, mine[far, :], other[far, :]) + sign * gain_ref[...] * gap


def final_kernel(
    local_ref, top_col, bottom_col, gap_ref, gain_ref, res_ref, res_other, end_ref, end_other,
    out_ref, token_ref, held, sem,
):
    nz, _, width = local_ref.shape
    depth = lax.axis_index("depth")
    sign = jnp.where(depth < 2, 1.0, -1.0)

    token_ref[...] = jnp.zeros_like(token_ref)

    def out_copy(chunk):
        lanes = pl.ds(pl.multiple_of(chunk * CHUNK, CHUNK), CHUNK)
        return pltpu.make_async_copy(held.at[:, :, lanes], out_ref.at[:, :, lanes], sem.at[chunk])

    @pl.loop(0, width // CHUNK)
    def _(chunk):
        lanes = pl.ds(pl.multiple_of(chunk * CHUNK, CHUNK), CHUNK)
        flow_chip = (sign * (end_ref[:, lanes] - end_other[:, lanes]) + 1.0) * rcp(
            res_ref[:, lanes] + res_other[:, lanes]
        )
        flow_core = gap_ref[:, lanes] + gain_ref[:, lanes] * flow_chip
        j_in = jnp.where(depth == 0, 0.0, jnp.where(depth == 2, flow_chip, flow_core))
        j_out = jnp.where(depth == 3, 0.0, jnp.where(depth == 1, flow_chip, flow_core))
        for z in range(nz):
            held[z, :, lanes] = (
                local_ref[z, :, lanes] + top_col[z, :, lanes] * j_in - bottom_col[z, :, lanes] * j_out
            )
        out_copy(chunk).start()

    @pl.loop(0, width // CHUNK)
    def _(chunk):
        out_copy(chunk).wait()


def shift_rows(x, by):
    return pltpu.roll(x, by % x.shape[0], 0)


def shift_lanes(x, by):
    return pltpu.roll(x, by % x.shape[1], 1)


def harmonic(first, second):
    total = first + second
    return 2.0 * first * second * rcp(jnp.where(total > 0.0, total, 1.0))


def face_k(pond, ground, conv, shift):
    pond_two, ground_two, conv_two = shift(pond), shift(ground), shift(conv)
    depth_face = 0.5 * (pond + pond_two)
    slope = pond_two + ground_two - (pond + ground)
    return (
        jnp.exp2((5.0 / 3.0 * LOG2E) * jnp.log(depth_face))
        * harmonic(conv, conv_two)
        * lax.rsqrt(jnp.abs(slope) + SLOPE_FLOOR)
    )


def relay_kernel(rows_ref, from_core, _, sent_ref):
    window = sent_ref.shape[1] // 2
    depth = lax.axis_index("depth")
    is_even = lax.rem(depth, 2) == 0
    cut = pl.ds(pl.multiple_of(window_start(depth ^ 2, rows_ref.shape[1] // 4, window), LANES), window)
    own, other = rows_ref[:, cut], from_core[:, pl.ds(window, window)]
    sent_ref[:, pl.ds(0, window)] = jnp.where(is_even, own, other)
    sent_ref[:, pl.ds(window, window)] = jnp.where(is_even, other, own)


def surface_kernel(
    own_ref, exfil_ref, pair_core, pair_chip, rows_ref, from_core, from_chip, _, out_ref, last,
):
    window = last.shape[1]
    width = exfil_ref.shape[1]
    quarter = width // 4
    lat = lax.axis_index("lat")
    depth = lax.axis_index("depth")
    is_even = lax.rem(depth, 2) == 0
    upper = lax.broadcasted_iota(jnp.int32, (ROWS, window), 0) < 4
    first, second = pl.ds(0, window), pl.ds(window, window)

    cut = pl.ds(pl.multiple_of(window_start(depth, quarter, window), LANES), window)
    mine, other = rows_ref[:, cut], from_core[:, first]
    here = (jnp.where(is_even, mine, other), jnp.where(is_even, other, mine))
    there = (from_chip[:, first], from_chip[:, second])
    outer = [jnp.where(depth < 2, a, b) for a, b in zip(here + there, there + here)]
    near = jnp.where(depth == 0, exfil_ref[:, first], pair_core[:, pl.ds(3 * width, window)])
    near = jnp.where(depth < 2, near, pair_chip[:, pl.ds(width, window)])

    def extended(rows, own):
        own = pltpu.roll(own, 4, 0)
        return jnp.concatenate([jnp.where(upper, rows, own), jnp.where(upper, own, rows)], axis=0)

    exfil, pond, ground, conv = (
        extended(rows, own) for rows, own in zip(outer, (near, own_ref[0], own_ref[1], own_ref[2]))
    )
    row = lax.broadcasted_iota(jnp.int32, conv.shape, 0)
    outside = ((row < 4) & (lat == 0)) | ((row >= 12) & (lat == lax.axis_size("lat") - 1))
    conv = jnp.where(outside, 0.0, conv)
    k_down = face_k(pond, ground, conv, lambda x: shift_rows(x, -1))
    k_up = shift_rows(k_down, 1)
    k_right = face_k(pond, ground, conv, lambda x: shift_lanes(x, -1))
    lane = lax.broadcasted_iota(jnp.int32, conv.shape, 1)
    k_right = jnp.where(lane < window - 1, k_right, 0.0)
    k_left = shift_lanes(k_right, 1)
    diag = 1.0 / SURFACE_STEP + k_up + k_down + k_left + k_right
    rhs = pond * (1.0 / SURFACE_STEP)
    rhs = rhs + k_up * (shift_rows(ground, 1) - ground) + k_down * (shift_rows(ground, -1) - ground)
    rhs = rhs + k_left * (shift_lanes(ground, 1) - ground) + k_right * (shift_lanes(ground, -1) - ground)
    inv = rcp(diag)
    k_up, k_down, k_left, k_right = k_up * inv, k_down * inv, k_left * inv, k_right * inv
    rhs = (rhs + exfil) * inv
    level = pond
    for _ in range(SWEEPS):
        level = (
            rhs
            + k_up * shift_rows(level, 1)
            + k_down * shift_rows(level, -1)
            + k_left * shift_lanes(level, 1)
            + k_right * shift_lanes(level, -1)
        )
    last[...] = level
    start = pl.multiple_of(
        depth * quarter - window_start(depth, quarter, window), LANES
    )
    cut = pl.ds(start, quarter)
    lower_half = lax.broadcasted_iota(jnp.int32, (ROWS, quarter), 0) >= 4
    upper = pltpu.roll(last[pl.ds(0, ROWS), cut], 4, 0)
    lower = pltpu.roll(last[pl.ds(ROWS, ROWS), cut], 4, 0)
    out_ref[...] = jnp.where(lower_half, lower, upper)


def per_device(
    head, head_old, soil, cond_table, shape_table, pore_table, pond, ground, ponded, river
):
    nz, rows, width = head.shape
    window = width // 4 + 2 * LANES
    lat_count = lax.axis_size("lat")
    up, down = [], []
    for i in range(lat_count):
        for j in range(4):
            after, place = (i + 1, j) if i < lat_count - 1 else (0, j ^ 2)
            up.append((4 * i + j, 4 * after + place))
            down.append((4 * after + place, 4 * i + j))
    core = [(0, 1), (1, 0), (2, 3), (3, 2)]
    chip = [(0, 2), (2, 0), (1, 3), (3, 1)]
    block = f32(nz, rows, width)
    padded = f32(nz, rows, width + LANES)
    plane = f32(rows, width)

    side = f32(rows, 2 * (nz // ROWS) * width + width // 2)

    own_up, own_down, tables, exfil, own_fields = call(
        pack_kernel,
        "pack",
        [in_hbm(x) for x in (cond_table, shape_table, pore_table, head, soil, pond, ground, ponded, river)],
        [side, side, f32(6, ROWS, LANES), plane, f32(3, rows, window)],
        scratch=[
            pltpu.SMEM((3, cond_table.shape[0]), jnp.float32),
            pltpu.VMEM((2, nz // ROWS, ROWS, width), jnp.int32),
            pltpu.VMEM((rows, width), jnp.float32),
            pltpu.VMEM((rows, width), jnp.int32),
            pltpu.VMEM((rows, width), jnp.float32),
            pltpu.VMEM((rows, width), jnp.float32),
            pltpu.VMEM((rows, width), jnp.int32),
            pltpu.VMEM((rows, width), jnp.int32),
            pltpu.SemaphoreType.DMA((9 + 4 * (nz // ROWS),)),
        ],
    )
    from_above = lax.ppermute(own_up, ("lat", "depth"), up)
    from_below = lax.ppermute(own_down, ("lat", "depth"), down)

    head_v, sigma, base, ratio, inv, top_col, bottom_col, resist = call(
        factor_kernel,
        "factor",
        [in_vmem(tables), in_vmem(exfil)] + [in_hbm(x) for x in (head, head_old, soil)],
        [padded, padded] + [block] * 5 + [f32(rows, 3 * width + 2 * window)],
        scratch=[
            pltpu.VMEM((nz, rows, width), jnp.float32),
            pltpu.VMEM((nz, rows, width), jnp.int32),
            pltpu.SemaphoreType.DMA((3, width // CHUNK)),
        ],
    )
    resist_other = lax.ppermute(resist, "depth", core)
    base, sums = call(
        lateral_kernel,
        "lateral",
        [in_vmem(x) for x in (head_v, sigma, base, top_col, bottom_col)],
        [block, f32(2 * rows, width)],
        scratch=[pltpu.VMEM((3, nz, rows, LANES), jnp.float32)],
    )
    pair_inv, gain, chip_sent = call(
        pair_kernel,
        "pair",
        [in_vmem(x) for x in (resist, resist_other, exfil, sums)],
        [plane, plane, f32(rows, width + window)],
    )
    chip_other = lax.ppermute(chip_sent, "depth", chip)

    flux, ends, field_rows, windows = call(
        halo_kernel,
        "halo",
        [in_vmem(x) for x in (own_up, own_down, from_above, from_below, top_col, bottom_col, sums, gain)],
        [f32(2, nz, width), f32(2 * rows, width), plane, f32(rows, 2 * window)],
    )
    ends_other = lax.ppermute(ends, "depth", core)
    windows_core = lax.ppermute(windows, "depth", core)
    local = call(
        local_kernel, "local", [in_vmem(x) for x in (flux, base, ratio, inv, head_v)], [block]
    )[0]
    gap, chip_end = call(
        ends_kernel, "ends", [in_vmem(x) for x in (ends, ends_other, pair_inv, gain)], [plane, plane]
    )
    chip_end_other = lax.ppermute(chip_end, "depth", chip)
    relayed = call(
        relay_kernel,
        "relay",
        [in_vmem(x) for x in (field_rows, windows_core, chip_end)],
        [f32(rows, 2 * window)],
    )[0]
    windows_chip = lax.ppermute(relayed, "depth", chip)
    head_new, token = call(
        final_kernel,
        "final",
        [
            in_vmem(x)
            for x in (local, top_col, bottom_col, gap, gain, chip_sent, chip_other, chip_end, chip_end_other)
        ],
        [jax.ShapeDtypeStruct((nz, rows, width), jnp.float32), f32(ROWS, LANES)],
        out_specs=[ANY, VMEM],
        scratch=[pltpu.VMEM((nz, rows, width), jnp.float32), pltpu.SemaphoreType.DMA((width // CHUNK,))],
    )
    surface_new = call(
        surface_kernel,
        "surface",
        [
            in_vmem(x)
            for x in (own_fields, exfil, resist_other, chip_other, field_rows, windows_core, windows_chip, token)
        ],
        [jax.ShapeDtypeStruct((rows, width // 4), jnp.float32)],
        scratch=[pltpu.VMEM((2 * rows, window), jnp.float32)],
    )[0]
    return (head_new, surface_new)


def solution(mesh):
    placed = (
        P("depth", "lat", None),
        P("depth", "lat", None),
        P("depth", "lat", None),
        P(),
        P(),
        P(),
        P("lat", None),
        P("lat", None),
        P("lat", None),
        P("lat", None),
    )
    return jax.shard_map(
        per_device,
        mesh=mesh,
        in_specs=placed,
        out_specs=(P("depth", "lat", None), P("lat", "depth")),
        check_vma=False,
    )
```

```python
import jax
import jax.numpy as jnp
from jax import lax
from jax.experimental import pallas as pl
from jax.experimental.pallas import tpu as pltpu
from jax.sharding import PartitionSpec as P

SWEEPS = 4

TIME_STEP = 20.0
SURFACE_STEP = 2.0
SPECIFIC_STORAGE = 0.01
LAND_CONVEYANCE = 3.0
RIVER_CONVEYANCE = 10.0
SLOPE_FLOOR = 0.01

LOG2E = 1.4426950408889634
LN2 = 0.6931471805599453
CLOSED = 1e37

LANES = 128
ROWS = 8
CHUNK = 512
AHEAD = 3
VMEM_LIMIT = 8 * 1024 * 1024

VMEM = pl.BlockSpec(memory_space=pltpu.VMEM)
ANY = pl.BlockSpec(memory_space=pl.ANY)


def f32(*shape):
    return pltpu.VMEM(shape, jnp.float32)


def in_vmem(x):
    return (VMEM, pltpu.with_memory_space_constraint(x, pltpu.VMEM))


def in_hbm(x):
    return (ANY, pltpu.with_memory_space_constraint(x, pltpu.HBM))


FLOPS = {}


def call(kernel, name, args, out_shape, out_specs=None, scratch=()):
    return pl.pallas_call(
        kernel,
        out_shape=out_shape,
        in_specs=[spec for spec, _ in args],
        out_specs=out_specs or [VMEM] * len(out_shape),
        scratch_shapes=list(scratch),
        compiler_params=pltpu.CompilerParams(vmem_limit_bytes=VMEM_LIMIT),
        cost_estimate=pl.CostEstimate(flops=FLOPS.get(name, 1), bytes_accessed=1, transcendentals=0),
        name=name,
    )(*(x for _, x in args))


def rcp(x):
    return pl.reciprocal(x, approx=True)


def lookup(table, soil):
    numbers = lax.GatherDimensionNumbers(
        offset_dims=(),
        collapsed_slice_dims=(0,),
        start_index_map=(0,),
        operand_batching_dims=(1,),
        start_indices_batching_dims=(1,),
    )
    low, high = table
    blocks = []
    for top in range(0, soil.shape[0], ROWS):
        parts = []
        for start in range(0, soil.shape[1], LANES):
            kind = soil[top : top + ROWS, start : start + LANES]
            index = (kind & (ROWS - 1))[..., None]
            found = [
                lax.gather(half, index, numbers, (1, 1), mode=lax.GatherScatterMode.PROMISE_IN_BOUNDS)
                for half in table
            ]
            parts.append(jnp.where(kind < ROWS, *found))
        blocks.append(jnp.concatenate(parts, axis=1) if len(parts) > 1 else parts[0])
    return jnp.concatenate(blocks, axis=0) if len(blocks) > 1 else blocks[0]


def window_start(quarter, width, window):
    return jnp.clip(quarter * width - LANES, 0, 4 * width - window)


def static_window(quarter, width, window):
    return pl.ds(min(max(quarter * width - LANES, 0), 4 * width - window), window)


def pack_kernel(
    cond_ref, shape_ref, pore_ref, head_ref, soil_ref, pond_ref, ground_ref, ponded_ref, river_ref,
    up_ref, down_ref, table_ref, exfil_ref, own_ref,
    small, soils, head_top, soil_top, pond, ground, ponded, river, sem,
):
    nz, _, width = head_ref.shape
    groups = nz // ROWS
    quarter = width // 4
    window = quarter + 2 * LANES
    half = width // 2
    depth = lax.axis_index("depth")
    sides = (up_ref, down_ref)
    pairs = [
        (cond_ref, small.at[0]),
        (shape_ref, small.at[1]),
        (pore_ref, small.at[2]),
        (head_ref.at[0], head_top),
        (soil_ref.at[0], soil_top),
        (pond_ref, pond),
        (ponded_ref, ponded),
        (ground_ref, ground),
        (river_ref, river),
    ]
    fields = len(pairs)
    for group in range(groups):
        layers = pl.ds(group * ROWS, ROWS)
        for side, (target, row) in enumerate(zip(sides, (ROWS - 1, 0))):
            pairs.append((soil_ref.at[layers, row, :], soils.at[side, group]))
            pairs.append((head_ref.at[layers, row, :], target.at[:, pl.ds(group * width, width)]))
    copies = [pltpu.make_async_copy(source, target, sem.at[i]) for i, (source, target) in enumerate(pairs)]
    for copy in copies:
        copy.start()

    for copy in copies[:3]:
        copy.wait()
    row = lax.broadcasted_iota(jnp.int32, (ROWS, LANES), 0)
    registers = []
    for place in range(3):
        halves = []
        for top in (0, ROWS):
            value = jnp.ones((ROWS, LANES), jnp.float32)
            for soil_kind in range(top, min(top + ROWS, cond_ref.shape[0])):
                value = jnp.where(row == soil_kind - top, small[place, soil_kind], value)
            halves.append(value)
        registers.append(halves)
    cond_table, shape_table, pore_table = registers
    half_res = [0.5 / value for value in cond_table]
    steep = [value * LOG2E for value in shape_table]
    pore_table = [value * (1.0 / TIME_STEP) for value in pore_table]
    for place, halves in enumerate((half_res, steep, pore_table)):
        table_ref[2 * place] = halves[0]
        table_ref[2 * place + 1] = halves[1]

    for copy in copies[3:fields]:
        copy.wait()
    wet_pond = ponded[...].astype(jnp.float32) * pond[...]
    conductivity = lookup(cond_table, soil_top[...]) * jnp.exp2(
        lookup(steep, soil_top[...]) * jnp.minimum(head_top[...], 0.0)
    )
    exfil = -conductivity * (2.0 * (wet_pond - head_top[...]) + 1.0)
    exfil_ref[...] = exfil
    conv = LAND_CONVEYANCE + (RIVER_CONVEYANCE - LAND_CONVEYANCE) * river[...].astype(jnp.float32)
    field = jnp.where(
        depth < 2, jnp.where(depth == 0, exfil, pond[...]), jnp.where(depth == 2, ground[...], conv)
    )
    upper = lax.broadcasted_iota(jnp.int32, (ROWS, half), 0) < 4
    into = pl.ds(2 * groups * width, half)
    left, right = field[:, :half], field[:, half:]
    up_ref[:, into] = jnp.where(upper, pltpu.roll(left, 4, 0), right)
    down_ref[:, into] = jnp.where(upper, left, pltpu.roll(right, 4, 0))
    cut = pl.ds(pl.multiple_of(window_start(depth, quarter, window), LANES), window)
    own_ref[0] = pond[:, cut]
    own_ref[1] = ground[:, cut]
    own_ref[2] = LAND_CONVEYANCE + (RIVER_CONVEYANCE - LAND_CONVEYANCE) * river[:, cut].astype(jnp.float32)

    following = iter(copies[fields:])
    for group in range(groups):
        for side, target in enumerate(sides):
            next(following).wait()
            next(following).wait()
            head = target[:, pl.ds(group * width, width)]
            soil = soils[side, group]
            target[:, pl.ds((groups + group) * width, width)] = lookup(half_res, soil) * jnp.exp2(
                -lookup(steep, soil) * jnp.minimum(head, 0.0)
            )


def factor_kernel(
    table_ref, exfil_ref, head_hbm, old_hbm, soil_hbm,
    head_ref, sigma, base, ratio, inv, top_col, bottom_col, resist_ref, old_ref, soil_ref, sem,
):
    nz, _, width = base.shape
    depth = lax.axis_index("depth")
    is_top = jnp.where(depth == 0, 1.0, 0.0)
    is_bottom = jnp.where(depth == 3, 1.0, 0.0)
    is_even = lax.rem(depth, 2) == 0
    chunks = width // CHUNK

    def fetch(chunk):
        lanes = pl.ds(pl.multiple_of(chunk * CHUNK, CHUNK), CHUNK)
        return [
            pltpu.make_async_copy(source.at[:, :, lanes], target.at[:, :, lanes], sem.at[i, chunk])
            for i, (source, target) in enumerate(((head_hbm, head_ref), (soil_hbm, soil_ref), (old_hbm, old_ref)))
        ]

    for chunk in range(AHEAD):
        for copy in fetch(chunk):
            copy.start()
    half_res, steep, porosity = ((table_ref[2 * place], table_ref[2 * place + 1]) for place in range(3))
    sigma[:, :, pl.ds(width, LANES)] = jnp.full((nz, ROWS, LANES), CLOSED, jnp.float32)
    head_ref[:, :, pl.ds(width, LANES)] = jnp.zeros((nz, ROWS, LANES), jnp.float32)

    @pl.loop(0, chunks)
    def _(chunk):
        lanes = pl.ds(pl.multiple_of(chunk * CHUNK, CHUNK), CHUNK)
        for copy in fetch(chunk):
            copy.wait()

        @pl.when(chunk + AHEAD < chunks)
        def _():
            for copy in fetch(chunk + AHEAD):
                copy.start()

        def state(z):
            head = head_ref[z, :, lanes]
            old = old_ref[z, :, lanes]
            soil = soil_ref[z, :, lanes]
            alpha = lookup(steep, soil)
            power = alpha * jnp.minimum(head, 0.0)
            wet = jnp.exp2(power)
            wet_old = jnp.exp2(alpha * jnp.minimum(old, 0.0))
            res = lookup(half_res, soil) * rcp(wet)
            sigma[z, :, lanes] = res
            pore = lookup(porosity, soil)
            pore_wet = pore * wet
            storage = pore * wet_old - pore_wet + (SPECIFIC_STORAGE / TIME_STEP) * (old - head)
            capacity = SPECIFIC_STORAGE / TIME_STEP + (alpha * LN2) * pore_wet
            return head, res, storage, capacity

        now = state(0)
        sigma_top = now[1]
        face_above = flux_above = ratio_above = column = None
        for z in range(nz):
            head, res, b, d = now
            if z == 0:
                b = b - exfil_ref[:, lanes] * is_top
                d = d + rcp(res) * is_top
            else:
                b = b + flux_above
                d = d + face_above * (1.0 - ratio_above)
            if z == nz - 1:
                b = b - 0.5 * rcp(res) * is_bottom
            else:
                after = state(z + 1)
                face = rcp(res + after[1])
                flux = face * (head - after[0] + 1.0)
                b = b - flux
                d = d + face
            pivot_inv = rcp(d)
            base[z, :, lanes] = b
            inv[z, :, lanes] = pivot_inv
            column = pivot_inv if z == 0 else column * pivot_inv
            if z < nz - 1:
                ratio_above = face * pivot_inv
                ratio[z, :, lanes] = ratio_above
                top_col[z, :, lanes] = column
                column = column * face
                face_above, flux_above = face, flux
                now = after
        first, last = column, pivot_inv
        top_col[nz - 1, :, lanes] = first
        bottom_col[nz - 1, :, lanes] = last
        corner = first
        r_bottom = res + last
        for z in reversed(range(nz - 1)):
            m = ratio[z, :, lanes]
            first = top_col[z, :, lanes] + m * first
            last = m * last
            top_col[z, :, lanes] = first
            bottom_col[z, :, lanes] = last
        r_top = sigma_top + first
        resist_ref[:, lanes] = jnp.where(is_even, r_bottom, r_top)
        resist_ref[:, pl.ds(pl.multiple_of(width + chunk * CHUNK, CHUNK), CHUNK)] = jnp.where(is_even, r_top, r_bottom)
        resist_ref[:, pl.ds(pl.multiple_of(2 * width + chunk * CHUNK, CHUNK), CHUNK)] = corner


def lateral_kernel(
    head_ref, sigma, base_in, top_col, bottom_col, base, sums_ref, carried,
):
    nz, _, width = base.shape
    sublane = lax.broadcasted_iota(jnp.int32, (ROWS, CHUNK), 0)
    inner = sublane < ROWS - 1
    lane = lax.broadcasted_iota(jnp.int32, (ROWS, LANES), 1)
    is_first, is_last = lane == 0, lane == LANES - 1
    count = CHUNK // LANES

    def left(x):
        return pltpu.roll(x, LANES - 1, 1)

    def registers(x):
        return [x[:, k * LANES : (k + 1) * LANES] for k in range(x.shape[1] // LANES)]

    for z in range(nz):
        carried[0, z] = left(sigma[z, :, pl.ds(0, LANES)])
        carried[1, z] = left(head_ref[z, :, pl.ds(0, LANES)])
        carried[2, z] = jnp.zeros((ROWS, LANES), jnp.float32)

    @pl.loop(0, width // CHUNK)
    def _(chunk):
        start = pl.multiple_of(chunk * CHUNK, CHUNK)
        lanes = pl.ds(start, CHUNK)
        after = pl.ds(pl.multiple_of(start + LANES, LANES), CHUNK)
        top_sum = bottom_sum = None
        for z in range(nz):
            s, h = sigma[z, :, lanes], head_ref[z, :, lanes]
            moved = []
            for place, array in ((0, sigma), (1, head_ref)):
                found = [carried[place, z]] + [left(x) for x in registers(array[z, :, after])]
                carried[place, z] = found[count]
                moved.append(
                    jnp.concatenate(
                        [jnp.where(is_last, found[k + 1], found[k]) for k in range(count)], axis=1
                    )
                )
            s_right, h_right = moved
            flux_y = rcp(s + s_right) * (h_right - h)
            found = [carried[2, z]] + [pltpu.roll(x, 1, 1) for x in registers(flux_y)]
            carried[2, z] = found[count]
            flux_left = jnp.concatenate(
                [jnp.where(is_first, found[k], found[k + 1]) for k in range(count)], axis=1
            )
            flux_x = rcp(s + pltpu.roll(s, ROWS - 1, 0)) * (pltpu.roll(h, ROWS - 1, 0) - h)
            flux_x = jnp.where(inner, flux_x, 0.0)
            b = base_in[z, :, lanes] + (flux_y - flux_left) + (flux_x - pltpu.roll(flux_x, 1, 0))
            base[z, :, lanes] = b
            first = top_col[z, :, lanes] * b
            last = bottom_col[z, :, lanes] * b
            top_sum = first if z == 0 else top_sum + first
            bottom_sum = last if z == 0 else bottom_sum + last
        sums_ref[pl.ds(0, ROWS), lanes] = top_sum + head_ref[0, :, lanes]
        sums_ref[pl.ds(ROWS, ROWS), lanes] = bottom_sum + head_ref[nz - 1, :, lanes]


def pair_kernel(mine, other, exfil_ref, _, pair_inv_ref, gain_ref, sent_ref):
    width = gain_ref.shape[1]
    window = (sent_ref.shape[1] - width) // 2
    depth = lax.axis_index("depth")
    inner = (depth == 1) | (depth == 2)
    near, far, corner = (pl.ds(place * width, width) for place in range(3))
    pair_inv = rcp(mine[:, near] + other[:, near])
    inner_corner = jnp.where(inner, mine[:, corner], other[:, corner])
    gain = inner_corner * pair_inv
    pair_inv_ref[...] = pair_inv
    gain_ref[...] = gain
    sent_ref[:, pl.ds(0, width)] = jnp.where(inner, mine[:, far], other[:, far]) - inner_corner * gain
    for place, quarters in enumerate((depth ^ 2, depth ^ 3)):
        cut = pl.ds(pl.multiple_of(window_start(quarters, width // 4, window), LANES), window)
        sent_ref[:, pl.ds(width + place * window, window)] = exfil_ref[:, cut]


def halo_kernel(
    own_up, own_down, from_above, from_below, top_col, bottom_col, sums_ref, _, flux_ref, near_ref, far_ref, rows_ref, windows_ref,
):
    nz, _, width = top_col.shape
    lat = lax.axis_index("lat")
    has_above = jnp.where(lat == 0, 0.0, 1.0)
    has_below = jnp.where(lat == lax.axis_size("lat") - 1, 0.0, 1.0)
    is_even = lax.rem(lax.axis_index("depth"), 2) == 0
    sublane = lax.broadcasted_iota(jnp.int32, (ROWS, CHUNK), 0)
    for side, other, own, scale in ((0, from_below, own_up, has_below), (1, from_above, own_down, has_above)):
        for group in range(nz // ROWS):
            heads = pl.ds(group * width, width)
            sigmas = pl.ds((nz // ROWS + group) * width, width)
            flux_ref[side, pl.ds(group * ROWS, ROWS), :] = rcp(other[:, sigmas] + own[:, sigmas]) * (
                (other[:, heads] - own[:, heads]) * scale
            )

    @pl.loop(0, width // CHUNK)
    def _(chunk):
        lanes = pl.ds(pl.multiple_of(chunk * CHUNK, CHUNK), CHUNK)
        top_sum = sums_ref[pl.ds(0, ROWS), lanes]
        bottom_sum = sums_ref[pl.ds(ROWS, ROWS), lanes]
        for z in range(nz):
            row = pl.ds(z, 1)
            added = jnp.where(sublane == 0, flux_ref[1, row, lanes], 0.0)
            added = jnp.where(sublane == ROWS - 1, flux_ref[0, row, lanes], added)
            top_sum = top_sum + top_col[z, :, lanes] * added
            bottom_sum = bottom_sum + bottom_col[z, :, lanes] * added
        near_ref[:, lanes] = jnp.where(is_even, bottom_sum, top_sum)
        far_ref[:, lanes] = jnp.where(is_even, top_sum, bottom_sum)

    half = width // 2
    extra = pl.ds(own_up.shape[1] - half, half)
    upper = lax.broadcasted_iota(jnp.int32, (ROWS, half), 0) < 4
    above, below = from_above[:, extra], from_below[:, extra]
    rows_ref[:, pl.ds(0, half)] = jnp.where(upper, above, pltpu.roll(below, 4, 0))
    rows_ref[:, pl.ds(half, half)] = jnp.where(upper, pltpu.roll(above, 4, 0), below)
    quarter = width // 4
    window = windows_ref.shape[1] // 2
    depth = lax.axis_index("depth")
    for place, quarters in enumerate((depth ^ 2, depth ^ 3)):
        cut = pl.ds(pl.multiple_of(window_start(quarters, quarter, window), LANES), window)
        windows_ref[:, pl.ds(place * window, window)] = rows_ref[:, cut]


def local_kernel(flux_ref, base, ratio, inv, head_ref, out_ref):
    nz, _, width = base.shape
    sublane = lax.broadcasted_iota(jnp.int32, (ROWS, CHUNK), 0)

    @pl.loop(0, width // CHUNK)
    def _(chunk):
        lanes = pl.ds(pl.multiple_of(chunk * CHUNK, CHUNK), CHUNK)
        y = None
        for z in range(nz):
            row = pl.ds(z, 1)
            added = jnp.where(sublane == 0, flux_ref[1, row, lanes], 0.0)
            added = jnp.where(sublane == ROWS - 1, flux_ref[0, row, lanes], added)
            rhs = base[z, :, lanes] + added
            y = rhs if z == 0 else rhs + ratio[z - 1, :, lanes] * y
            if z < nz - 1:
                out_ref[z, :, lanes] = y
        x = y * inv[nz - 1, :, lanes]
        out_ref[nz - 1, :, lanes] = x + head_ref[nz - 1, :, lanes]
        for z in reversed(range(nz - 1)):
            x = out_ref[z, :, lanes] * inv[z, :, lanes] + ratio[z, :, lanes] * x
            out_ref[z, :, lanes] = x + head_ref[z, :, lanes]


def ends_kernel(mine, other, far_mine, far_other, pair_inv_ref, gain_ref, gap_ref, chip_end_ref):
    depth = lax.axis_index("depth")
    inner = (depth == 1) | (depth == 2)
    sign = jnp.where(depth < 2, 1.0, -1.0)
    own, others = mine[...], other[...]
    gap = sign * jnp.where(inner, others - own, own - others) + 1.0
    gap_ref[...] = gap * pair_inv_ref[...]
    chip_end_ref[...] = jnp.where(inner, far_mine[...], far_other[...]) + sign * gain_ref[...] * gap


def final_kernel(
    local_ref, top_col, bottom_col, gap_ref, gain_ref, res_ref, res_other, end_ref, end_other,
    own_ref, exfil_ref, rows_ref, from_chip, from_core,
    out_ref, surface_ref, held, last, sem,
):
    nz, _, width = local_ref.shape
    depth = lax.axis_index("depth")
    sign = jnp.where(depth < 2, 1.0, -1.0)

    def out_copy(chunk):
        lanes = pl.ds(pl.multiple_of(chunk * CHUNK, CHUNK), CHUNK)
        return pltpu.make_async_copy(held.at[:, :, lanes], out_ref.at[:, :, lanes], sem.at[chunk])

    @pl.loop(0, width // CHUNK)
    def _(chunk):
        lanes = pl.ds(pl.multiple_of(chunk * CHUNK, CHUNK), CHUNK)
        flow_chip = (sign * (end_ref[:, lanes] - end_other[:, lanes]) + 1.0) * rcp(
            res_ref[:, lanes] + res_other[:, lanes]
        )
        flow_core = gap_ref[:, lanes] + gain_ref[:, lanes] * flow_chip
        j_in = jnp.where(depth == 0, 0.0, jnp.where(depth == 2, flow_chip, flow_core))
        j_out = jnp.where(depth == 3, 0.0, jnp.where(depth == 1, flow_chip, flow_core))
        for z in range(nz):
            held[z, :, lanes] = (
                local_ref[z, :, lanes] + top_col[z, :, lanes] * j_in - bottom_col[z, :, lanes] * j_out
            )
        out_copy(chunk).start()

    surface(own_ref, exfil_ref, rows_ref, from_chip, from_core, res_other, surface_ref, last)

    @pl.loop(0, width // CHUNK)
    def _(chunk):
        out_copy(chunk).wait()


def shift_rows(x, by):
    return pltpu.roll(x, by % x.shape[0], 0)


def shift_lanes(x, by):
    return pltpu.roll(x, by % x.shape[1], 1)


def harmonic(first, second):
    total = first + second
    return 2.0 * first * second * rcp(jnp.where(total > 0.0, total, 1.0))


def face_k(pond, ground, conv, shift):
    pond_two, ground_two, conv_two = shift(pond), shift(ground), shift(conv)
    depth_face = 0.5 * (pond + pond_two)
    slope = pond_two + ground_two - (pond + ground)
    return (
        jnp.exp2((5.0 / 3.0 * LOG2E) * jnp.log(depth_face))
        * harmonic(conv, conv_two)
        * lax.rsqrt(jnp.abs(slope) + SLOPE_FLOOR)
    )


def relay_kernel(rows_ref, exfil_ref, from_chip, chip_other, _, __, sent_ref):
    window = sent_ref.shape[1] // 3
    depth = lax.axis_index("depth")
    is_low = depth < 2
    cut = pl.ds(pl.multiple_of(window_start(depth ^ 1, rows_ref.shape[1] // 4, window), LANES), window)
    first, second, third = (pl.ds(place * window, window) for place in range(3))
    own, other = rows_ref[:, cut], from_chip[:, second]
    sent_ref[:, first] = jnp.where(is_low, own, other)
    sent_ref[:, second] = jnp.where(is_low, other, own)
    sent_ref[:, third] = jnp.where(
        is_low, exfil_ref[:, cut], chip_other[:, pl.ds(chip_other.shape[1] - window, window)]
    )


def surface(own_ref, exfil_ref, rows_ref, from_chip, from_core, chip_other, out_ref, last):
    window = last.shape[1]
    width = exfil_ref.shape[1]
    quarter = width // 4
    lat = lax.axis_index("lat")
    depth = lax.axis_index("depth")
    is_even = lax.rem(depth, 2) == 0
    upper = lax.broadcasted_iota(jnp.int32, (ROWS, window), 0) < 4
    first, second, third = (pl.ds(place * window, window) for place in range(3))

    cut = pl.ds(pl.multiple_of(window_start(depth, quarter, window), LANES), window)
    mine, other = rows_ref[:, cut], from_chip[:, first]
    here = (jnp.where(depth < 2, mine, other), jnp.where(depth < 2, other, mine))
    there = (from_core[:, first], from_core[:, second])
    outer = [jnp.where(is_even, a, b) for low, high in zip(here, there) for a, b in ((low, high), (high, low))]
    near = jnp.where(depth == 0, exfil_ref[:, first], chip_other[:, pl.ds(width, window)])
    near = jnp.where(is_even, near, from_core[:, third])

    def extended(rows, own):
        own = pltpu.roll(own, 4, 0)
        return jnp.concatenate([jnp.where(upper, rows, own), jnp.where(upper, own, rows)], axis=0)

    exfil, pond, ground, conv = (
        extended(rows, own) for rows, own in zip(outer, (near, own_ref[0], own_ref[1], own_ref[2]))
    )
    row = lax.broadcasted_iota(jnp.int32, conv.shape, 0)
    outside = ((row < 4) & (lat == 0)) | ((row >= 12) & (lat == lax.axis_size("lat") - 1))
    conv = jnp.where(outside, 0.0, conv)
    k_down = face_k(pond, ground, conv, lambda x: shift_rows(x, -1))
    k_up = shift_rows(k_down, 1)
    k_right = face_k(pond, ground, conv, lambda x: shift_lanes(x, -1))
    lane = lax.broadcasted_iota(jnp.int32, conv.shape, 1)
    k_right = jnp.where(lane < window - 1, k_right, 0.0)
    k_left = shift_lanes(k_right, 1)
    diag = 1.0 / SURFACE_STEP + k_up + k_down + k_left + k_right
    rhs = pond * (1.0 / SURFACE_STEP)
    rhs = rhs + k_up * (shift_rows(ground, 1) - ground) + k_down * (shift_rows(ground, -1) - ground)
    rhs = rhs + k_left * (shift_lanes(ground, 1) - ground) + k_right * (shift_lanes(ground, -1) - ground)
    inv = rcp(diag)
    k_up, k_down, k_left, k_right = k_up * inv, k_down * inv, k_left * inv, k_right * inv
    rhs = (rhs + exfil) * inv
    level = pond
    for _ in range(SWEEPS):
        level = (
            rhs
            + k_up * shift_rows(level, 1)
            + k_down * shift_rows(level, -1)
            + k_left * shift_lanes(level, 1)
            + k_right * shift_lanes(level, -1)
        )
    last[...] = level
    start = pl.multiple_of(
        depth * quarter - window_start(depth, quarter, window), LANES
    )
    cut = pl.ds(start, quarter)
    lower_half = lax.broadcasted_iota(jnp.int32, (ROWS, quarter), 0) >= 4
    upper = pltpu.roll(last[pl.ds(0, ROWS), cut], 4, 0)
    lower = pltpu.roll(last[pl.ds(ROWS, ROWS), cut], 4, 0)
    out_ref[...] = jnp.where(lower_half, lower, upper)


def per_device(
    head, head_old, soil, cond_table, shape_table, pore_table, pond, ground, ponded, river
):
    nz, rows, width = head.shape
    window = width // 4 + 2 * LANES
    lat_count = lax.axis_size("lat")
    up, down = [], []
    for i in range(lat_count):
        for j in range(4):
            after, place = (i + 1, j) if i < lat_count - 1 else (0, j ^ 2)
            up.append((4 * i + j, 4 * after + place))
            down.append((4 * after + place, 4 * i + j))
    core = [(0, 1), (1, 0), (2, 3), (3, 2)]
    chip = [(0, 2), (2, 0), (1, 3), (3, 1)]
    block = f32(nz, rows, width)
    padded = f32(nz, rows, width + LANES)
    plane = f32(rows, width)

    side = f32(rows, 2 * (nz // ROWS) * width + width // 2)

    own_up, own_down, tables, exfil, own_fields = call(
        pack_kernel,
        "pack",
        [in_hbm(x) for x in (cond_table, shape_table, pore_table, head, soil, pond, ground, ponded, river)],
        [side, side, f32(6, ROWS, LANES), plane, f32(3, rows, window)],
        scratch=[
            pltpu.SMEM((3, cond_table.shape[0]), jnp.float32),
            pltpu.VMEM((2, nz // ROWS, ROWS, width), jnp.int32),
            pltpu.VMEM((rows, width), jnp.float32),
            pltpu.VMEM((rows, width), jnp.int32),
            pltpu.VMEM((rows, width), jnp.float32),
            pltpu.VMEM((rows, width), jnp.float32),
            pltpu.VMEM((rows, width), jnp.int32),
            pltpu.VMEM((rows, width), jnp.int32),
            pltpu.SemaphoreType.DMA((9 + 4 * (nz // ROWS),)),
        ],
    )
    from_above = lax.ppermute(own_up, ("lat", "depth"), up)
    from_below = lax.ppermute(own_down, ("lat", "depth"), down)

    head_v, sigma, base, ratio, inv, top_col, bottom_col, resist = call(
        factor_kernel,
        "factor",
        [in_vmem(tables), in_vmem(exfil)] + [in_hbm(x) for x in (head, head_old, soil)],
        [padded, padded] + [block] * 5 + [f32(rows, 3 * width)],
        scratch=[
            pltpu.VMEM((nz, rows, width), jnp.float32),
            pltpu.VMEM((nz, rows, width), jnp.int32),
            pltpu.SemaphoreType.DMA((3, width // CHUNK)),
        ],
    )
    resist_other = lax.ppermute(resist, "depth", core)
    base, sums = call(
        lateral_kernel,
        "lateral",
        [in_vmem(x) for x in (head_v, sigma, base, top_col, bottom_col)],
        [block, f32(2 * rows, width)],
        scratch=[pltpu.VMEM((3, nz, rows, LANES), jnp.float32)],
    )
    pair_inv, gain, chip_sent = call(
        pair_kernel,
        "pair",
        [in_vmem(x) for x in (resist, resist_other, exfil, sums)],
        [plane, plane, f32(rows, width + 2 * window)],
    )
    chip_other = lax.ppermute(chip_sent, "depth", chip)

    flux, ends, far_ends, field_rows, windows = call(
        halo_kernel,
        "halo",
        [in_vmem(x) for x in (own_up, own_down, from_above, from_below, top_col, bottom_col, sums, gain)],
        [f32(2, nz, width), plane, plane, plane, f32(rows, 2 * window)],
    )
    near_other = lax.ppermute(ends, "depth", core)
    far_other = lax.ppermute(far_ends, "depth", core)
    windows_chip = lax.ppermute(windows, "depth", chip)
    local = call(
        local_kernel, "local", [in_vmem(x) for x in (flux, base, ratio, inv, head_v)], [block]
    )[0]
    gap, chip_end = call(
        ends_kernel, "ends", [in_vmem(x) for x in (ends, near_other, far_ends, far_other, pair_inv, gain)], [plane, plane]
    )
    chip_end_other = lax.ppermute(chip_end, "depth", chip)
    relayed = call(
        relay_kernel,
        "relay",
        [in_vmem(x) for x in (field_rows, exfil, windows_chip, chip_other, chip_end, local)],
        [f32(rows, 3 * window)],
    )[0]
    windows_core = lax.ppermute(relayed, "depth", core)
    head_new, surface_new = call(
        final_kernel,
        "final",
        [
            in_vmem(x)
            for x in (
                local, top_col, bottom_col, gap, gain, chip_sent, chip_other, chip_end, chip_end_other,
                own_fields, exfil, field_rows, windows_chip, windows_core,
            )
        ],
        [
            jax.ShapeDtypeStruct((nz, rows, width), jnp.float32),
            jax.ShapeDtypeStruct((rows, width // 4), jnp.float32),
        ],
        out_specs=[ANY, VMEM],
        scratch=[
            pltpu.VMEM((nz, rows, width), jnp.float32),
            pltpu.VMEM((2 * rows, window), jnp.float32),
            pltpu.SemaphoreType.DMA((width // CHUNK,)),
        ],
    )
    return (head_new, surface_new)


def solution(mesh):
    placed = (
        P("depth", "lat", None),
        P("depth", "lat", None),
        P("depth", "lat", None),
        P(),
        P(),
        P(),
        P("lat", None),
        P("lat", None),
        P("lat", None),
        P("lat", None),
    )
    return jax.shard_map(
        per_device,
        mesh=mesh,
        in_specs=placed,
        out_specs=(P("depth", "lat", None), P("lat", "depth")),
        check_vma=False,
    )
```

```python
import jax
import jax.numpy as jnp
from jax import lax
from jax.experimental import pallas as pl
from jax.experimental.pallas import tpu as pltpu
from jax.sharding import PartitionSpec as P

SWEEPS = 4

TIME_STEP = 20.0
SURFACE_STEP = 2.0
SPECIFIC_STORAGE = 0.01
LAND_CONVEYANCE = 3.0
RIVER_CONVEYANCE = 10.0
SLOPE_FLOOR = 0.01

LOG2E = 1.4426950408889634
LN2 = 0.6931471805599453
CLOSED = 1e37

LANES = 128
ROWS = 8
CHUNK = 512
HALO_CHUNK = 1024
AHEAD = 3
VMEM_LIMIT = 8 * 1024 * 1024

VMEM = pl.BlockSpec(memory_space=pltpu.VMEM)
ANY = pl.BlockSpec(memory_space=pl.ANY)


def f32(*shape):
    return pltpu.VMEM(shape, jnp.float32)


def in_vmem(x):
    return (VMEM, pltpu.with_memory_space_constraint(x, pltpu.VMEM))


def in_hbm(x):
    return (ANY, pltpu.with_memory_space_constraint(x, pltpu.HBM))


FLOPS = {}


def call(kernel, name, args, out_shape, out_specs=None, scratch=()):
    return pl.pallas_call(
        kernel,
        out_shape=out_shape,
        in_specs=[spec for spec, _ in args],
        out_specs=out_specs or [VMEM] * len(out_shape),
        scratch_shapes=list(scratch),
        compiler_params=pltpu.CompilerParams(vmem_limit_bytes=VMEM_LIMIT),
        cost_estimate=pl.CostEstimate(flops=FLOPS.get(name, 1), bytes_accessed=1, transcendentals=0),
        name=name,
    )(*(x for _, x in args))


def rcp(x):
    return pl.reciprocal(x, approx=True)


def lookup(table, soil):
    numbers = lax.GatherDimensionNumbers(
        offset_dims=(),
        collapsed_slice_dims=(0,),
        start_index_map=(0,),
        operand_batching_dims=(1,),
        start_indices_batching_dims=(1,),
    )
    low, high = table
    blocks = []
    for top in range(0, soil.shape[0], ROWS):
        parts = []
        for start in range(0, soil.shape[1], LANES):
            kind = soil[top : top + ROWS, start : start + LANES]
            index = (kind & (ROWS - 1))[..., None]
            found = [
                lax.gather(half, index, numbers, (1, 1), mode=lax.GatherScatterMode.PROMISE_IN_BOUNDS)
                for half in table
            ]
            parts.append(jnp.where(kind < ROWS, *found))
        blocks.append(jnp.concatenate(parts, axis=1) if len(parts) > 1 else parts[0])
    return jnp.concatenate(blocks, axis=0) if len(blocks) > 1 else blocks[0]


def window_start(quarter, width, window):
    return jnp.clip(quarter * width - LANES, 0, 4 * width - window)


def static_window(quarter, width, window):
    return pl.ds(min(max(quarter * width - LANES, 0), 4 * width - window), window)


def pack_kernel(
    cond_ref, shape_ref, pore_ref, head_ref, soil_ref, pond_ref, ground_ref, ponded_ref, river_ref,
    up_ref, down_ref, table_ref, exfil_ref, own_ref,
    small, soils, head_top, soil_top, pond, ground, ponded, river, sem,
):
    nz, _, width = head_ref.shape
    groups = nz // ROWS
    quarter = width // 4
    window = quarter + 2 * LANES
    half = width // 2
    depth = lax.axis_index("depth")
    sides = (up_ref, down_ref)
    pairs = [
        (cond_ref, small.at[0]),
        (shape_ref, small.at[1]),
        (pore_ref, small.at[2]),
        (head_ref.at[0], head_top),
        (soil_ref.at[0], soil_top),
        (pond_ref, pond),
        (ponded_ref, ponded),
        (ground_ref, ground),
        (river_ref, river),
    ]
    fields = len(pairs)
    for group in range(groups):
        layers = pl.ds(group * ROWS, ROWS)
        for side, (target, row) in enumerate(zip(sides, (ROWS - 1, 0))):
            pairs.append((soil_ref.at[layers, row, :], soils.at[side, group]))
            pairs.append((head_ref.at[layers, row, :], target.at[:, pl.ds(group * width, width)]))
    copies = [pltpu.make_async_copy(source, target, sem.at[i]) for i, (source, target) in enumerate(pairs)]
    for copy in copies:
        copy.start()

    for copy in copies[:3]:
        copy.wait()
    row = lax.broadcasted_iota(jnp.int32, (ROWS, LANES), 0)
    registers = []
    for place in range(3):
        halves = []
        for top in (0, ROWS):
            value = jnp.ones((ROWS, LANES), jnp.float32)
            for soil_kind in range(top, min(top + ROWS, cond_ref.shape[0])):
                value = jnp.where(row == soil_kind - top, small[place, soil_kind], value)
            halves.append(value)
        registers.append(halves)
    cond_table, shape_table, pore_table = registers
    half_res = [0.5 / value for value in cond_table]
    steep = [value * LOG2E for value in shape_table]
    pore_table = [value * (1.0 / TIME_STEP) for value in pore_table]
    for place, halves in enumerate((half_res, steep, pore_table)):
        table_ref[2 * place] = halves[0]
        table_ref[2 * place + 1] = halves[1]

    for copy in copies[3:fields]:
        copy.wait()
    wet_pond = ponded[...].astype(jnp.float32) * pond[...]
    conductivity = lookup(cond_table, soil_top[...]) * jnp.exp2(
        lookup(steep, soil_top[...]) * jnp.minimum(head_top[...], 0.0)
    )
    exfil = -conductivity * (2.0 * (wet_pond - head_top[...]) + 1.0)
    exfil_ref[...] = exfil
    conv = LAND_CONVEYANCE + (RIVER_CONVEYANCE - LAND_CONVEYANCE) * river[...].astype(jnp.float32)
    field = jnp.where(
        depth < 2, jnp.where(depth == 0, exfil, pond[...]), jnp.where(depth == 2, ground[...], conv)
    )
    upper = lax.broadcasted_iota(jnp.int32, (ROWS, half), 0) < 4
    into = pl.ds(2 * groups * width, half)
    left, right = field[:, :half], field[:, half:]
    up_ref[:, into] = jnp.where(upper, pltpu.roll(left, 4, 0), right)
    down_ref[:, into] = jnp.where(upper, left, pltpu.roll(right, 4, 0))
    cut = pl.ds(pl.multiple_of(window_start(depth, quarter, window), LANES), window)
    own_ref[0] = pond[:, cut]
    own_ref[1] = ground[:, cut]
    own_ref[2] = LAND_CONVEYANCE + (RIVER_CONVEYANCE - LAND_CONVEYANCE) * river[:, cut].astype(jnp.float32)

    following = iter(copies[fields:])
    for group in range(groups):
        for side, target in enumerate(sides):
            next(following).wait()
            next(following).wait()
            head = target[:, pl.ds(group * width, width)]
            soil = soils[side, group]
            target[:, pl.ds((groups + group) * width, width)] = lookup(half_res, soil) * jnp.exp2(
                -lookup(steep, soil) * jnp.minimum(head, 0.0)
            )


def factor_kernel(
    table_ref, exfil_ref, head_hbm, old_hbm, soil_hbm,
    head_ref, sigma, base, ratio, inv, top_col, bottom_col, resist_ref, old_ref, soil_ref, sem,
):
    nz, _, width = base.shape
    depth = lax.axis_index("depth")
    is_top = jnp.where(depth == 0, 1.0, 0.0)
    is_bottom = jnp.where(depth == 3, 1.0, 0.0)
    is_even = lax.rem(depth, 2) == 0
    chunks = width // CHUNK

    def fetch(chunk):
        lanes = pl.ds(pl.multiple_of(chunk * CHUNK, CHUNK), CHUNK)
        return [
            pltpu.make_async_copy(source.at[:, :, lanes], target.at[:, :, lanes], sem.at[i, chunk])
            for i, (source, target) in enumerate(((head_hbm, head_ref), (soil_hbm, soil_ref), (old_hbm, old_ref)))
        ]

    for chunk in range(AHEAD):
        for copy in fetch(chunk):
            copy.start()
    half_res, steep, porosity = ((table_ref[2 * place], table_ref[2 * place + 1]) for place in range(3))
    sigma[:, :, pl.ds(width, LANES)] = jnp.full((nz, ROWS, LANES), CLOSED, jnp.float32)
    head_ref[:, :, pl.ds(width, LANES)] = jnp.zeros((nz, ROWS, LANES), jnp.float32)

    @pl.loop(0, chunks)
    def _(chunk):
        lanes = pl.ds(pl.multiple_of(chunk * CHUNK, CHUNK), CHUNK)
        for copy in fetch(chunk):
            copy.wait()

        @pl.when(chunk + AHEAD < chunks)
        def _():
            for copy in fetch(chunk + AHEAD):
                copy.start()

        def state(z):
            head = head_ref[z, :, lanes]
            old = old_ref[z, :, lanes]
            soil = soil_ref[z, :, lanes]
            alpha = lookup(steep, soil)
            power = alpha * jnp.minimum(head, 0.0)
            wet = jnp.exp2(power)
            wet_old = jnp.exp2(alpha * jnp.minimum(old, 0.0))
            res = lookup(half_res, soil) * rcp(wet)
            sigma[z, :, lanes] = res
            pore = lookup(porosity, soil)
            pore_wet = pore * wet
            storage = pore * wet_old - pore_wet + (SPECIFIC_STORAGE / TIME_STEP) * (old - head)
            capacity = SPECIFIC_STORAGE / TIME_STEP + (alpha * LN2) * pore_wet
            return head, res, storage, capacity

        now = state(0)
        sigma_top = now[1]
        face_above = flux_above = ratio_above = column = None
        for z in range(nz):
            head, res, b, d = now
            if z == 0:
                b = b - exfil_ref[:, lanes] * is_top
                d = d + rcp(res) * is_top
            else:
                b = b + flux_above
                d = d + face_above * (1.0 - ratio_above)
            if z == nz - 1:
                b = b - 0.5 * rcp(res) * is_bottom
            else:
                after = state(z + 1)
                face = rcp(res + after[1])
                flux = face * (head - after[0] + 1.0)
                b = b - flux
                d = d + face
            pivot_inv = rcp(d)
            base[z, :, lanes] = b
            inv[z, :, lanes] = pivot_inv
            column = pivot_inv if z == 0 else column * pivot_inv
            if z < nz - 1:
                ratio_above = face * pivot_inv
                ratio[z, :, lanes] = ratio_above
                top_col[z, :, lanes] = column
                column = column * face
                face_above, flux_above = face, flux
                now = after
        first, last = column, pivot_inv
        top_col[nz - 1, :, lanes] = first
        bottom_col[nz - 1, :, lanes] = last
        corner = first
        r_bottom = res + last
        for z in reversed(range(nz - 1)):
            m = ratio[z, :, lanes]
            first = top_col[z, :, lanes] + m * first
            last = m * last
            top_col[z, :, lanes] = first
            bottom_col[z, :, lanes] = last
        r_top = sigma_top + first
        resist_ref[:, lanes] = jnp.where(is_even, r_bottom, r_top)
        resist_ref[:, pl.ds(pl.multiple_of(width + chunk * CHUNK, CHUNK), CHUNK)] = jnp.where(is_even, r_top, r_bottom)
        resist_ref[:, pl.ds(pl.multiple_of(2 * width + chunk * CHUNK, CHUNK), CHUNK)] = corner


def lateral_kernel(
    head_ref, sigma, base_in, top_col, bottom_col, _, base, sums_ref, rows_ref, carried, sem,
):
    nz, _, width = base.shape
    copies = [
        pltpu.make_async_copy(array.at[:, row, :], rows_ref.at[2 * place + side], sem.at[2 * place + side])
        for place, array in enumerate((top_col, bottom_col))
        for side, row in enumerate((ROWS - 1, 0))
    ]
    for copy in copies:
        copy.start()
    sublane = lax.broadcasted_iota(jnp.int32, (ROWS, CHUNK), 0)
    inner = sublane < ROWS - 1
    lane = lax.broadcasted_iota(jnp.int32, (ROWS, LANES), 1)
    is_first, is_last = lane == 0, lane == LANES - 1
    count = CHUNK // LANES

    def left(x):
        return pltpu.roll(x, LANES - 1, 1)

    def registers(x):
        return [x[:, k * LANES : (k + 1) * LANES] for k in range(x.shape[1] // LANES)]

    for z in range(nz):
        carried[0, z] = left(sigma[z, :, pl.ds(0, LANES)])
        carried[1, z] = left(head_ref[z, :, pl.ds(0, LANES)])
        carried[2, z] = jnp.zeros((ROWS, LANES), jnp.float32)

    @pl.loop(0, width // CHUNK)
    def _(chunk):
        start = pl.multiple_of(chunk * CHUNK, CHUNK)
        lanes = pl.ds(start, CHUNK)
        after = pl.ds(pl.multiple_of(start + LANES, LANES), CHUNK)
        top_sum = bottom_sum = None
        for z in range(nz):
            s, h = sigma[z, :, lanes], head_ref[z, :, lanes]
            moved = []
            for place, array in ((0, sigma), (1, head_ref)):
                found = [carried[place, z]] + [left(x) for x in registers(array[z, :, after])]
                carried[place, z] = found[count]
                moved.append(
                    jnp.concatenate(
                        [jnp.where(is_last, found[k + 1], found[k]) for k in range(count)], axis=1
                    )
                )
            s_right, h_right = moved
            flux_y = rcp(s + s_right) * (h_right - h)
            found = [carried[2, z]] + [pltpu.roll(x, 1, 1) for x in registers(flux_y)]
            carried[2, z] = found[count]
            flux_left = jnp.concatenate(
                [jnp.where(is_first, found[k], found[k + 1]) for k in range(count)], axis=1
            )
            flux_x = rcp(s + pltpu.roll(s, ROWS - 1, 0)) * (pltpu.roll(h, ROWS - 1, 0) - h)
            flux_x = jnp.where(inner, flux_x, 0.0)
            b = base_in[z, :, lanes] + (flux_y - flux_left) + (flux_x - pltpu.roll(flux_x, 1, 0))
            base[z, :, lanes] = b
            first = top_col[z, :, lanes] * b
            last = bottom_col[z, :, lanes] * b
            top_sum = first if z == 0 else top_sum + first
            bottom_sum = last if z == 0 else bottom_sum + last
        sums_ref[pl.ds(0, ROWS), lanes] = top_sum + head_ref[0, :, lanes]
        sums_ref[pl.ds(ROWS, ROWS), lanes] = bottom_sum + head_ref[nz - 1, :, lanes]

    for copy in copies:
        copy.wait()


def pair_kernel(mine, other, exfil_ref, pair_inv_ref, gain_ref, sent_ref):
    width = gain_ref.shape[1]
    window = (sent_ref.shape[1] - width) // 2
    depth = lax.axis_index("depth")
    inner = (depth == 1) | (depth == 2)
    near, far, corner = (pl.ds(place * width, width) for place in range(3))
    pair_inv = rcp(mine[:, near] + other[:, near])
    inner_corner = jnp.where(inner, mine[:, corner], other[:, corner])
    gain = inner_corner * pair_inv
    pair_inv_ref[...] = pair_inv
    gain_ref[...] = gain
    sent_ref[:, pl.ds(0, width)] = jnp.where(inner, mine[:, far], other[:, far]) - inner_corner * gain
    for place, quarters in enumerate((depth ^ 2, depth ^ 3)):
        cut = pl.ds(pl.multiple_of(window_start(quarters, width // 4, window), LANES), window)
        sent_ref[:, pl.ds(width + place * window, window)] = exfil_ref[:, cut]


def halo_kernel(
    own_up, own_down, from_above, from_below, end_rows, sums_ref, _, flux_ref, near_ref, far_ref, rows_ref, windows_ref,
):
    _, nz, width = flux_ref.shape
    lat = lax.axis_index("lat")
    has_above = jnp.where(lat == 0, 0.0, 1.0)
    has_below = jnp.where(lat == lax.axis_size("lat") - 1, 0.0, 1.0)
    is_even = lax.rem(lax.axis_index("depth"), 2) == 0
    sublane = lax.broadcasted_iota(jnp.int32, (ROWS, HALO_CHUNK), 0)

    @pl.loop(0, width // HALO_CHUNK)
    def _(chunk):
        start = pl.multiple_of(chunk * HALO_CHUNK, HALO_CHUNK)
        lanes = pl.ds(start, HALO_CHUNK)
        added = [[], []]
        for side, other, own, scale in ((0, from_below, own_up, has_below), (1, from_above, own_down, has_above)):
            totals = [None, None]
            for group in range(nz // ROWS):
                heads = pl.ds(pl.multiple_of(group * width + start, HALO_CHUNK), HALO_CHUNK)
                sigmas = pl.ds(pl.multiple_of((nz // ROWS + group) * width + start, HALO_CHUNK), HALO_CHUNK)
                layers = pl.ds(group * ROWS, ROWS)
                flux = rcp(other[:, sigmas] + own[:, sigmas]) * ((other[:, heads] - own[:, heads]) * scale)
                flux_ref[side, layers, lanes] = flux
                for end in range(2):
                    part = flux * end_rows[2 * end + side, layers, lanes]
                    totals[end] = part if group == 0 else totals[end] + part
            for end in range(2):
                total = totals[end]
                for by in (4, 2, 1):
                    total = total + pltpu.roll(total, by, 0)
                added[end].append(total)
        sums = []
        for end in range(2):
            total = jnp.where(sublane == 0, added[end][1], 0.0)
            total = jnp.where(sublane == ROWS - 1, added[end][0], total)
            sums.append(sums_ref[pl.ds(end * ROWS, ROWS), lanes] + total)
        near_ref[:, lanes] = jnp.where(is_even, sums[1], sums[0])
        far_ref[:, lanes] = jnp.where(is_even, sums[0], sums[1])

    half = width // 2
    extra = pl.ds(own_up.shape[1] - half, half)
    upper = lax.broadcasted_iota(jnp.int32, (ROWS, half), 0) < 4
    above, below = from_above[:, extra], from_below[:, extra]
    rows_ref[:, pl.ds(0, half)] = jnp.where(upper, above, pltpu.roll(below, 4, 0))
    rows_ref[:, pl.ds(half, half)] = jnp.where(upper, pltpu.roll(above, 4, 0), below)
    quarter = width // 4
    window = windows_ref.shape[1] // 2
    depth = lax.axis_index("depth")
    for place, quarters in enumerate((depth ^ 2, depth ^ 3)):
        cut = pl.ds(pl.multiple_of(window_start(quarters, quarter, window), LANES), window)
        windows_ref[:, pl.ds(place * window, window)] = rows_ref[:, cut]


def local_kernel(flux_ref, base, ratio, inv, head_ref, out_ref):
    nz, _, width = base.shape
    sublane = lax.broadcasted_iota(jnp.int32, (ROWS, CHUNK), 0)

    @pl.loop(0, width // CHUNK)
    def _(chunk):
        lanes = pl.ds(pl.multiple_of(chunk * CHUNK, CHUNK), CHUNK)
        y = None
        for z in range(nz):
            row = pl.ds(z, 1)
            added = jnp.where(sublane == 0, flux_ref[1, row, lanes], 0.0)
            added = jnp.where(sublane == ROWS - 1, flux_ref[0, row, lanes], added)
            rhs = base[z, :, lanes] + added
            y = rhs if z == 0 else rhs + ratio[z - 1, :, lanes] * y
            if z < nz - 1:
                out_ref[z, :, lanes] = y
        x = y * inv[nz - 1, :, lanes]
        out_ref[nz - 1, :, lanes] = x + head_ref[nz - 1, :, lanes]
        for z in reversed(range(nz - 1)):
            x = out_ref[z, :, lanes] * inv[z, :, lanes] + ratio[z, :, lanes] * x
            out_ref[z, :, lanes] = x + head_ref[z, :, lanes]


def ends_kernel(mine, other, far_mine, far_other, pair_inv_ref, gain_ref, gap_ref, chip_end_ref):
    depth = lax.axis_index("depth")
    inner = (depth == 1) | (depth == 2)
    sign = jnp.where(depth < 2, 1.0, -1.0)
    own, others = mine[...], other[...]
    gap = sign * jnp.where(inner, others - own, own - others) + 1.0
    gap_ref[...] = gap * pair_inv_ref[...]
    chip_end_ref[...] = jnp.where(inner, far_mine[...], far_other[...]) + sign * gain_ref[...] * gap


def final_kernel(
    local_ref, top_col, bottom_col, gap_ref, gain_ref, res_ref, res_other, end_ref, end_other, level_ref,
    out_ref, surface_ref, held, sem, level_sem,
):
    nz, _, width = local_ref.shape
    depth = lax.axis_index("depth")
    sign = jnp.where(depth < 2, 1.0, -1.0)

    level_copy = pltpu.make_async_copy(level_ref, surface_ref, level_sem)
    level_copy.start()

    def out_copy(chunk):
        lanes = pl.ds(pl.multiple_of(chunk * CHUNK, CHUNK), CHUNK)
        return pltpu.make_async_copy(held.at[:, :, lanes], out_ref.at[:, :, lanes], sem.at[chunk])

    @pl.loop(0, width // CHUNK)
    def _(chunk):
        lanes = pl.ds(pl.multiple_of(chunk * CHUNK, CHUNK), CHUNK)
        flow_chip = (sign * (end_ref[:, lanes] - end_other[:, lanes]) + 1.0) * rcp(
            res_ref[:, lanes] + res_other[:, lanes]
        )
        flow_core = gap_ref[:, lanes] + gain_ref[:, lanes] * flow_chip
        j_in = jnp.where(depth == 0, 0.0, jnp.where(depth == 2, flow_chip, flow_core))
        j_out = jnp.where(depth == 3, 0.0, jnp.where(depth == 1, flow_chip, flow_core))
        for z in range(nz):
            held[z, :, lanes] = (
                local_ref[z, :, lanes] + top_col[z, :, lanes] * j_in - bottom_col[z, :, lanes] * j_out
            )
        out_copy(chunk).start()

    @pl.loop(0, width // CHUNK)
    def _(chunk):
        out_copy(chunk).wait()

    level_copy.wait()


def shift_rows(x, by):
    return pltpu.roll(x, by % x.shape[0], 0)


def shift_lanes(x, by):
    return pltpu.roll(x, by % x.shape[1], 1)


def harmonic(first, second):
    total = first + second
    return 2.0 * first * second * rcp(jnp.where(total > 0.0, total, 1.0))


def face_k(pond, ground, conv, shift):
    pond_two, ground_two, conv_two = shift(pond), shift(ground), shift(conv)
    depth_face = 0.5 * (pond + pond_two)
    slope = pond_two + ground_two - (pond + ground)
    return (
        jnp.exp2((5.0 / 3.0 * LOG2E) * jnp.log(depth_face))
        * harmonic(conv, conv_two)
        * lax.rsqrt(jnp.abs(slope) + SLOPE_FLOOR)
    )


def relay_kernel(rows_ref, exfil_ref, from_chip, chip_other, _, __, sent_ref):
    window = sent_ref.shape[1] // 3
    depth = lax.axis_index("depth")
    is_low = depth < 2
    cut = pl.ds(pl.multiple_of(window_start(depth ^ 1, rows_ref.shape[1] // 4, window), LANES), window)
    first, second, third = (pl.ds(place * window, window) for place in range(3))
    own, other = rows_ref[:, cut], from_chip[:, second]
    sent_ref[:, first] = jnp.where(is_low, own, other)
    sent_ref[:, second] = jnp.where(is_low, other, own)
    sent_ref[:, third] = jnp.where(
        is_low, exfil_ref[:, cut], chip_other[:, pl.ds(chip_other.shape[1] - window, window)]
    )


def surface_kernel(own_ref, exfil_ref, rows_ref, from_chip, from_core, chip_other, out_ref, last):
    window = last.shape[1]
    width = exfil_ref.shape[1]
    quarter = width // 4
    lat = lax.axis_index("lat")
    depth = lax.axis_index("depth")
    is_even = lax.rem(depth, 2) == 0
    upper = lax.broadcasted_iota(jnp.int32, (ROWS, window), 0) < 4
    first, second, third = (pl.ds(place * window, window) for place in range(3))

    cut = pl.ds(pl.multiple_of(window_start(depth, quarter, window), LANES), window)
    mine, other = rows_ref[:, cut], from_chip[:, first]
    here = (jnp.where(depth < 2, mine, other), jnp.where(depth < 2, other, mine))
    there = (from_core[:, first], from_core[:, second])
    outer = [jnp.where(is_even, a, b) for low, high in zip(here, there) for a, b in ((low, high), (high, low))]
    near = jnp.where(depth == 0, exfil_ref[:, first], chip_other[:, pl.ds(width, window)])
    near = jnp.where(is_even, near, from_core[:, third])

    def extended(rows, own):
        own = pltpu.roll(own, 4, 0)
        return jnp.concatenate([jnp.where(upper, rows, own), jnp.where(upper, own, rows)], axis=0)

    exfil, pond, ground, conv = (
        extended(rows, own) for rows, own in zip(outer, (near, own_ref[0], own_ref[1], own_ref[2]))
    )
    row = lax.broadcasted_iota(jnp.int32, conv.shape, 0)
    outside = ((row < 4) & (lat == 0)) | ((row >= 12) & (lat == lax.axis_size("lat") - 1))
    conv = jnp.where(outside, 0.0, conv)
    k_down = face_k(pond, ground, conv, lambda x: shift_rows(x, -1))
    k_up = shift_rows(k_down, 1)
    k_right = face_k(pond, ground, conv, lambda x: shift_lanes(x, -1))
    lane = lax.broadcasted_iota(jnp.int32, conv.shape, 1)
    k_right = jnp.where(lane < window - 1, k_right, 0.0)
    k_left = shift_lanes(k_right, 1)
    diag = 1.0 / SURFACE_STEP + k_up + k_down + k_left + k_right
    rhs = pond * (1.0 / SURFACE_STEP)
    rhs = rhs + k_up * (shift_rows(ground, 1) - ground) + k_down * (shift_rows(ground, -1) - ground)
    rhs = rhs + k_left * (shift_lanes(ground, 1) - ground) + k_right * (shift_lanes(ground, -1) - ground)
    inv = rcp(diag)
    k_up, k_down, k_left, k_right = k_up * inv, k_down * inv, k_left * inv, k_right * inv
    rhs = (rhs + exfil) * inv
    level = pond
    for _ in range(SWEEPS):
        level = (
            rhs
            + k_up * shift_rows(level, 1)
            + k_down * shift_rows(level, -1)
            + k_left * shift_lanes(level, 1)
            + k_right * shift_lanes(level, -1)
        )
    last[...] = level
    start = pl.multiple_of(
        depth * quarter - window_start(depth, quarter, window), LANES
    )
    cut = pl.ds(start, quarter)
    lower_half = lax.broadcasted_iota(jnp.int32, (ROWS, quarter), 0) >= 4
    upper = pltpu.roll(last[pl.ds(0, ROWS), cut], 4, 0)
    lower = pltpu.roll(last[pl.ds(ROWS, ROWS), cut], 4, 0)
    out_ref[...] = jnp.where(lower_half, lower, upper)


def per_device(
    head, head_old, soil, cond_table, shape_table, pore_table, pond, ground, ponded, river
):
    nz, rows, width = head.shape
    window = width // 4 + 2 * LANES
    lat_count = lax.axis_size("lat")
    up, down = [], []
    for i in range(lat_count):
        for j in range(4):
            after, place = (i + 1, j) if i < lat_count - 1 else (0, j ^ 2)
            up.append((4 * i + j, 4 * after + place))
            down.append((4 * after + place, 4 * i + j))
    core = [(0, 1), (1, 0), (2, 3), (3, 2)]
    chip = [(0, 2), (2, 0), (1, 3), (3, 1)]
    block = f32(nz, rows, width)
    padded = f32(nz, rows, width + LANES)
    plane = f32(rows, width)

    side = f32(rows, 2 * (nz // ROWS) * width + width // 2)

    own_up, own_down, tables, exfil, own_fields = call(
        pack_kernel,
        "pack",
        [in_hbm(x) for x in (cond_table, shape_table, pore_table, head, soil, pond, ground, ponded, river)],
        [side, side, f32(6, ROWS, LANES), plane, f32(3, rows, window)],
        scratch=[
            pltpu.SMEM((3, cond_table.shape[0]), jnp.float32),
            pltpu.VMEM((2, nz // ROWS, ROWS, width), jnp.int32),
            pltpu.VMEM((rows, width), jnp.float32),
            pltpu.VMEM((rows, width), jnp.int32),
            pltpu.VMEM((rows, width), jnp.float32),
            pltpu.VMEM((rows, width), jnp.float32),
            pltpu.VMEM((rows, width), jnp.int32),
            pltpu.VMEM((rows, width), jnp.int32),
            pltpu.SemaphoreType.DMA((9 + 4 * (nz // ROWS),)),
        ],
    )
    from_above = lax.ppermute(own_up, ("lat", "depth"), up)
    from_below = lax.ppermute(own_down, ("lat", "depth"), down)

    head_v, sigma, base, ratio, inv, top_col, bottom_col, resist = call(
        factor_kernel,
        "factor",
        [in_vmem(tables), in_vmem(exfil)] + [in_hbm(x) for x in (head, head_old, soil)],
        [padded, padded] + [block] * 5 + [f32(rows, 3 * width)],
        scratch=[
            pltpu.VMEM((nz, rows, width), jnp.float32),
            pltpu.VMEM((nz, rows, width), jnp.int32),
            pltpu.SemaphoreType.DMA((3, width // CHUNK)),
        ],
    )
    resist_other = lax.ppermute(resist, "depth", core)
    pair_inv, gain, chip_sent = call(
        pair_kernel,
        "pair",
        [in_vmem(x) for x in (resist, resist_other, exfil)],
        [plane, plane, f32(rows, width + 2 * window)],
    )
    chip_other = lax.ppermute(chip_sent, "depth", chip)

    base, sums, end_rows = call(
        lateral_kernel,
        "lateral",
        [in_vmem(x) for x in (head_v, sigma, base, top_col, bottom_col, gain)],
        [block, f32(2 * rows, width), f32(4, nz, width)],
        scratch=[pltpu.VMEM((3, nz, rows, LANES), jnp.float32), pltpu.SemaphoreType.DMA((4,))],
    )
    flux, ends, far_ends, field_rows, windows = call(
        halo_kernel,
        "halo",
        [in_vmem(x) for x in (own_up, own_down, from_above, from_below, end_rows, sums, gain)],
        [f32(2, nz, width), plane, plane, plane, f32(rows, 2 * window)],
    )
    near_other = lax.ppermute(ends, "depth", core)
    far_other = lax.ppermute(far_ends, "depth", core)
    windows_chip = lax.ppermute(windows, "depth", chip)
    local = call(
        local_kernel, "local", [in_vmem(x) for x in (flux, base, ratio, inv, head_v)], [block]
    )[0]
    gap, chip_end = call(
        ends_kernel, "ends", [in_vmem(x) for x in (ends, near_other, far_ends, far_other, pair_inv, gain)], [plane, plane]
    )
    chip_end_other = lax.ppermute(chip_end, "depth", chip)
    relayed = call(
        relay_kernel,
        "relay",
        [in_vmem(x) for x in (field_rows, exfil, windows_chip, chip_other, chip_end, local)],
        [f32(rows, 3 * window)],
    )[0]
    windows_core = lax.ppermute(relayed, "depth", core)
    level = call(
        surface_kernel,
        "surface",
        [
            in_vmem(x)
            for x in (own_fields, exfil, field_rows, windows_chip, windows_core, chip_other)
        ],
        [f32(rows, width // 4)],
        scratch=[pltpu.VMEM((2 * rows, window), jnp.float32)],
    )[0]
    head_new, surface_new = call(
        final_kernel,
        "final",
        [
            in_vmem(x)
            for x in (
                local, top_col, bottom_col, gap, gain, chip_sent, chip_other, chip_end, chip_end_other, level,
            )
        ],
        [
            jax.ShapeDtypeStruct((nz, rows, width), jnp.float32),
            jax.ShapeDtypeStruct((rows, width // 4), jnp.float32),
        ],
        out_specs=[ANY, ANY],
        scratch=[
            pltpu.VMEM((nz, rows, width), jnp.float32),
            pltpu.SemaphoreType.DMA((width // CHUNK,)),
            pltpu.SemaphoreType.DMA,
        ],
    )
    return (head_new, surface_new)


def solution(mesh):
    placed = (
        P("depth", "lat", None),
        P("depth", "lat", None),
        P("depth", "lat", None),
        P(),
        P(),
        P(),
        P("lat", None),
        P("lat", None),
        P("lat", None),
        P("lat", None),
    )
    return jax.shard_map(
        per_device,
        mesh=mesh,
        in_specs=placed,
        out_specs=(P("depth", "lat", None), P("lat", "depth")),
        check_vma=False,
    )
```

```python
import jax
import jax.numpy as jnp
from jax import lax
from jax.experimental import pallas as pl
from jax.experimental.pallas import tpu as pltpu
from jax.sharding import PartitionSpec as P

SWEEPS = 4

TIME_STEP = 20.0
SURFACE_STEP = 2.0
SPECIFIC_STORAGE = 0.01
LAND_CONVEYANCE = 3.0
RIVER_CONVEYANCE = 10.0
SLOPE_FLOOR = 0.01

LOG2E = 1.4426950408889634
LN2 = 0.6931471805599453
CLOSED = 1e37

LANES = 128
ROWS = 8
CHUNK = 512
HALO_CHUNK = 1024
AHEAD = 5
VMEM_LIMIT = 8 * 1024 * 1024

VMEM = pl.BlockSpec(memory_space=pltpu.VMEM)
ANY = pl.BlockSpec(memory_space=pl.ANY)


def f32(*shape):
    return pltpu.VMEM(shape, jnp.float32)


def in_vmem(x):
    return (VMEM, pltpu.with_memory_space_constraint(x, pltpu.VMEM))


def in_hbm(x):
    return (ANY, pltpu.with_memory_space_constraint(x, pltpu.HBM))


FLOPS = {}


def call(kernel, name, args, out_shape, out_specs=None, scratch=()):
    return pl.pallas_call(
        kernel,
        out_shape=out_shape,
        in_specs=[spec for spec, _ in args],
        out_specs=out_specs or [VMEM] * len(out_shape),
        scratch_shapes=list(scratch),
        compiler_params=pltpu.CompilerParams(vmem_limit_bytes=VMEM_LIMIT),
        cost_estimate=pl.CostEstimate(flops=FLOPS.get(name, 1), bytes_accessed=1, transcendentals=0),
        name=name,
    )(*(x for _, x in args))


def rcp(x):
    return pl.reciprocal(x, approx=True)


def lookup(table, soil):
    numbers = lax.GatherDimensionNumbers(
        offset_dims=(),
        collapsed_slice_dims=(0,),
        start_index_map=(0,),
        operand_batching_dims=(1,),
        start_indices_batching_dims=(1,),
    )
    low, high = table
    blocks = []
    for top in range(0, soil.shape[0], ROWS):
        parts = []
        for start in range(0, soil.shape[1], LANES):
            kind = soil[top : top + ROWS, start : start + LANES]
            index = (kind & (ROWS - 1))[..., None]
            found = [
                lax.gather(half, index, numbers, (1, 1), mode=lax.GatherScatterMode.PROMISE_IN_BOUNDS)
                for half in table
            ]
            parts.append(jnp.where(kind < ROWS, *found))
        blocks.append(jnp.concatenate(parts, axis=1) if len(parts) > 1 else parts[0])
    return jnp.concatenate(blocks, axis=0) if len(blocks) > 1 else blocks[0]


def window_start(quarter, width, window):
    return jnp.clip(quarter * width - LANES, 0, 4 * width - window)


def static_window(quarter, width, window):
    return pl.ds(min(max(quarter * width - LANES, 0), 4 * width - window), window)


def pack_kernel(
    cond_ref, shape_ref, pore_ref, head_ref, soil_ref, pond_ref, ground_ref, ponded_ref, river_ref,
    up_ref, down_ref, table_ref, exfil_ref, own_ref,
    small, soils, head_top, soil_top, pond, ground, ponded, river, sem,
):
    nz, _, width = head_ref.shape
    groups = nz // ROWS
    quarter = width // 4
    window = quarter + 2 * LANES
    half = width // 2
    depth = lax.axis_index("depth")
    sides = (up_ref, down_ref)
    pairs = [
        (cond_ref, small.at[0]),
        (shape_ref, small.at[1]),
        (pore_ref, small.at[2]),
        (head_ref.at[0], head_top),
        (soil_ref.at[0], soil_top),
        (pond_ref, pond),
        (ponded_ref, ponded),
        (ground_ref, ground),
        (river_ref, river),
    ]
    fields = len(pairs)
    for group in range(groups):
        layers = pl.ds(group * ROWS, ROWS)
        for side, (target, row) in enumerate(zip(sides, (ROWS - 1, 0))):
            pairs.append((soil_ref.at[layers, row, :], soils.at[side, group]))
            pairs.append((head_ref.at[layers, row, :], target.at[:, pl.ds(group * width, width)]))
    copies = [pltpu.make_async_copy(source, target, sem.at[i]) for i, (source, target) in enumerate(pairs)]
    for copy in copies:
        copy.start()

    for copy in copies[:3]:
        copy.wait()
    row = lax.broadcasted_iota(jnp.int32, (ROWS, LANES), 0)
    registers = []
    for place in range(3):
        halves = []
        for top in (0, ROWS):
            value = jnp.ones((ROWS, LANES), jnp.float32)
            for soil_kind in range(top, min(top + ROWS, cond_ref.shape[0])):
                value = jnp.where(row == soil_kind - top, small[place, soil_kind], value)
            halves.append(value)
        registers.append(halves)
    cond_table, shape_table, pore_table = registers
    half_res = [0.5 / value for value in cond_table]
    steep = [value * LOG2E for value in shape_table]
    pore_table = [value * (1.0 / TIME_STEP) for value in pore_table]
    for place, halves in enumerate((half_res, steep, pore_table)):
        table_ref[2 * place] = halves[0]
        table_ref[2 * place + 1] = halves[1]

    for copy in copies[3:fields]:
        copy.wait()
    wet_pond = ponded[...].astype(jnp.float32) * pond[...]
    conductivity = lookup(cond_table, soil_top[...]) * jnp.exp2(
        lookup(steep, soil_top[...]) * jnp.minimum(head_top[...], 0.0)
    )
    exfil = -conductivity * (2.0 * (wet_pond - head_top[...]) + 1.0)
    exfil_ref[...] = exfil
    conv = LAND_CONVEYANCE + (RIVER_CONVEYANCE - LAND_CONVEYANCE) * river[...].astype(jnp.float32)
    field = jnp.where(
        depth < 2, jnp.where(depth == 0, exfil, pond[...]), jnp.where(depth == 2, ground[...], conv)
    )
    upper = lax.broadcasted_iota(jnp.int32, (ROWS, half), 0) < 4
    into = pl.ds(2 * groups * width, half)
    left, right = field[:, :half], field[:, half:]
    up_ref[:, into] = jnp.where(upper, pltpu.roll(left, 4, 0), right)
    down_ref[:, into] = jnp.where(upper, left, pltpu.roll(right, 4, 0))
    cut = pl.ds(pl.multiple_of(window_start(depth, quarter, window), LANES), window)
    own_ref[0] = pond[:, cut]
    own_ref[1] = ground[:, cut]
    own_ref[2] = LAND_CONVEYANCE + (RIVER_CONVEYANCE - LAND_CONVEYANCE) * river[:, cut].astype(jnp.float32)

    following = iter(copies[fields:])
    for group in range(groups):
        for side, target in enumerate(sides):
            next(following).wait()
            next(following).wait()
            head = target[:, pl.ds(group * width, width)]
            soil = soils[side, group]
            target[:, pl.ds((groups + group) * width, width)] = lookup(half_res, soil) * jnp.exp2(
                -lookup(steep, soil) * jnp.minimum(head, 0.0)
            )


def factor_kernel(
    table_ref, exfil_ref, head_hbm, old_hbm, soil_hbm,
    head_ref, sigma, base, ratio, inv, top_col, bottom_col, resist_ref, old_ref, soil_ref, sem,
):
    nz, _, width = base.shape
    depth = lax.axis_index("depth")
    is_top = jnp.where(depth == 0, 1.0, 0.0)
    is_bottom = jnp.where(depth == 3, 1.0, 0.0)
    is_even = lax.rem(depth, 2) == 0
    chunks = width // CHUNK

    def fetch(chunk):
        lanes = pl.ds(pl.multiple_of(chunk * CHUNK, CHUNK), CHUNK)
        return [
            pltpu.make_async_copy(source.at[:, :, lanes], target.at[:, :, lanes], sem.at[i, chunk])
            for i, (source, target) in enumerate(((head_hbm, head_ref), (soil_hbm, soil_ref), (old_hbm, old_ref)))
        ]

    for chunk in range(AHEAD):
        for copy in fetch(chunk):
            copy.start()
    half_res, steep, porosity = ((table_ref[2 * place], table_ref[2 * place + 1]) for place in range(3))
    sigma[:, :, pl.ds(width, LANES)] = jnp.full((nz, ROWS, LANES), CLOSED, jnp.float32)
    head_ref[:, :, pl.ds(width, LANES)] = jnp.zeros((nz, ROWS, LANES), jnp.float32)

    @pl.loop(0, chunks)
    def _(chunk):
        lanes = pl.ds(pl.multiple_of(chunk * CHUNK, CHUNK), CHUNK)
        for copy in fetch(chunk):
            copy.wait()

        @pl.when(chunk + AHEAD < chunks)
        def _():
            for copy in fetch(chunk + AHEAD):
                copy.start()

        def state(z):
            head = head_ref[z, :, lanes]
            old = old_ref[z, :, lanes]
            soil = soil_ref[z, :, lanes]
            alpha = lookup(steep, soil)
            power = alpha * jnp.minimum(head, 0.0)
            wet = jnp.exp2(power)
            wet_old = jnp.exp2(alpha * jnp.minimum(old, 0.0))
            res = lookup(half_res, soil) * rcp(wet)
            sigma[z, :, lanes] = res
            pore = lookup(porosity, soil)
            pore_wet = pore * wet
            storage = pore * wet_old - pore_wet + (SPECIFIC_STORAGE / TIME_STEP) * (old - head)
            capacity = SPECIFIC_STORAGE / TIME_STEP + (alpha * LN2) * pore_wet
            return head, res, storage, capacity

        now = state(0)
        sigma_top = now[1]
        face_above = flux_above = ratio_above = column = None
        for z in range(nz):
            head, res, b, d = now
            if z == 0:
                b = b - exfil_ref[:, lanes] * is_top
                d = d + rcp(res) * is_top
            else:
                b = b + flux_above
                d = d + face_above * (1.0 - ratio_above)
            if z == nz - 1:
                b = b - 0.5 * rcp(res) * is_bottom
            else:
                after = state(z + 1)
                face = rcp(res + after[1])
                flux = face * (head - after[0] + 1.0)
                b = b - flux
                d = d + face
            pivot_inv = rcp(d)
            base[z, :, lanes] = b
            inv[z, :, lanes] = pivot_inv
            column = pivot_inv if z == 0 else column * pivot_inv
            if z < nz - 1:
                ratio_above = face * pivot_inv
                ratio[z, :, lanes] = ratio_above
                top_col[z, :, lanes] = column
                column = column * face
                face_above, flux_above = face, flux
                now = after
        first, last = column, pivot_inv
        top_col[nz - 1, :, lanes] = first
        bottom_col[nz - 1, :, lanes] = last
        corner = first
        r_bottom = res + last
        for z in reversed(range(nz - 1)):
            m = ratio[z, :, lanes]
            first = top_col[z, :, lanes] + m * first
            last = m * last
            top_col[z, :, lanes] = first
            bottom_col[z, :, lanes] = last
        r_top = sigma_top + first
        resist_ref[:, lanes] = jnp.where(is_even, r_bottom, r_top)
        resist_ref[:, pl.ds(pl.multiple_of(width + chunk * CHUNK, CHUNK), CHUNK)] = jnp.where(is_even, r_top, r_bottom)
        resist_ref[:, pl.ds(pl.multiple_of(2 * width + chunk * CHUNK, CHUNK), CHUNK)] = corner


def lateral_kernel(
    head_ref, sigma, base_in, top_col, bottom_col, _, base, sums_ref, rows_ref, carried,
):
    nz, _, width = base.shape
    sublane = lax.broadcasted_iota(jnp.int32, (ROWS, CHUNK), 0)
    inner = sublane < ROWS - 1
    lane = lax.broadcasted_iota(jnp.int32, (ROWS, LANES), 1)
    is_first, is_last = lane == 0, lane == LANES - 1
    count = CHUNK // LANES

    def left(x):
        return pltpu.roll(x, LANES - 1, 1)

    def registers(x):
        return [x[:, k * LANES : (k + 1) * LANES] for k in range(x.shape[1] // LANES)]

    for z in range(nz):
        carried[0, z] = left(sigma[z, :, pl.ds(0, LANES)])
        carried[1, z] = left(head_ref[z, :, pl.ds(0, LANES)])
        carried[2, z] = jnp.zeros((ROWS, LANES), jnp.float32)

    @pl.loop(0, width // CHUNK)
    def _(chunk):
        start = pl.multiple_of(chunk * CHUNK, CHUNK)
        lanes = pl.ds(start, CHUNK)
        after = pl.ds(pl.multiple_of(start + LANES, LANES), CHUNK)
        top_sum = bottom_sum = None
        for z in range(nz):
            s, h = sigma[z, :, lanes], head_ref[z, :, lanes]
            moved = []
            for place, array in ((0, sigma), (1, head_ref)):
                found = [carried[place, z]] + [left(x) for x in registers(array[z, :, after])]
                carried[place, z] = found[count]
                moved.append(
                    jnp.concatenate(
                        [jnp.where(is_last, found[k + 1], found[k]) for k in range(count)], axis=1
                    )
                )
            s_right, h_right = moved
            flux_y = rcp(s + s_right) * (h_right - h)
            found = [carried[2, z]] + [pltpu.roll(x, 1, 1) for x in registers(flux_y)]
            carried[2, z] = found[count]
            flux_left = jnp.concatenate(
                [jnp.where(is_first, found[k], found[k + 1]) for k in range(count)], axis=1
            )
            flux_x = rcp(s + pltpu.roll(s, ROWS - 1, 0)) * (pltpu.roll(h, ROWS - 1, 0) - h)
            flux_x = jnp.where(inner, flux_x, 0.0)
            b = base_in[z, :, lanes] + (flux_y - flux_left) + (flux_x - pltpu.roll(flux_x, 1, 0))
            base[z, :, lanes] = b
            ends = (top_col[z, :, lanes], bottom_col[z, :, lanes])
            for place, end in enumerate(ends):
                rows_ref[2 * place, pl.ds(z, 1), lanes] = end[ROWS - 1 :]
                rows_ref[2 * place + 1, pl.ds(z, 1), lanes] = end[:1]
            first, last = (end * b for end in ends)
            top_sum = first if z == 0 else top_sum + first
            bottom_sum = last if z == 0 else bottom_sum + last
        sums_ref[pl.ds(0, ROWS), lanes] = top_sum + head_ref[0, :, lanes]
        sums_ref[pl.ds(ROWS, ROWS), lanes] = bottom_sum + head_ref[nz - 1, :, lanes]


def pair_kernel(mine, other, exfil_ref, pair_inv_ref, gain_ref, sent_ref):
    width = gain_ref.shape[1]
    window = (sent_ref.shape[1] - width) // 2
    depth = lax.axis_index("depth")
    inner = (depth == 1) | (depth == 2)
    near, far, corner = (pl.ds(place * width, width) for place in range(3))
    pair_inv = rcp(mine[:, near] + other[:, near])
    inner_corner = jnp.where(inner, mine[:, corner], other[:, corner])
    gain = inner_corner * pair_inv
    pair_inv_ref[...] = pair_inv
    gain_ref[...] = gain
    sent_ref[:, pl.ds(0, width)] = jnp.where(inner, mine[:, far], other[:, far]) - inner_corner * gain
    for place, quarters in enumerate((depth ^ 2, depth ^ 3)):
        cut = pl.ds(pl.multiple_of(window_start(quarters, width // 4, window), LANES), window)
        sent_ref[:, pl.ds(width + place * window, window)] = exfil_ref[:, cut]


def halo_kernel(
    own_up, own_down, from_above, from_below, end_rows, sums_ref, _, flux_ref, near_ref, far_ref, rows_ref, windows_ref,
):
    _, nz, width = flux_ref.shape
    lat = lax.axis_index("lat")
    has_above = jnp.where(lat == 0, 0.0, 1.0)
    has_below = jnp.where(lat == lax.axis_size("lat") - 1, 0.0, 1.0)
    is_even = lax.rem(lax.axis_index("depth"), 2) == 0
    sublane = lax.broadcasted_iota(jnp.int32, (ROWS, HALO_CHUNK), 0)

    @pl.loop(0, width // HALO_CHUNK)
    def _(chunk):
        start = pl.multiple_of(chunk * HALO_CHUNK, HALO_CHUNK)
        lanes = pl.ds(start, HALO_CHUNK)
        added = [[], []]
        for side, other, own, scale in ((0, from_below, own_up, has_below), (1, from_above, own_down, has_above)):
            totals = [None, None]
            for group in range(nz // ROWS):
                heads = pl.ds(pl.multiple_of(group * width + start, HALO_CHUNK), HALO_CHUNK)
                sigmas = pl.ds(pl.multiple_of((nz // ROWS + group) * width + start, HALO_CHUNK), HALO_CHUNK)
                layers = pl.ds(group * ROWS, ROWS)
                flux = rcp(other[:, sigmas] + own[:, sigmas]) * ((other[:, heads] - own[:, heads]) * scale)
                flux_ref[side, layers, lanes] = flux
                for end in range(2):
                    part = flux * end_rows[2 * end + side, layers, lanes]
                    totals[end] = part if group == 0 else totals[end] + part
            for end in range(2):
                total = totals[end]
                for by in (4, 2, 1):
                    total = total + pltpu.roll(total, by, 0)
                added[end].append(total)
        sums = []
        for end in range(2):
            total = jnp.where(sublane == 0, added[end][1], 0.0)
            total = jnp.where(sublane == ROWS - 1, added[end][0], total)
            sums.append(sums_ref[pl.ds(end * ROWS, ROWS), lanes] + total)
        near_ref[:, lanes] = jnp.where(is_even, sums[1], sums[0])
        far_ref[:, lanes] = jnp.where(is_even, sums[0], sums[1])

    half = width // 2
    extra = pl.ds(own_up.shape[1] - half, half)
    upper = lax.broadcasted_iota(jnp.int32, (ROWS, half), 0) < 4
    above, below = from_above[:, extra], from_below[:, extra]
    rows_ref[:, pl.ds(0, half)] = jnp.where(upper, above, pltpu.roll(below, 4, 0))
    rows_ref[:, pl.ds(half, half)] = jnp.where(upper, pltpu.roll(above, 4, 0), below)
    quarter = width // 4
    window = windows_ref.shape[1] // 2
    depth = lax.axis_index("depth")
    for place, quarters in enumerate((depth ^ 2, depth ^ 3)):
        cut = pl.ds(pl.multiple_of(window_start(quarters, quarter, window), LANES), window)
        windows_ref[:, pl.ds(place * window, window)] = rows_ref[:, cut]


def local_kernel(flux_ref, base, ratio, inv, head_ref, out_ref):
    nz, _, width = base.shape
    sublane = lax.broadcasted_iota(jnp.int32, (ROWS, CHUNK), 0)

    @pl.loop(0, width // CHUNK)
    def _(chunk):
        lanes = pl.ds(pl.multiple_of(chunk * CHUNK, CHUNK), CHUNK)
        y = None
        for z in range(nz):
            row = pl.ds(z, 1)
            added = jnp.where(sublane == 0, flux_ref[1, row, lanes], 0.0)
            added = jnp.where(sublane == ROWS - 1, flux_ref[0, row, lanes], added)
            rhs = base[z, :, lanes] + added
            y = rhs if z == 0 else rhs + ratio[z - 1, :, lanes] * y
            if z < nz - 1:
                out_ref[z, :, lanes] = y
        x = y * inv[nz - 1, :, lanes]
        out_ref[nz - 1, :, lanes] = x + head_ref[nz - 1, :, lanes]
        for z in reversed(range(nz - 1)):
            x = out_ref[z, :, lanes] * inv[z, :, lanes] + ratio[z, :, lanes] * x
            out_ref[z, :, lanes] = x + head_ref[z, :, lanes]


def ends_kernel(mine, other, far_mine, far_other, pair_inv_ref, gain_ref, gap_ref, chip_end_ref):
    depth = lax.axis_index("depth")
    inner = (depth == 1) | (depth == 2)
    sign = jnp.where(depth < 2, 1.0, -1.0)
    own, others = mine[...], other[...]
    gap = sign * jnp.where(inner, others - own, own - others) + 1.0
    gap_ref[...] = gap * pair_inv_ref[...]
    chip_end_ref[...] = jnp.where(inner, far_mine[...], far_other[...]) + sign * gain_ref[...] * gap


def final_kernel(
    local_ref, top_col, bottom_col, gap_ref, gain_ref, res_ref, res_other, end_ref, end_other, level_ref,
    out_ref, surface_ref, held, sem, level_sem,
):
    nz, _, width = local_ref.shape
    depth = lax.axis_index("depth")
    sign = jnp.where(depth < 2, 1.0, -1.0)

    level_copy = pltpu.make_async_copy(level_ref, surface_ref, level_sem)
    level_copy.start()

    def out_copy(chunk):
        lanes = pl.ds(pl.multiple_of(chunk * CHUNK, CHUNK), CHUNK)
        return pltpu.make_async_copy(held.at[:, :, lanes], out_ref.at[:, :, lanes], sem.at[chunk])

    @pl.loop(0, width // CHUNK)
    def _(chunk):
        lanes = pl.ds(pl.multiple_of(chunk * CHUNK, CHUNK), CHUNK)
        flow_chip = (sign * (end_ref[:, lanes] - end_other[:, lanes]) + 1.0) * rcp(
            res_ref[:, lanes] + res_other[:, lanes]
        )
        flow_core = gap_ref[:, lanes] + gain_ref[:, lanes] * flow_chip
        j_in = jnp.where(depth == 0, 0.0, jnp.where(depth == 2, flow_chip, flow_core))
        j_out = jnp.where(depth == 3, 0.0, jnp.where(depth == 1, flow_chip, flow_core))
        for z in range(nz):
            held[z, :, lanes] = (
                local_ref[z, :, lanes] + top_col[z, :, lanes] * j_in - bottom_col[z, :, lanes] * j_out
            )
        out_copy(chunk).start()

    @pl.loop(0, width // CHUNK)
    def _(chunk):
        out_copy(chunk).wait()

    level_copy.wait()


def shift_rows(x, by):
    return pltpu.roll(x, by % x.shape[0], 0)


def shift_lanes(x, by):
    return pltpu.roll(x, by % x.shape[1], 1)


def harmonic(first, second):
    total = first + second
    return 2.0 * first * second * rcp(jnp.where(total > 0.0, total, 1.0))


def face_k(pond, ground, conv, shift):
    pond_two, ground_two, conv_two = shift(pond), shift(ground), shift(conv)
    depth_face = 0.5 * (pond + pond_two)
    slope = pond_two + ground_two - (pond + ground)
    return (
        jnp.exp2((5.0 / 3.0 * LOG2E) * jnp.log(depth_face))
        * harmonic(conv, conv_two)
        * lax.rsqrt(jnp.abs(slope) + SLOPE_FLOOR)
    )


def relay_kernel(rows_ref, exfil_ref, from_chip, chip_other, _, __, sent_ref):
    window = sent_ref.shape[1] // 3
    depth = lax.axis_index("depth")
    is_low = depth < 2
    cut = pl.ds(pl.multiple_of(window_start(depth ^ 1, rows_ref.shape[1] // 4, window), LANES), window)
    first, second, third = (pl.ds(place * window, window) for place in range(3))
    own, other = rows_ref[:, cut], from_chip[:, second]
    sent_ref[:, first] = jnp.where(is_low, own, other)
    sent_ref[:, second] = jnp.where(is_low, other, own)
    sent_ref[:, third] = jnp.where(
        is_low, exfil_ref[:, cut], chip_other[:, pl.ds(chip_other.shape[1] - window, window)]
    )


def surface_kernel(own_ref, exfil_ref, rows_ref, from_chip, from_core, chip_other, out_ref, last):
    window = last.shape[1]
    width = exfil_ref.shape[1]
    quarter = width // 4
    lat = lax.axis_index("lat")
    depth = lax.axis_index("depth")
    is_even = lax.rem(depth, 2) == 0
    upper = lax.broadcasted_iota(jnp.int32, (ROWS, window), 0) < 4
    first, second, third = (pl.ds(place * window, window) for place in range(3))

    cut = pl.ds(pl.multiple_of(window_start(depth, quarter, window), LANES), window)
    mine, other = rows_ref[:, cut], from_chip[:, first]
    here = (jnp.where(depth < 2, mine, other), jnp.where(depth < 2, other, mine))
    there = (from_core[:, first], from_core[:, second])
    outer = [jnp.where(is_even, a, b) for low, high in zip(here, there) for a, b in ((low, high), (high, low))]
    near = jnp.where(depth == 0, exfil_ref[:, first], chip_other[:, pl.ds(width, window)])
    near = jnp.where(is_even, near, from_core[:, third])

    def extended(rows, own):
        own = pltpu.roll(own, 4, 0)
        return jnp.concatenate([jnp.where(upper, rows, own), jnp.where(upper, own, rows)], axis=0)

    exfil, pond, ground, conv = (
        extended(rows, own) for rows, own in zip(outer, (near, own_ref[0], own_ref[1], own_ref[2]))
    )
    row = lax.broadcasted_iota(jnp.int32, conv.shape, 0)
    outside = ((row < 4) & (lat == 0)) | ((row >= 12) & (lat == lax.axis_size("lat") - 1))
    conv = jnp.where(outside, 0.0, conv)
    k_down = face_k(pond, ground, conv, lambda x: shift_rows(x, -1))
    k_up = shift_rows(k_down, 1)
    k_right = face_k(pond, ground, conv, lambda x: shift_lanes(x, -1))
    lane = lax.broadcasted_iota(jnp.int32, conv.shape, 1)
    k_right = jnp.where(lane < window - 1, k_right, 0.0)
    k_left = shift_lanes(k_right, 1)
    diag = 1.0 / SURFACE_STEP + k_up + k_down + k_left + k_right
    rhs = pond * (1.0 / SURFACE_STEP)
    rhs = rhs + k_up * (shift_rows(ground, 1) - ground) + k_down * (shift_rows(ground, -1) - ground)
    rhs = rhs + k_left * (shift_lanes(ground, 1) - ground) + k_right * (shift_lanes(ground, -1) - ground)
    inv = rcp(diag)
    k_up, k_down, k_left, k_right = k_up * inv, k_down * inv, k_left * inv, k_right * inv
    rhs = (rhs + exfil) * inv
    level = pond
    for _ in range(SWEEPS):
        level = (
            rhs
            + k_up * shift_rows(level, 1)
            + k_down * shift_rows(level, -1)
            + k_left * shift_lanes(level, 1)
            + k_right * shift_lanes(level, -1)
        )
    last[...] = level
    start = pl.multiple_of(
        depth * quarter - window_start(depth, quarter, window), LANES
    )
    cut = pl.ds(start, quarter)
    lower_half = lax.broadcasted_iota(jnp.int32, (ROWS, quarter), 0) >= 4
    upper = pltpu.roll(last[pl.ds(0, ROWS), cut], 4, 0)
    lower = pltpu.roll(last[pl.ds(ROWS, ROWS), cut], 4, 0)
    out_ref[...] = jnp.where(lower_half, lower, upper)


def per_device(
    head, head_old, soil, cond_table, shape_table, pore_table, pond, ground, ponded, river
):
    nz, rows, width = head.shape
    window = width // 4 + 2 * LANES
    lat_count = lax.axis_size("lat")
    up, down = [], []
    for i in range(lat_count):
        for j in range(4):
            after, place = (i + 1, j) if i < lat_count - 1 else (0, j ^ 2)
            up.append((4 * i + j, 4 * after + place))
            down.append((4 * after + place, 4 * i + j))
    core = [(0, 1), (1, 0), (2, 3), (3, 2)]
    chip = [(0, 2), (2, 0), (1, 3), (3, 1)]
    block = f32(nz, rows, width)
    padded = f32(nz, rows, width + LANES)
    plane = f32(rows, width)

    side = f32(rows, 2 * (nz // ROWS) * width + width // 2)

    own_up, own_down, tables, exfil, own_fields = call(
        pack_kernel,
        "pack",
        [in_hbm(x) for x in (cond_table, shape_table, pore_table, head, soil, pond, ground, ponded, river)],
        [side, side, f32(6, ROWS, LANES), plane, f32(3, rows, window)],
        scratch=[
            pltpu.SMEM((3, cond_table.shape[0]), jnp.float32),
            pltpu.VMEM((2, nz // ROWS, ROWS, width), jnp.int32),
            pltpu.VMEM((rows, width), jnp.float32),
            pltpu.VMEM((rows, width), jnp.int32),
            pltpu.VMEM((rows, width), jnp.float32),
            pltpu.VMEM((rows, width), jnp.float32),
            pltpu.VMEM((rows, width), jnp.int32),
            pltpu.VMEM((rows, width), jnp.int32),
            pltpu.SemaphoreType.DMA((9 + 4 * (nz // ROWS),)),
        ],
    )
    from_above = lax.ppermute(own_up, ("lat", "depth"), up)
    from_below = lax.ppermute(own_down, ("lat", "depth"), down)

    head_v, sigma, base, ratio, inv, top_col, bottom_col, resist = call(
        factor_kernel,
        "factor",
        [in_vmem(tables), in_vmem(exfil)] + [in_hbm(x) for x in (head, head_old, soil)],
        [padded, padded] + [block] * 5 + [f32(rows, 3 * width)],
        scratch=[
            pltpu.VMEM((nz, rows, width), jnp.float32),
            pltpu.VMEM((nz, rows, width), jnp.int32),
            pltpu.SemaphoreType.DMA((3, width // CHUNK)),
        ],
    )
    resist_other = lax.ppermute(resist, "depth", core)
    pair_inv, gain, chip_sent = call(
        pair_kernel,
        "pair",
        [in_vmem(x) for x in (resist, resist_other, exfil)],
        [plane, plane, f32(rows, width + 2 * window)],
    )
    chip_other = lax.ppermute(chip_sent, "depth", chip)

    base, sums, end_rows = call(
        lateral_kernel,
        "lateral",
        [in_vmem(x) for x in (head_v, sigma, base, top_col, bottom_col, gain)],
        [block, f32(2 * rows, width), f32(4, nz, width)],
        scratch=[pltpu.VMEM((3, nz, rows, LANES), jnp.float32)],
    )
    flux, ends, far_ends, field_rows, windows = call(
        halo_kernel,
        "halo",
        [in_vmem(x) for x in (own_up, own_down, from_above, from_below, end_rows, sums, gain)],
        [f32(2, nz, width), plane, plane, plane, f32(rows, 2 * window)],
    )
    near_other = lax.ppermute(ends, "depth", core)
    far_other = lax.ppermute(far_ends, "depth", core)
    windows_chip = lax.ppermute(windows, "depth", chip)
    local = call(
        local_kernel, "local", [in_vmem(x) for x in (flux, base, ratio, inv, head_v)], [block]
    )[0]
    gap, chip_end = call(
        ends_kernel, "ends", [in_vmem(x) for x in (ends, near_other, far_ends, far_other, pair_inv, gain)], [plane, plane]
    )
    chip_end_other = lax.ppermute(chip_end, "depth", chip)
    relayed = call(
        relay_kernel,
        "relay",
        [in_vmem(x) for x in (field_rows, exfil, windows_chip, chip_other, chip_end, local)],
        [f32(rows, 3 * window)],
    )[0]
    windows_core = lax.ppermute(relayed, "depth", core)
    level = call(
        surface_kernel,
        "surface",
        [
            in_vmem(x)
            for x in (own_fields, exfil, field_rows, windows_chip, windows_core, chip_other)
        ],
        [f32(rows, width // 4)],
        scratch=[pltpu.VMEM((2 * rows, window), jnp.float32)],
    )[0]
    head_new, surface_new = call(
        final_kernel,
        "final",
        [
            in_vmem(x)
            for x in (
                local, top_col, bottom_col, gap, gain, chip_sent, chip_other, chip_end, chip_end_other, level,
            )
        ],
        [
            jax.ShapeDtypeStruct((nz, rows, width), jnp.float32),
            jax.ShapeDtypeStruct((rows, width // 4), jnp.float32),
        ],
        out_specs=[ANY, ANY],
        scratch=[
            pltpu.VMEM((nz, rows, width), jnp.float32),
            pltpu.SemaphoreType.DMA((width // CHUNK,)),
            pltpu.SemaphoreType.DMA,
        ],
    )
    return (head_new, surface_new)


def solution(mesh):
    placed = (
        P("depth", "lat", None),
        P("depth", "lat", None),
        P("depth", "lat", None),
        P(),
        P(),
        P(),
        P("lat", None),
        P("lat", None),
        P("lat", None),
        P("lat", None),
    )
    return jax.shard_map(
        per_device,
        mesh=mesh,
        in_specs=placed,
        out_specs=(P("depth", "lat", None), P("lat", "depth")),
        check_vma=False,
    )
```

```python
import jax
import jax.numpy as jnp
from jax import lax
from jax.experimental import pallas as pl
from jax.experimental.pallas import tpu as pltpu
from jax.sharding import PartitionSpec as P

SWEEPS = 4

TIME_STEP = 20.0
SURFACE_STEP = 2.0
SPECIFIC_STORAGE = 0.01
LAND_CONVEYANCE = 3.0
RIVER_CONVEYANCE = 10.0
SLOPE_FLOOR = 0.01

LOG2E = 1.4426950408889634
LN2 = 0.6931471805599453
CLOSED = 1e37

LANES = 128
ROWS = 8
CHUNK = 512
HALO_CHUNK = 2048
AHEAD = 5
VMEM_LIMIT = 8 * 1024 * 1024

VMEM = pl.BlockSpec(memory_space=pltpu.VMEM)
ANY = pl.BlockSpec(memory_space=pl.ANY)


def f32(*shape):
    return pltpu.VMEM(shape, jnp.float32)


def in_vmem(x):
    return (VMEM, pltpu.with_memory_space_constraint(x, pltpu.VMEM))


def in_hbm(x):
    return (ANY, pltpu.with_memory_space_constraint(x, pltpu.HBM))


FLOPS = {}


def call(kernel, name, args, out_shape, out_specs=None, scratch=()):
    return pl.pallas_call(
        kernel,
        out_shape=out_shape,
        in_specs=[spec for spec, _ in args],
        out_specs=out_specs or [VMEM] * len(out_shape),
        scratch_shapes=list(scratch),
        compiler_params=pltpu.CompilerParams(vmem_limit_bytes=VMEM_LIMIT),
        cost_estimate=pl.CostEstimate(flops=FLOPS.get(name, 1), bytes_accessed=1, transcendentals=0),
        name=name,
    )(*(x for _, x in args))


def rcp(x):
    return pl.reciprocal(x, approx=True)


def lookup(table, soil):
    numbers = lax.GatherDimensionNumbers(
        offset_dims=(),
        collapsed_slice_dims=(0,),
        start_index_map=(0,),
        operand_batching_dims=(1,),
        start_indices_batching_dims=(1,),
    )
    low, high = table
    blocks = []
    for top in range(0, soil.shape[0], ROWS):
        parts = []
        for start in range(0, soil.shape[1], LANES):
            kind = soil[top : top + ROWS, start : start + LANES]
            index = (kind & (ROWS - 1))[..., None]
            found = [
                lax.gather(half, index, numbers, (1, 1), mode=lax.GatherScatterMode.PROMISE_IN_BOUNDS)
                for half in table
            ]
            parts.append(jnp.where(kind < ROWS, *found))
        blocks.append(jnp.concatenate(parts, axis=1) if len(parts) > 1 else parts[0])
    return jnp.concatenate(blocks, axis=0) if len(blocks) > 1 else blocks[0]


def window_start(quarter, width, window):
    return jnp.clip(quarter * width - LANES, 0, 4 * width - window)


def static_window(quarter, width, window):
    return pl.ds(min(max(quarter * width - LANES, 0), 4 * width - window), window)


def pack_kernel(
    cond_ref, shape_ref, pore_ref, head_ref, soil_ref, pond_ref, ground_ref, ponded_ref, river_ref,
    up_ref, down_ref, table_ref, exfil_ref, own_ref,
    small, soils, head_top, soil_top, pond, ground, ponded, river, sem,
):
    nz, _, width = head_ref.shape
    groups = nz // ROWS
    quarter = width // 4
    window = quarter + 2 * LANES
    half = width // 2
    depth = lax.axis_index("depth")
    sides = (up_ref, down_ref)
    pairs = [
        (cond_ref, small.at[0]),
        (shape_ref, small.at[1]),
        (pore_ref, small.at[2]),
        (head_ref.at[0], head_top),
        (soil_ref.at[0], soil_top),
        (pond_ref, pond),
        (ponded_ref, ponded),
        (ground_ref, ground),
        (river_ref, river),
    ]
    fields = len(pairs)
    for group in range(groups):
        layers = pl.ds(group * ROWS, ROWS)
        for side, (target, row) in enumerate(zip(sides, (ROWS - 1, 0))):
            pairs.append((soil_ref.at[layers, row, :], soils.at[side, group]))
            pairs.append((head_ref.at[layers, row, :], target.at[:, pl.ds(group * width, width)]))
    copies = [pltpu.make_async_copy(source, target, sem.at[i]) for i, (source, target) in enumerate(pairs)]
    for copy in copies:
        copy.start()

    for copy in copies[:3]:
        copy.wait()
    row = lax.broadcasted_iota(jnp.int32, (ROWS, LANES), 0)
    registers = []
    for place in range(3):
        halves = []
        for top in (0, ROWS):
            value = jnp.ones((ROWS, LANES), jnp.float32)
            for soil_kind in range(top, min(top + ROWS, cond_ref.shape[0])):
                value = jnp.where(row == soil_kind - top, small[place, soil_kind], value)
            halves.append(value)
        registers.append(halves)
    cond_table, shape_table, pore_table = registers
    half_res = [0.5 / value for value in cond_table]
    steep = [value * LOG2E for value in shape_table]
    pore_table = [value * (1.0 / TIME_STEP) for value in pore_table]
    for place, halves in enumerate((half_res, steep, pore_table)):
        table_ref[2 * place] = halves[0]
        table_ref[2 * place + 1] = halves[1]

    for copy in copies[3:fields]:
        copy.wait()
    wet_pond = ponded[...].astype(jnp.float32) * pond[...]
    conductivity = lookup(cond_table, soil_top[...]) * jnp.exp2(
        lookup(steep, soil_top[...]) * jnp.minimum(head_top[...], 0.0)
    )
    exfil = -conductivity * (2.0 * (wet_pond - head_top[...]) + 1.0)
    exfil_ref[...] = exfil
    conv = LAND_CONVEYANCE + (RIVER_CONVEYANCE - LAND_CONVEYANCE) * river[...].astype(jnp.float32)
    field = jnp.where(
        depth < 2, jnp.where(depth == 0, exfil, pond[...]), jnp.where(depth == 2, ground[...], conv)
    )
    upper = lax.broadcasted_iota(jnp.int32, (ROWS, half), 0) < 4
    into = pl.ds(2 * groups * width, half)
    left, right = field[:, :half], field[:, half:]
    up_ref[:, into] = jnp.where(upper, pltpu.roll(left, 4, 0), right)
    down_ref[:, into] = jnp.where(upper, left, pltpu.roll(right, 4, 0))
    cut = pl.ds(pl.multiple_of(window_start(depth, quarter, window), LANES), window)
    own_ref[0] = pond[:, cut]
    own_ref[1] = ground[:, cut]
    own_ref[2] = LAND_CONVEYANCE + (RIVER_CONVEYANCE - LAND_CONVEYANCE) * river[:, cut].astype(jnp.float32)

    following = iter(copies[fields:])
    for group in range(groups):
        for side, target in enumerate(sides):
            next(following).wait()
            next(following).wait()
            head = target[:, pl.ds(group * width, width)]
            soil = soils[side, group]
            target[:, pl.ds((groups + group) * width, width)] = lookup(half_res, soil) * jnp.exp2(
                -lookup(steep, soil) * jnp.minimum(head, 0.0)
            )


def factor_kernel(
    table_ref, exfil_ref, head_hbm, old_hbm, soil_hbm,
    head_ref, sigma, base, ratio, inv, top_col, bottom_col, resist_ref, old_ref, soil_ref, sem,
):
    nz, _, width = base.shape
    depth = lax.axis_index("depth")
    is_top = jnp.where(depth == 0, 1.0, 0.0)
    is_bottom = jnp.where(depth == 3, 1.0, 0.0)
    is_even = lax.rem(depth, 2) == 0
    chunks = width // CHUNK

    def fetch(chunk):
        lanes = pl.ds(pl.multiple_of(chunk * CHUNK, CHUNK), CHUNK)
        return [
            pltpu.make_async_copy(source.at[:, :, lanes], target.at[:, :, lanes], sem.at[i, chunk])
            for i, (source, target) in enumerate(((head_hbm, head_ref), (soil_hbm, soil_ref), (old_hbm, old_ref)))
        ]

    for chunk in range(AHEAD):
        for copy in fetch(chunk):
            copy.start()
    half_res, steep, porosity = ((table_ref[2 * place], table_ref[2 * place + 1]) for place in range(3))
    sigma[:, :, pl.ds(width, LANES)] = jnp.full((nz, ROWS, LANES), CLOSED, jnp.float32)
    head_ref[:, :, pl.ds(width, LANES)] = jnp.zeros((nz, ROWS, LANES), jnp.float32)

    @pl.loop(0, chunks)
    def _(chunk):
        lanes = pl.ds(pl.multiple_of(chunk * CHUNK, CHUNK), CHUNK)
        for copy in fetch(chunk):
            copy.wait()

        @pl.when(chunk + AHEAD < chunks)
        def _():
            for copy in fetch(chunk + AHEAD):
                copy.start()

        def state(z):
            head = head_ref[z, :, lanes]
            old = old_ref[z, :, lanes]
            soil = soil_ref[z, :, lanes]
            alpha = lookup(steep, soil)
            power = alpha * jnp.minimum(head, 0.0)
            wet = jnp.exp2(power)
            wet_old = jnp.exp2(alpha * jnp.minimum(old, 0.0))
            res = lookup(half_res, soil) * rcp(wet)
            sigma[z, :, lanes] = res
            pore = lookup(porosity, soil)
            pore_wet = pore * wet
            storage = pore * wet_old - pore_wet + (SPECIFIC_STORAGE / TIME_STEP) * (old - head)
            capacity = SPECIFIC_STORAGE / TIME_STEP + (alpha * LN2) * pore_wet
            return head, res, storage, capacity

        now = state(0)
        sigma_top = now[1]
        face_above = flux_above = ratio_above = column = None
        for z in range(nz):
            head, res, b, d = now
            if z == 0:
                b = b - exfil_ref[:, lanes] * is_top
                d = d + rcp(res) * is_top
            else:
                b = b + flux_above
                d = d + face_above * (1.0 - ratio_above)
            if z == nz - 1:
                b = b - 0.5 * rcp(res) * is_bottom
            else:
                after = state(z + 1)
                face = rcp(res + after[1])
                flux = face * (head - after[0] + 1.0)
                b = b - flux
                d = d + face
            pivot_inv = rcp(d)
            base[z, :, lanes] = b
            inv[z, :, lanes] = pivot_inv
            column = pivot_inv if z == 0 else column * pivot_inv
            if z < nz - 1:
                ratio_above = face * pivot_inv
                ratio[z, :, lanes] = ratio_above
                top_col[z, :, lanes] = column
                column = column * face
                face_above, flux_above = face, flux
                now = after
        first, last = column, pivot_inv
        top_col[nz - 1, :, lanes] = first
        bottom_col[nz - 1, :, lanes] = last
        corner = first
        r_bottom = res + last
        for z in reversed(range(nz - 1)):
            m = ratio[z, :, lanes]
            first = top_col[z, :, lanes] + m * first
            last = m * last
            top_col[z, :, lanes] = first
            bottom_col[z, :, lanes] = last
        r_top = sigma_top + first
        resist_ref[:, lanes] = jnp.where(is_even, r_bottom, r_top)
        resist_ref[:, pl.ds(pl.multiple_of(width + chunk * CHUNK, CHUNK), CHUNK)] = jnp.where(is_even, r_top, r_bottom)
        resist_ref[:, pl.ds(pl.multiple_of(2 * width + chunk * CHUNK, CHUNK), CHUNK)] = corner


def lateral_kernel(
    head_ref, sigma, base_in, top_col, bottom_col, _, base, sums_ref, rows_ref, carried,
):
    nz, _, width = base.shape
    sublane = lax.broadcasted_iota(jnp.int32, (ROWS, CHUNK), 0)
    inner = sublane < ROWS - 1
    lane = lax.broadcasted_iota(jnp.int32, (ROWS, LANES), 1)
    is_first, is_last = lane == 0, lane == LANES - 1
    count = CHUNK // LANES

    def left(x):
        return pltpu.roll(x, LANES - 1, 1)

    def registers(x):
        return [x[:, k * LANES : (k + 1) * LANES] for k in range(x.shape[1] // LANES)]

    for z in range(nz):
        carried[0, z] = left(sigma[z, :, pl.ds(0, LANES)])
        carried[1, z] = left(head_ref[z, :, pl.ds(0, LANES)])
        carried[2, z] = jnp.zeros((ROWS, LANES), jnp.float32)

    @pl.loop(0, width // CHUNK)
    def _(chunk):
        start = pl.multiple_of(chunk * CHUNK, CHUNK)
        lanes = pl.ds(start, CHUNK)
        after = pl.ds(pl.multiple_of(start + LANES, LANES), CHUNK)
        top_sum = bottom_sum = None
        for z in range(nz):
            s, h = sigma[z, :, lanes], head_ref[z, :, lanes]
            moved = []
            for place, array in ((0, sigma), (1, head_ref)):
                found = [carried[place, z]] + [left(x) for x in registers(array[z, :, after])]
                carried[place, z] = found[count]
                moved.append(
                    jnp.concatenate(
                        [jnp.where(is_last, found[k + 1], found[k]) for k in range(count)], axis=1
                    )
                )
            s_right, h_right = moved
            flux_y = rcp(s + s_right) * (h_right - h)
            found = [carried[2, z]] + [pltpu.roll(x, 1, 1) for x in registers(flux_y)]
            carried[2, z] = found[count]
            flux_left = jnp.concatenate(
                [jnp.where(is_first, found[k], found[k + 1]) for k in range(count)], axis=1
            )
            flux_x = rcp(s + pltpu.roll(s, ROWS - 1, 0)) * (pltpu.roll(h, ROWS - 1, 0) - h)
            flux_x = jnp.where(inner, flux_x, 0.0)
            b = base_in[z, :, lanes] + (flux_y - flux_left) + (flux_x - pltpu.roll(flux_x, 1, 0))
            base[z, :, lanes] = b
            ends = (top_col[z, :, lanes], bottom_col[z, :, lanes])
            for place, end in enumerate(ends):
                rows_ref[2 * place, pl.ds(z, 1), lanes] = end[ROWS - 1 :]
                rows_ref[2 * place + 1, pl.ds(z, 1), lanes] = end[:1]
            first, last = (end * b for end in ends)
            top_sum = first if z == 0 else top_sum + first
            bottom_sum = last if z == 0 else bottom_sum + last
        sums_ref[pl.ds(0, ROWS), lanes] = top_sum + head_ref[0, :, lanes]
        sums_ref[pl.ds(ROWS, ROWS), lanes] = bottom_sum + head_ref[nz - 1, :, lanes]


def pair_kernel(mine, other, exfil_ref, pair_inv_ref, gain_ref, sent_ref):
    width = gain_ref.shape[1]
    window = (sent_ref.shape[1] - width) // 2
    depth = lax.axis_index("depth")
    inner = (depth == 1) | (depth == 2)
    near, far, corner = (pl.ds(place * width, width) for place in range(3))
    pair_inv = rcp(mine[:, near] + other[:, near])
    inner_corner = jnp.where(inner, mine[:, corner], other[:, corner])
    gain = inner_corner * pair_inv
    pair_inv_ref[...] = pair_inv
    gain_ref[...] = gain
    sent_ref[:, pl.ds(0, width)] = jnp.where(inner, mine[:, far], other[:, far]) - inner_corner * gain
    for place, quarters in enumerate((depth ^ 2, depth ^ 3)):
        cut = pl.ds(pl.multiple_of(window_start(quarters, width // 4, window), LANES), window)
        sent_ref[:, pl.ds(width + place * window, window)] = exfil_ref[:, cut]


def halo_kernel(
    own_up, own_down, from_above, from_below, end_rows, sums_ref, _, flux_ref, near_ref, far_ref, rows_ref, windows_ref,
):
    _, nz, width = flux_ref.shape
    lat = lax.axis_index("lat")
    has_above = jnp.where(lat == 0, 0.0, 1.0)
    has_below = jnp.where(lat == lax.axis_size("lat") - 1, 0.0, 1.0)
    is_even = lax.rem(lax.axis_index("depth"), 2) == 0
    sublane = lax.broadcasted_iota(jnp.int32, (ROWS, HALO_CHUNK), 0)

    @pl.loop(0, width // HALO_CHUNK)
    def _(chunk):
        start = pl.multiple_of(chunk * HALO_CHUNK, HALO_CHUNK)
        lanes = pl.ds(start, HALO_CHUNK)
        added = [[], []]
        for side, other, own, scale in ((0, from_below, own_up, has_below), (1, from_above, own_down, has_above)):
            totals = [None, None]
            for group in range(nz // ROWS):
                heads = pl.ds(pl.multiple_of(group * width + start, HALO_CHUNK), HALO_CHUNK)
                sigmas = pl.ds(pl.multiple_of((nz // ROWS + group) * width + start, HALO_CHUNK), HALO_CHUNK)
                layers = pl.ds(group * ROWS, ROWS)
                flux = rcp(other[:, sigmas] + own[:, sigmas]) * ((other[:, heads] - own[:, heads]) * scale)
                flux_ref[side, layers, lanes] = flux
                for end in range(2):
                    part = flux * end_rows[2 * end + side, layers, lanes]
                    totals[end] = part if group == 0 else totals[end] + part
            for end in range(2):
                total = totals[end]
                for by in (4, 2, 1):
                    total = total + pltpu.roll(total, by, 0)
                added[end].append(total)
        sums = []
        for end in range(2):
            total = jnp.where(sublane == 0, added[end][1], 0.0)
            total = jnp.where(sublane == ROWS - 1, added[end][0], total)
            sums.append(sums_ref[pl.ds(end * ROWS, ROWS), lanes] + total)
        near_ref[:, lanes] = jnp.where(is_even, sums[1], sums[0])
        far_ref[:, lanes] = jnp.where(is_even, sums[0], sums[1])

    half = width // 2
    extra = pl.ds(own_up.shape[1] - half, half)
    upper = lax.broadcasted_iota(jnp.int32, (ROWS, half), 0) < 4
    above, below = from_above[:, extra], from_below[:, extra]
    rows_ref[:, pl.ds(0, half)] = jnp.where(upper, above, pltpu.roll(below, 4, 0))
    rows_ref[:, pl.ds(half, half)] = jnp.where(upper, pltpu.roll(above, 4, 0), below)
    quarter = width // 4
    window = windows_ref.shape[1] // 2
    depth = lax.axis_index("depth")
    for place, quarters in enumerate((depth ^ 2, depth ^ 3)):
        cut = pl.ds(pl.multiple_of(window_start(quarters, quarter, window), LANES), window)
        windows_ref[:, pl.ds(place * window, window)] = rows_ref[:, cut]


def local_kernel(flux_ref, base, ratio, inv, head_ref, out_ref):
    nz, _, width = base.shape
    sublane = lax.broadcasted_iota(jnp.int32, (ROWS, CHUNK), 0)

    @pl.loop(0, width // CHUNK)
    def _(chunk):
        lanes = pl.ds(pl.multiple_of(chunk * CHUNK, CHUNK), CHUNK)
        y = None
        for z in range(nz):
            row = pl.ds(z, 1)
            added = jnp.where(sublane == 0, flux_ref[1, row, lanes], 0.0)
            added = jnp.where(sublane == ROWS - 1, flux_ref[0, row, lanes], added)
            rhs = base[z, :, lanes] + added
            y = rhs if z == 0 else rhs + ratio[z - 1, :, lanes] * y
            if z < nz - 1:
                out_ref[z, :, lanes] = y
        x = y * inv[nz - 1, :, lanes]
        out_ref[nz - 1, :, lanes] = x + head_ref[nz - 1, :, lanes]
        for z in reversed(range(nz - 1)):
            x = out_ref[z, :, lanes] * inv[z, :, lanes] + ratio[z, :, lanes] * x
            out_ref[z, :, lanes] = x + head_ref[z, :, lanes]


def ends_kernel(mine, other, far_mine, far_other, pair_inv_ref, gain_ref, gap_ref, chip_end_ref):
    depth = lax.axis_index("depth")
    inner = (depth == 1) | (depth == 2)
    sign = jnp.where(depth < 2, 1.0, -1.0)
    own, others = mine[...], other[...]
    gap = sign * jnp.where(inner, others - own, own - others) + 1.0
    gap_ref[...] = gap * pair_inv_ref[...]
    chip_end_ref[...] = jnp.where(inner, far_mine[...], far_other[...]) + sign * gain_ref[...] * gap


def final_kernel(
    local_ref, top_col, bottom_col, gap_ref, gain_ref, res_ref, res_other, end_ref, end_other, level_ref,
    out_ref, surface_ref, held, sem, level_sem,
):
    nz, _, width = local_ref.shape
    depth = lax.axis_index("depth")
    sign = jnp.where(depth < 2, 1.0, -1.0)

    level_copy = pltpu.make_async_copy(level_ref, surface_ref, level_sem)
    level_copy.start()

    def out_copy(chunk):
        lanes = pl.ds(pl.multiple_of(chunk * CHUNK, CHUNK), CHUNK)
        return pltpu.make_async_copy(held.at[:, :, lanes], out_ref.at[:, :, lanes], sem.at[chunk])

    @pl.loop(0, width // CHUNK)
    def _(chunk):
        lanes = pl.ds(pl.multiple_of(chunk * CHUNK, CHUNK), CHUNK)
        flow_chip = (sign * (end_ref[:, lanes] - end_other[:, lanes]) + 1.0) * rcp(
            res_ref[:, lanes] + res_other[:, lanes]
        )
        flow_core = gap_ref[:, lanes] + gain_ref[:, lanes] * flow_chip
        j_in = jnp.where(depth == 0, 0.0, jnp.where(depth == 2, flow_chip, flow_core))
        j_out = jnp.where(depth == 3, 0.0, jnp.where(depth == 1, flow_chip, flow_core))
        for z in range(nz):
            held[z, :, lanes] = (
                local_ref[z, :, lanes] + top_col[z, :, lanes] * j_in - bottom_col[z, :, lanes] * j_out
            )
        out_copy(chunk).start()

    @pl.loop(0, width // CHUNK)
    def _(chunk):
        out_copy(chunk).wait()

    level_copy.wait()


def shift_rows(x, by):
    return pltpu.roll(x, by % x.shape[0], 0)


def shift_lanes(x, by):
    return pltpu.roll(x, by % x.shape[1], 1)


def harmonic(first, second):
    total = first + second
    return 2.0 * first * second * rcp(jnp.where(total > 0.0, total, 1.0))


def face_k(pond, ground, conv, shift):
    pond_two, ground_two, conv_two = shift(pond), shift(ground), shift(conv)
    depth_face = 0.5 * (pond + pond_two)
    slope = pond_two + ground_two - (pond + ground)
    return (
        jnp.exp2((5.0 / 3.0 * LOG2E) * jnp.log(depth_face))
        * harmonic(conv, conv_two)
        * lax.rsqrt(jnp.abs(slope) + SLOPE_FLOOR)
    )


def relay_kernel(rows_ref, exfil_ref, from_chip, chip_other, _, __, sent_ref):
    window = sent_ref.shape[1] // 3
    depth = lax.axis_index("depth")
    is_low = depth < 2
    cut = pl.ds(pl.multiple_of(window_start(depth ^ 1, rows_ref.shape[1] // 4, window), LANES), window)
    first, second, third = (pl.ds(place * window, window) for place in range(3))
    own, other = rows_ref[:, cut], from_chip[:, second]
    sent_ref[:, first] = jnp.where(is_low, own, other)
    sent_ref[:, second] = jnp.where(is_low, other, own)
    sent_ref[:, third] = jnp.where(
        is_low, exfil_ref[:, cut], chip_other[:, pl.ds(chip_other.shape[1] - window, window)]
    )


def surface_kernel(own_ref, exfil_ref, rows_ref, from_chip, from_core, chip_other, out_ref, last):
    window = last.shape[1]
    width = exfil_ref.shape[1]
    quarter = width // 4
    lat = lax.axis_index("lat")
    depth = lax.axis_index("depth")
    is_even = lax.rem(depth, 2) == 0
    upper = lax.broadcasted_iota(jnp.int32, (ROWS, window), 0) < 4
    first, second, third = (pl.ds(place * window, window) for place in range(3))

    cut = pl.ds(pl.multiple_of(window_start(depth, quarter, window), LANES), window)
    mine, other = rows_ref[:, cut], from_chip[:, first]
    here = (jnp.where(depth < 2, mine, other), jnp.where(depth < 2, other, mine))
    there = (from_core[:, first], from_core[:, second])
    outer = [jnp.where(is_even, a, b) for low, high in zip(here, there) for a, b in ((low, high), (high, low))]
    near = jnp.where(depth == 0, exfil_ref[:, first], chip_other[:, pl.ds(width, window)])
    near = jnp.where(is_even, near, from_core[:, third])

    def extended(rows, own):
        own = pltpu.roll(own, 4, 0)
        return jnp.concatenate([jnp.where(upper, rows, own), jnp.where(upper, own, rows)], axis=0)

    exfil, pond, ground, conv = (
        extended(rows, own) for rows, own in zip(outer, (near, own_ref[0], own_ref[1], own_ref[2]))
    )
    row = lax.broadcasted_iota(jnp.int32, conv.shape, 0)
    outside = ((row < 4) & (lat == 0)) | ((row >= 12) & (lat == lax.axis_size("lat") - 1))
    conv = jnp.where(outside, 0.0, conv)
    k_down = face_k(pond, ground, conv, lambda x: shift_rows(x, -1))
    k_up = shift_rows(k_down, 1)
    k_right = face_k(pond, ground, conv, lambda x: shift_lanes(x, -1))
    lane = lax.broadcasted_iota(jnp.int32, conv.shape, 1)
    k_right = jnp.where(lane < window - 1, k_right, 0.0)
    k_left = shift_lanes(k_right, 1)
    diag = 1.0 / SURFACE_STEP + k_up + k_down + k_left + k_right
    rhs = pond * (1.0 / SURFACE_STEP)
    rhs = rhs + k_up * (shift_rows(ground, 1) - ground) + k_down * (shift_rows(ground, -1) - ground)
    rhs = rhs + k_left * (shift_lanes(ground, 1) - ground) + k_right * (shift_lanes(ground, -1) - ground)
    inv = rcp(diag)
    k_up, k_down, k_left, k_right = k_up * inv, k_down * inv, k_left * inv, k_right * inv
    rhs = (rhs + exfil) * inv
    level = pond
    for _ in range(SWEEPS):
        level = (
            rhs
            + k_up * shift_rows(level, 1)
            + k_down * shift_rows(level, -1)
            + k_left * shift_lanes(level, 1)
            + k_right * shift_lanes(level, -1)
        )
    last[...] = level
    start = pl.multiple_of(
        depth * quarter - window_start(depth, quarter, window), LANES
    )
    cut = pl.ds(start, quarter)
    lower_half = lax.broadcasted_iota(jnp.int32, (ROWS, quarter), 0) >= 4
    upper = pltpu.roll(last[pl.ds(0, ROWS), cut], 4, 0)
    lower = pltpu.roll(last[pl.ds(ROWS, ROWS), cut], 4, 0)
    out_ref[...] = jnp.where(lower_half, lower, upper)


def per_device(
    head, head_old, soil, cond_table, shape_table, pore_table, pond, ground, ponded, river
):
    nz, rows, width = head.shape
    window = width // 4 + 2 * LANES
    lat_count = lax.axis_size("lat")
    up, down = [], []
    for i in range(lat_count):
        for j in range(4):
            after, place = (i + 1, j) if i < lat_count - 1 else (0, j ^ 2)
            up.append((4 * i + j, 4 * after + place))
            down.append((4 * after + place, 4 * i + j))
    core = [(0, 1), (1, 0), (2, 3), (3, 2)]
    chip = [(0, 2), (2, 0), (1, 3), (3, 1)]
    block = f32(nz, rows, width)
    padded = f32(nz, rows, width + LANES)
    plane = f32(rows, width)

    side = f32(rows, 2 * (nz // ROWS) * width + width // 2)

    own_up, own_down, tables, exfil, own_fields = call(
        pack_kernel,
        "pack",
        [in_hbm(x) for x in (cond_table, shape_table, pore_table, head, soil, pond, ground, ponded, river)],
        [side, side, f32(6, ROWS, LANES), plane, f32(3, rows, window)],
        scratch=[
            pltpu.SMEM((3, cond_table.shape[0]), jnp.float32),
            pltpu.VMEM((2, nz // ROWS, ROWS, width), jnp.int32),
            pltpu.VMEM((rows, width), jnp.float32),
            pltpu.VMEM((rows, width), jnp.int32),
            pltpu.VMEM((rows, width), jnp.float32),
            pltpu.VMEM((rows, width), jnp.float32),
            pltpu.VMEM((rows, width), jnp.int32),
            pltpu.VMEM((rows, width), jnp.int32),
            pltpu.SemaphoreType.DMA((9 + 4 * (nz // ROWS),)),
        ],
    )
    from_above = lax.ppermute(own_up, ("lat", "depth"), up)
    from_below = lax.ppermute(own_down, ("lat", "depth"), down)

    head_v, sigma, base, ratio, inv, top_col, bottom_col, resist = call(
        factor_kernel,
        "factor",
        [in_vmem(tables), in_vmem(exfil)] + [in_hbm(x) for x in (head, head_old, soil)],
        [padded, padded] + [block] * 5 + [f32(rows, 3 * width)],
        scratch=[
            pltpu.VMEM((nz, rows, width), jnp.float32),
            pltpu.VMEM((nz, rows, width), jnp.int32),
            pltpu.SemaphoreType.DMA((3, width // CHUNK)),
        ],
    )
    resist_other = lax.ppermute(resist, "depth", core)
    pair_inv, gain, chip_sent = call(
        pair_kernel,
        "pair",
        [in_vmem(x) for x in (resist, resist_other, exfil)],
        [plane, plane, f32(rows, width + 2 * window)],
    )
    chip_other = lax.ppermute(chip_sent, "depth", chip)

    base, sums, end_rows = call(
        lateral_kernel,
        "lateral",
        [in_vmem(x) for x in (head_v, sigma, base, top_col, bottom_col, gain)],
        [block, f32(2 * rows, width), f32(4, nz, width)],
        scratch=[pltpu.VMEM((3, nz, rows, LANES), jnp.float32)],
    )
    flux, ends, far_ends, field_rows, windows = call(
        halo_kernel,
        "halo",
        [in_vmem(x) for x in (own_up, own_down, from_above, from_below, end_rows, sums, gain)],
        [f32(2, nz, width), plane, plane, plane, f32(rows, 2 * window)],
    )
    near_other = lax.ppermute(ends, "depth", core)
    far_other = lax.ppermute(far_ends, "depth", core)
    windows_chip = lax.ppermute(windows, "depth", chip)
    local = call(
        local_kernel, "local", [in_vmem(x) for x in (flux, base, ratio, inv, head_v)], [block]
    )[0]
    gap, chip_end = call(
        ends_kernel, "ends", [in_vmem(x) for x in (ends, near_other, far_ends, far_other, pair_inv, gain)], [plane, plane]
    )
    chip_end_other = lax.ppermute(chip_end, "depth", chip)
    relayed = call(
        relay_kernel,
        "relay",
        [in_vmem(x) for x in (field_rows, exfil, windows_chip, chip_other, chip_end, local)],
        [f32(rows, 3 * window)],
    )[0]
    windows_core = lax.ppermute(relayed, "depth", core)
    level = call(
        surface_kernel,
        "surface",
        [
            in_vmem(x)
            for x in (own_fields, exfil, field_rows, windows_chip, windows_core, chip_other)
        ],
        [f32(rows, width // 4)],
        scratch=[pltpu.VMEM((2 * rows, window), jnp.float32)],
    )[0]
    head_new, surface_new = call(
        final_kernel,
        "final",
        [
            in_vmem(x)
            for x in (
                local, top_col, bottom_col, gap, gain, chip_sent, chip_other, chip_end, chip_end_other, level,
            )
        ],
        [
            jax.ShapeDtypeStruct((nz, rows, width), jnp.float32),
            jax.ShapeDtypeStruct((rows, width // 4), jnp.float32),
        ],
        out_specs=[ANY, ANY],
        scratch=[
            pltpu.VMEM((nz, rows, width), jnp.float32),
            pltpu.SemaphoreType.DMA((width // CHUNK,)),
            pltpu.SemaphoreType.DMA,
        ],
    )
    return (head_new, surface_new)


def solution(mesh):
    placed = (
        P("depth", "lat", None),
        P("depth", "lat", None),
        P("depth", "lat", None),
        P(),
        P(),
        P(),
        P("lat", None),
        P("lat", None),
        P("lat", None),
        P("lat", None),
    )
    return jax.shard_map(
        per_device,
        mesh=mesh,
        in_specs=placed,
        out_specs=(P("depth", "lat", None), P("lat", "depth")),
        check_vma=False,
    )
```
